128 devices in a mesh: row: 16 (over x, z), col: 8 (over y, core).
Axes of the slice: x: 4, y: 4, z: 4, core: 2. Of those that a mesh axis runs over, the one named last changes fastest.
Arguments:
- layer_input: bfloat16 [1536, 8192], P(None, 'row'), may hold values from -6 to 6
- output_grad: bfloat16 [1536, 29568], P(None, 'col'), may hold values from -0.15625 to 0.15625
- sketch: bfloat16 [29568, 576], P('col'), may hold values from -6 to 6
- first_moment: float32 [512, 29568], P('row', 'col'), may hold values from -6 to 6
- second_moment: float32 [512, 29568], P('row', 'col'), may hold values from 0.001 to 0.01
Outputs:
- update: float32 [8192, 29568], P('row', 'col')
- new_first: float32 [512, 29568], P('row', 'col')
- new_second: float32 [512, 29568], P('row', 'col')
The draws below stay inside these ranges and needn't reach their ends.
All inputs are finite; a program needn't handle non-finite values.
Results may differ from the reference program's by a relative error of at most 0.023.
Values may be sent and summed in bfloat16 or wider, within the bound.
No kernel may reach another device: no remote copies, remote signals or barrier semaphores. Data moves between devices by JAX's collectives and lax.ppermute only.
A program may use at most 128 MiB of HBM per device.

```python
import math
import jax
import jax.numpy as jnp
from jax import lax

D = 8192
FF = 29568
RANK = 512
ADAM_STEP = 10
TOKENS = 1536
SKETCH = 576
N_ROW = 16


def steps_of(key, extent, pieces, low, largest):
    def one(dim, shards_of):
        heights = jax.random.uniform(jax.random.fold_in(jax.random.fold_in(key, 6), dim), (shards_of,), jnp.float32, low / len(pieces), largest / len(pieces))
        return jnp.repeat(jnp.exp(heights), extent[dim] // shards_of).reshape((-1,) + (1,) * (len(extent) - dim - 1))

    level = one(*pieces[0])
    for cut in pieces[1:]:
        level = level * one(*cut)
    return level


def gaussian(key, shape, deviation, bound, shards=(), kind=jnp.bfloat16):
    drawn = jax.random.normal(key, shape, jnp.float32) * deviation
    if len(shards) > 0:
        drawn = steps_of(key, shape, shards, -0.22, 0.18) * drawn
    return jnp.clip(drawn, min=-bound, max=bound).astype(kind)


def setup_inputs(seed: int = 0) -> dict:
    streams_of = jax.random.split(jax.random.key(seed), 6)
    return {
        "layer_input": gaussian(streams_of[0], (TOKENS, D), 1.0, 6.0, ((1, 16),)),
        "output_grad": gaussian(streams_of[1], (TOKENS, FF), TOKENS ** -0.5, 0.15625, ((1, 8),)),
        "sketch": gaussian(streams_of[2], (FF, SKETCH), 1.0, 6.0, ((0, 8),)),
        "first_moment": gaussian(streams_of[3], (RANK, FF), 1.0, 6.0, ((0, 16), (1, 8)), jnp.float32),
        "second_moment": jnp.clip(jnp.exp(math.log(0.01) - 2.30258502 * jax.random.uniform(streams_of[4], (RANK, FF), jnp.float32) ** steps_of(streams_of[4], (RANK, FF), ((0, 16), (1, 8)), -0.2, 0.2)), 0.001, 0.01),
    }


beta_one = 0.9
beta_two = 0.999
adam_epsilon = 1e-08

def orthonormal_basis(sketched):
    gram = jnp.dot(sketched.T.astype(jnp.float32), sketched.astype(jnp.float32), precision=lax.Precision.HIGHEST, preferred_element_type=jnp.float32)
    factor_low = jnp.linalg.cholesky(gram)
    return lax.linalg.triangular_solve(factor_low, sketched, left_side=False, lower=True, transpose_a=True)

def reference(layer_input, output_grad, sketch, first_moment, second_moment):
    gradient = jnp.dot(layer_input.T.astype(jnp.float32), output_grad.astype(jnp.float32), preferred_element_type=jnp.float32).astype(jnp.bfloat16)
    sketched = jnp.dot(gradient.astype(jnp.float32), sketch.astype(jnp.float32), preferred_element_type=jnp.float32)
    basis = orthonormal_basis(sketched)
    projector = basis[:, :RANK].astype(jnp.bfloat16)
    tile_rows = D // N_ROW
    proj_tiles = projector.reshape(N_ROW, tile_rows, RANK)
    grad_tiles = gradient.reshape(N_ROW, tile_rows, FF)

    def add_tile(running, tiles):
        partial_sum = jnp.dot(tiles[0].T.astype(jnp.float32), tiles[1].astype(jnp.float32), preferred_element_type=jnp.float32).astype(jnp.bfloat16)
        partial_sum = lax.optimization_barrier(partial_sum)
        return (running + partial_sum.astype(jnp.float32), None)
    projected, _ = lax.scan(add_tile, jnp.zeros((RANK, FF), jnp.float32), (proj_tiles, grad_tiles))
    new_first = beta_one * first_moment + (1.0 - beta_one) * projected
    new_second = beta_two * second_moment + (1.0 - beta_two) * projected * projected
    first_hat = new_first / (1.0 - beta_one ** ADAM_STEP)
    second_hat = new_second / (1.0 - beta_two ** ADAM_STEP)
    normalized = (first_hat / (jnp.sqrt(second_hat) + adam_epsilon)).astype(jnp.bfloat16)
    update = jnp.dot(projector.astype(jnp.float32), normalized.astype(jnp.float32), preferred_element_type=jnp.float32)
    return (update, new_first, new_second)
```

```python
import jax
import jax.numpy as jnp
from jax import lax
from jax.experimental import pallas as pl
from jax.experimental.pallas import tpu as pltpu
from jax.sharding import PartitionSpec as P

RANK = 512
ADAM_STEP = 10
BLOCK = 128
TILE = 640

beta_one = 0.9
beta_two = 0.999
adam_epsilon = 1e-08

f32 = jnp.float32
bf16 = jnp.bfloat16
HIGHEST = lax.Precision.HIGHEST

EXTENT = {"x": 4, "z": 4, "y": 4, "core": 2}
HOME = {"x": ("row", 4), "z": ("row", 1), "y": ("col", 2), "core": ("col", 1)}


def place(sub):
    axis, stride = HOME[sub]
    return lax.axis_index(axis) // stride % EXTENT[sub]


def shift(value, sub, by):
    axis, stride = HOME[sub]
    n = EXTENT[sub]
    pairs = []
    for i in range(16 if axis == "row" else 8):
        at = i // stride % n
        pairs.append((i, i + ((at + by) % n - at) * stride))
    return lax.ppermute(value, axis, pairs)


def scatter_sum(value, sub):
    n, me = EXTENT[sub], place(sub)
    pick = lambda k: lax.dynamic_index_in_dim(value, (me + k) % n, 0, keepdims=False)
    got = [shift(pick(k), sub, k) for k in range(1, n)]
    total = pick(0)
    for term in got:
        total = total + term
    return total


def gather(value, sub):
    n, me = EXTENT[sub], place(sub)
    got = [value] + [shift(value, sub, k) for k in range(1, n)]
    out = jnp.zeros((n,) + value.shape, value.dtype)
    for k in range(n):
        out = lax.dynamic_update_index_in_dim(out, got[k], (me - k) % n, 0)
    return out


def full_sum(value, sub):
    total = value
    for k in range(1, EXTENT[sub]):
        total = total + shift(value, sub, k)
    return total


def lane_of(value, k):
    return jnp.take_along_axis(value, jnp.full(value.shape, k, jnp.int32), axis=1)


def invert_block(rows, lane, sub):
    scale = [None] * len(rows)
    for k in range(len(rows) * 8):
        g, r = divmod(k, 8)
        column = lane_of(rows[g], k)
        row = jnp.broadcast_to(rows[g][r : r + 1], (8, BLOCK))
        pivot = jnp.broadcast_to(column[r : r + 1], (8, BLOCK))
        inverse = 1.0 / pivot
        unit = jnp.where(lane == k, 1.0, row)
        for h in range(g, len(rows)):
            factor = (column if h == g else lane_of(rows[h], k)) * inverse
            reduced = jnp.where(lane == k, 0.0, rows[h]) - factor * unit
            if h == g:
                rows[g] = jnp.where(sub > r, reduced, jnp.where(sub == r, unit, rows[g]))
            else:
                rows[h] = reduced
        root = lax.rsqrt(pivot)
        scale[g] = root if scale[g] is None else jnp.where(sub == r, root, scale[g])
    return [a * b for a, b in zip(rows, scale)]


def factor_kernel(gram_ref, out_ref, work):
    size, padded = gram_ref.shape[0], work.shape[0]
    work[...] = jnp.zeros_like(work)
    work[:size, :size] = gram_ref[...]
    lane = lax.broadcasted_iota(jnp.int32, (8, BLOCK), 1)
    sub = lax.broadcasted_iota(jnp.int32, (8, BLOCK), 0)
    row_in = lax.broadcasted_iota(jnp.int32, (BLOCK, BLOCK), 0)
    lane_in = lax.broadcasted_iota(jnp.int32, (BLOCK, BLOCK), 1)
    if padded > size:
        last = pl.ds(padded - BLOCK, BLOCK)
        spare = (row_in == lane_in) & (row_in >= size - (padded - BLOCK))
        work[last, last] = jnp.where(spare, 1.0, work[last, last])
    lanes = lax.broadcasted_iota(jnp.int32, (BLOCK, padded), 1)

    def step(b, carry):
        o = pl.multiple_of(b * BLOCK, BLOCK)
        here = pl.ds(o, BLOCK)
        rows = [work[pl.ds(pl.multiple_of(o + 8 * h, 8), 8), here] for h in range(BLOCK // 8)]
        inverse = jnp.concatenate(invert_block(rows, lane, sub), axis=0)
        inverse = jnp.where(row_in >= lane_in, inverse, 0.0)
        panel = work[here, :]
        work[:, here] = jnp.zeros((padded, BLOCK), f32)
        solved = jnp.dot(inverse, panel, precision=HIGHEST, preferred_element_type=f32)
        work[here, :] = solved
        work[here, here] = inverse
        later = jnp.where(lanes >= o + BLOCK, solved, 0.0)
        work[...] -= lax.dot_general(
            later, work[here, :], (((0,), (0,)), ((), ())), precision=HIGHEST, preferred_element_type=f32
        )
        return carry

    lax.fori_loop(0, padded // BLOCK, step, 0)
    row_at = lax.broadcasted_iota(jnp.int32, (padded, padded), 0)
    lane_at = lax.broadcasted_iota(jnp.int32, (padded, padded), 1)
    out_ref[...] = jnp.where(row_at >= lane_at, work[...], 0.0)[:size, :size]


def inverse_factor(gram):
    size = gram.shape[0]
    padded = pl.cdiv(size, BLOCK) * BLOCK
    return pl.pallas_call(
        factor_kernel,
        out_shape=jax.ShapeDtypeStruct((size, size), f32),
        in_specs=[pl.BlockSpec(memory_space=pltpu.VMEM)],
        out_specs=pl.BlockSpec(memory_space=pltpu.VMEM),
        scratch_shapes=[pltpu.VMEM((padded, padded), f32)],
        compiler_params=pltpu.CompilerParams(vmem_limit_bytes=32 << 20),
        cost_estimate=pl.CostEstimate(flops=12 * size**3, bytes_accessed=8 * size**2, transcendentals=0),
        name="inverse_factor",
    )(gram)


def moments(first, second, projected):
    new_first = beta_one * first + (1.0 - beta_one) * projected
    new_second = beta_two * second + (1.0 - beta_two) * projected * projected
    return new_first, new_second


def step_kernel(
    at_ref, mixed_ref, projector_ref, grad_ref, first_ref, second_ref, own_first_ref, own_second_ref,
    update_ref, new_first_ref, new_second_ref, projected_ref,
):
    projected_ref[...] = jnp.dot(mixed_ref[...], grad_ref[...], preferred_element_type=f32)
    new_first, new_second = moments(
        first_ref[...].astype(f32), second_ref[...].astype(f32), projected_ref[...]
    )
    first_hat = new_first / (1.0 - beta_one**ADAM_STEP)
    second_hat = new_second / (1.0 - beta_two**ADAM_STEP)
    normalized = (first_hat / (jnp.sqrt(second_hat) + adam_epsilon)).astype(bf16)
    update_ref[...] = jnp.dot(projector_ref[...], normalized, preferred_element_type=f32)
    owned = own_first_ref.shape[0]
    mine = projected_ref[pl.ds(pl.multiple_of(at_ref[0] * owned, owned), owned), :]
    new_first_ref[...], new_second_ref[...] = moments(own_first_ref[...], own_second_ref[...], mine)


def adam_step(at, mixed, projector, output_grad, first, second, own_first, own_second):
    tokens, width = output_grad.shape
    features, rank = projector.shape
    owned = own_first.shape[0]
    whole = lambda shape: pl.BlockSpec(shape, lambda i, at: (0, 0))
    strip = lambda rows: pl.BlockSpec((rows, TILE), lambda i, at: (0, i))
    return pl.pallas_call(
        step_kernel,
        out_shape=(
            jax.ShapeDtypeStruct((features, width), f32),
            jax.ShapeDtypeStruct((owned, width), f32),
            jax.ShapeDtypeStruct((owned, width), f32),
        ),
        grid_spec=pltpu.PrefetchScalarGridSpec(
            num_scalar_prefetch=1,
            grid=(pl.cdiv(width, TILE),),
            in_specs=[whole((rank, tokens)), whole((features, rank)), strip(tokens)]
            + [strip(rank), strip(rank), strip(owned), strip(owned)],
            out_specs=[strip(features), strip(owned), strip(owned)],
            scratch_shapes=[pltpu.VMEM((rank, TILE), f32)],
        ),
        compiler_params=pltpu.CompilerParams(vmem_limit_bytes=48 << 20),
        cost_estimate=pl.CostEstimate(
            flops=2 * rank * width * (tokens + features),
            bytes_accessed=width * (2 * tokens + 4 * rank + 4 * features + 16 * owned),
            transcendentals=rank * width,
        ),
        name="adam_step",
    )(at, mixed, projector, output_grad, first, second, own_first, own_second)


def two_parts(value):
    high = value.astype(bf16)
    return high, (value - high.astype(f32)).astype(bf16)


def local(layer_input, output_grad, sketch, first_moment, second_moment):
    tokens, features = layer_input.shape
    columns = sketch.shape[1]
    first_rows = lax.all_gather(first_moment.astype(bf16), "row", axis=0, tiled=True)
    second_rows = lax.all_gather(second_moment.astype(bf16), "row", axis=0, tiled=True)

    token_sketch = jnp.dot(output_grad, sketch, preferred_element_type=f32)
    turned = lambda part: lax.dot_general(
        part, layer_input, (((0,), (0,)), ((), ())), preferred_element_type=f32
    )
    high, low = two_parts(token_sketch)
    partial = turned(high) + turned(low)
    half = scatter_sum(partial.reshape(2, columns // 2, features), "core")
    owned_rows = scatter_sum(half.reshape(4, columns // 8, features), "y")
    sketched = gather(gather(owned_rows, "y").reshape(columns // 2, features), "core")
    sketched = sketched.reshape(columns, features)

    gram_rows = lax.dot_general(
        owned_rows, sketched, (((1,), (1,)), ((), ())), precision=HIGHEST, preferred_element_type=f32
    )
    gram_rows = full_sum(full_sum(gram_rows, "x"), "z")
    gram = gather(gather(gram_rows, "y").reshape(columns // 2, columns), "core").reshape(columns, columns)

    share = tokens // 128
    own_tokens = lax.dynamic_index_in_dim(
        layer_input.reshape(16, 8, share, features), lax.axis_index("col"), 1, keepdims=False
    ).reshape(tokens // 8, features)
    sketched_high, rest = two_parts(sketched)
    times = lambda part: lax.dot_general(
        own_tokens, part, (((1,), (1,)), ((), ())), preferred_element_type=f32
    )
    mixed = times(sketched_high) + times(rest)
    mixed = scatter_sum(mixed.reshape(4, 4 * share, columns), "x")
    mixed = scatter_sum(mixed.reshape(4, share, columns), "z")
    mixed = lax.all_gather(mixed, ("row", "col"), axis=0, tiled=True)

    inverse = inverse_factor(gram)
    basis = lax.dot_general(
        sketched, inverse, (((0,), (1,)), ((), ())), precision=HIGHEST, preferred_element_type=f32
    )
    projector = basis[:, :RANK].astype(bf16)
    turned_mixed = lax.dot_general(
        inverse[:RANK], mixed, (((1,), (1,)), ((), ())), precision=HIGHEST, preferred_element_type=f32
    ).astype(bf16)
    at = lax.axis_index("row").astype(jnp.int32).reshape(1)
    return adam_step(
        at, turned_mixed, projector, output_grad, first_rows, second_rows, first_moment, second_moment
    )


def solution(mesh):
    placed = (P(None, "row"), P(None, "col"), P("col", None), P("row", "col"), P("row", "col"))
    return jax.shard_map(
        local,
        mesh=mesh,
        in_specs=placed,
        out_specs=(P("row", "col"), P("row", "col"), P("row", "col")),
        check_vma=False,
    )
```

```python
import jax
import jax.numpy as jnp
from jax import lax
from jax.experimental import pallas as pl
from jax.experimental.pallas import tpu as pltpu
from jax.sharding import PartitionSpec as P

RANK = 512
ADAM_STEP = 10
BLOCK = 128
TILE = 640
TOKEN_TILE = 256
MIX_TILE = 384

beta_one = 0.9
beta_two = 0.999
adam_epsilon = 1e-08

f32 = jnp.float32
bf16 = jnp.bfloat16
HIGHEST = lax.Precision.HIGHEST

EXTENT = {"x": 4, "z": 4, "y": 4, "core": 2}
HOME = {"x": ("row", 4), "z": ("row", 1), "y": ("col", 2), "core": ("col", 1)}


def place(sub):
    axis, stride = HOME[sub]
    return lax.axis_index(axis) // stride % EXTENT[sub]


def shift(value, sub, by):
    axis, stride = HOME[sub]
    n = EXTENT[sub]
    pairs = []
    for i in range(16 if axis == "row" else 8):
        at = i // stride % n
        pairs.append((i, i + ((at + by) % n - at) * stride))
    return lax.ppermute(value, axis, pairs)


def scatter_sum(value, sub):
    n, me = EXTENT[sub], place(sub)
    pick = lambda k: lax.dynamic_index_in_dim(value, (me + k) % n, 0, keepdims=False)
    got = [shift(pick(k), sub, k) for k in range(1, n)]
    total = pick(0)
    for term in got:
        total = total + term
    return total


def gather(value, sub):
    n, me = EXTENT[sub], place(sub)
    got = [value] + [shift(value, sub, k) for k in range(1, n)]
    out = jnp.zeros((n,) + value.shape, value.dtype)
    for k in range(n):
        out = lax.dynamic_update_index_in_dim(out, got[k], (me - k) % n, 0)
    return out


def full_sum(value, sub):
    total = value
    for k in range(1, EXTENT[sub]):
        total = total + shift(value, sub, k)
    return total


def lane_of(value, k):
    return jnp.take_along_axis(value, jnp.full(value.shape, k, jnp.int32), axis=1)


def invert_block(rows, lane, sub):
    scale = [None] * len(rows)
    for k in range(len(rows) * 8):
        g, r = divmod(k, 8)
        column = lane_of(rows[g], k)
        row = jnp.broadcast_to(rows[g][r : r + 1], (8, BLOCK))
        pivot = jnp.broadcast_to(column[r : r + 1], (8, BLOCK))
        inverse = 1.0 / pivot
        unit = jnp.where(lane == k, 1.0, row)
        for h in range(g, len(rows)):
            factor = (column if h == g else lane_of(rows[h], k)) * inverse
            reduced = jnp.where(lane == k, 0.0, rows[h]) - factor * unit
            if h == g:
                rows[g] = jnp.where(sub > r, reduced, jnp.where(sub == r, unit, rows[g]))
            else:
                rows[h] = reduced
        root = lax.rsqrt(pivot)
        scale[g] = root if scale[g] is None else jnp.where(sub == r, root, scale[g])
    return [a * b for a, b in zip(rows, scale)]


def factor_kernel(gram_ref, out_ref, work):
    size, padded = gram_ref.shape[0], work.shape[0]
    work[...] = jnp.zeros_like(work)
    work[:size, :size] = gram_ref[...]
    lane = lax.broadcasted_iota(jnp.int32, (8, BLOCK), 1)
    sub = lax.broadcasted_iota(jnp.int32, (8, BLOCK), 0)
    row_in = lax.broadcasted_iota(jnp.int32, (BLOCK, BLOCK), 0)
    lane_in = lax.broadcasted_iota(jnp.int32, (BLOCK, BLOCK), 1)
    if padded > size:
        last = pl.ds(padded - BLOCK, BLOCK)
        spare = (row_in == lane_in) & (row_in >= size - (padded - BLOCK))
        work[last, last] = jnp.where(spare, 1.0, work[last, last])
    lanes = lax.broadcasted_iota(jnp.int32, (BLOCK, padded), 1)

    def step(b, carry):
        o = pl.multiple_of(b * BLOCK, BLOCK)
        here = pl.ds(o, BLOCK)
        rows = [work[pl.ds(pl.multiple_of(o + 8 * h, 8), 8), here] for h in range(BLOCK // 8)]
        inverse = jnp.concatenate(invert_block(rows, lane, sub), axis=0)
        inverse = jnp.where(row_in >= lane_in, inverse, 0.0)
        panel = work[here, :]
        work[:, here] = jnp.zeros((padded, BLOCK), f32)
        solved = jnp.dot(inverse, panel, precision=HIGHEST, preferred_element_type=f32)
        work[here, :] = solved
        work[here, here] = inverse
        later = jnp.where(lanes >= o + BLOCK, solved, 0.0)
        work[...] -= lax.dot_general(
            later, work[here, :], (((0,), (0,)), ((), ())), precision=HIGHEST, preferred_element_type=f32
        )
        return carry

    lax.fori_loop(0, padded // BLOCK, step, 0)
    row_at = lax.broadcasted_iota(jnp.int32, (padded, padded), 0)
    lane_at = lax.broadcasted_iota(jnp.int32, (padded, padded), 1)
    out_ref[...] = jnp.where(row_at >= lane_at, work[...], 0.0)[:size, :size]


def inverse_factor(gram):
    size = gram.shape[0]
    padded = pl.cdiv(size, BLOCK) * BLOCK
    return pl.pallas_call(
        factor_kernel,
        out_shape=jax.ShapeDtypeStruct((size, size), f32),
        in_specs=[pl.BlockSpec(memory_space=pltpu.VMEM)],
        out_specs=pl.BlockSpec(memory_space=pltpu.VMEM),
        scratch_shapes=[pltpu.VMEM((padded, padded), f32)],
        compiler_params=pltpu.CompilerParams(vmem_limit_bytes=32 << 20),
        cost_estimate=pl.CostEstimate(flops=12 * size**3, bytes_accessed=8 * size**2, transcendentals=0),
        name="inverse_factor",
    )(gram)


def two_parts(value):
    high = value.astype(bf16)
    return high, (value - high.astype(f32)).astype(bf16)


def sketch_kernel(sketch_ref, grad_ref, input_ref, out_ref):
    token_sketch = jnp.dot(sketch_ref[...], grad_ref[...], preferred_element_type=f32)
    high, low = two_parts(token_sketch)
    values = input_ref[...]
    term = jnp.dot(high, values, preferred_element_type=f32) + jnp.dot(low, values, preferred_element_type=f32)

    @pl.when(pl.program_id(0) == 0)
    def _():
        out_ref[...] = term

    @pl.when(pl.program_id(0) > 0)
    def _():
        out_ref[...] += term


def sketched_term(sketch_turned, grad_turned, layer_input):
    columns, width = sketch_turned.shape
    tokens, features = layer_input.shape
    return pl.pallas_call(
        sketch_kernel,
        out_shape=jax.ShapeDtypeStruct((columns, features), f32),
        grid=(tokens // TOKEN_TILE,),
        in_specs=[
            pl.BlockSpec((columns, width), lambda i: (0, 0)),
            pl.BlockSpec((width, TOKEN_TILE), lambda i: (0, i)),
            pl.BlockSpec((TOKEN_TILE, features), lambda i: (i, 0)),
        ],
        out_specs=pl.BlockSpec((columns, features), lambda i: (0, 0)),
        compiler_params=pltpu.CompilerParams(vmem_limit_bytes=48 << 20),
        cost_estimate=pl.CostEstimate(
            flops=2 * columns * tokens * (width + 2 * features),
            bytes_accessed=2 * width * (columns + tokens) + 2 * tokens * features + 4 * columns * features,
            transcendentals=0,
        ),
        name="sketched_term",
    )(sketch_turned, grad_turned, layer_input)


def mix_kernel(inverse_ref, mixed_ref, out_ref):
    values = jnp.concatenate([mixed_ref[i] for i in range(mixed_ref.shape[0])], axis=0)
    high, low = two_parts(values)
    inverse_high, inverse_low = two_parts(inverse_ref[...])
    times = lambda a, b: lax.dot_general(a, b, (((1,), (1,)), ((), ())), preferred_element_type=f32)
    total = times(inverse_high, low) + times(inverse_low, high) + times(inverse_high, high)
    out_ref[...] = total.astype(out_ref.dtype)


def mixed_tokens(inverse, mixed):
    blocks, share, columns = mixed.shape
    group = MIX_TILE // share
    return pl.pallas_call(
        mix_kernel,
        out_shape=jax.ShapeDtypeStruct((RANK, blocks * share), bf16),
        grid=(blocks // group,),
        in_specs=[
            pl.BlockSpec((RANK, columns), lambda i: (0, 0)),
            pl.BlockSpec((group, share, columns), lambda i: (i, 0, 0)),
        ],
        out_specs=pl.BlockSpec((RANK, MIX_TILE), lambda i: (0, i)),
        compiler_params=pltpu.CompilerParams(vmem_limit_bytes=48 << 20),
        cost_estimate=pl.CostEstimate(
            flops=6 * RANK * columns * blocks * share,
            bytes_accessed=4 * blocks * share * columns + 2 * RANK * blocks * share,
            transcendentals=0,
        ),
        name="mixed_tokens",
    )(inverse, mixed)


def moments(first, second, projected):
    new_first = beta_one * first + (1.0 - beta_one) * projected
    new_second = beta_two * second + (1.0 - beta_two) * projected * projected
    return new_first, new_second


def step_kernel(
    at_ref, mixed_ref, projector_ref, grad_ref, gathered_ref, own_first_ref, own_second_ref,
    update_ref, new_first_ref, new_second_ref, projected_ref,
):
    projected_ref[...] = lax.dot_general(
        mixed_ref[...], grad_ref[...], (((1,), (1,)), ((), ())), preferred_element_type=f32
    )
    owned = own_first_ref.shape[0]
    first = gathered_ref[:, :owned, :].reshape(projected_ref.shape).astype(f32)
    second = gathered_ref[:, owned:, :].reshape(projected_ref.shape).astype(f32)
    new_first, new_second = moments(first, second, projected_ref[...])
    first_hat = new_first / (1.0 - beta_one**ADAM_STEP)
    second_hat = new_second / (1.0 - beta_two**ADAM_STEP)
    normalized = (first_hat / (jnp.sqrt(second_hat) + adam_epsilon)).astype(bf16)
    update_ref[...] = lax.dot_general(
        normalized, projector_ref[...], (((0,), (0,)), ((), ())), preferred_element_type=f32
    )
    mine = projected_ref[pl.ds(pl.multiple_of(at_ref[0] * owned, owned), owned), :]
    new_first_ref[...], new_second_ref[...] = moments(own_first_ref[...], own_second_ref[...], mine)


def adam_step(at, mixed, projector, grad_turned, gathered, own_first, own_second):
    width, tokens = grad_turned.shape
    rank, features = projector.shape
    owned = own_first.shape[0]
    whole = lambda shape: pl.BlockSpec(shape, lambda i, at: (0, 0))
    strip = lambda rows: pl.BlockSpec((rows, TILE), lambda i, at: (0, i))
    turned = lambda columns: pl.BlockSpec((TILE, columns), lambda i, at: (i, 0))
    return pl.pallas_call(
        step_kernel,
        out_shape=(
            jax.ShapeDtypeStruct((width, features), f32),
            jax.ShapeDtypeStruct((owned, width), f32),
            jax.ShapeDtypeStruct((owned, width), f32),
        ),
        grid_spec=pltpu.PrefetchScalarGridSpec(
            num_scalar_prefetch=1,
            grid=(pl.cdiv(width, TILE),),
            in_specs=[
                whole((rank, tokens)),
                whole((rank, features)),
                turned(tokens),
                pl.BlockSpec((rank // owned, 2 * owned, TILE), lambda i, at: (0, 0, i)),
                strip(owned),
                strip(owned),
            ],
            out_specs=[turned(features), strip(owned), strip(owned)],
            scratch_shapes=[pltpu.VMEM((rank, TILE), f32)],
        ),
        compiler_params=pltpu.CompilerParams(vmem_limit_bytes=48 << 20),
        cost_estimate=pl.CostEstimate(
            flops=2 * rank * width * (tokens + features),
            bytes_accessed=width * (2 * tokens + 4 * rank + 4 * features + 16 * owned),
            transcendentals=rank * width,
        ),
        name="adam_step",
    )(at, mixed, projector, grad_turned, gathered, own_first, own_second)


def local(layer_input, output_grad, sketch, first_moment, second_moment):
    tokens, features = layer_input.shape
    columns = sketch.shape[1]
    own = columns // 8
    share = tokens // 128
    grad_turned = output_grad.T
    both = jnp.concatenate([first_moment.astype(bf16), second_moment.astype(bf16)], axis=0)
    gathered = lax.all_gather(both, "row", axis=0, tiled=False)

    partial = sketched_term(sketch.T, grad_turned, layer_input)
    half = scatter_sum(partial.reshape(2, columns // 2, features), "core")
    owned_rows = scatter_sum(half.reshape(4, own, features), "y")
    sketched = gather(gather(owned_rows, "y").reshape(columns // 2, features), "core")
    sketched = sketched.reshape(columns, features)

    own_tokens = lax.dynamic_index_in_dim(
        layer_input.reshape(4, 4, 8, share, features), lax.axis_index("col"), 2, keepdims=False
    ).reshape(4, 4 * share, features)
    left = jnp.concatenate(
        [jnp.broadcast_to(owned_rows, (4, own, features)), own_tokens.astype(f32)], axis=1
    )
    both_terms = lax.dot_general(
        left.reshape(4 * (own + 4 * share), features), sketched, (((1,), (1,)), ((), ())),
        precision=HIGHEST, preferred_element_type=f32,
    )
    both_terms = scatter_sum(both_terms.reshape(4, own + 4 * share, columns), "x")
    both_terms = jnp.concatenate(
        [
            jnp.broadcast_to(both_terms[:own], (4, own, columns)),
            both_terms[own:].reshape(4, share, columns),
        ],
        axis=1,
    )
    both_terms = scatter_sum(both_terms, "z")
    mixed, gathered = lax.optimization_barrier((both_terms[own:], gathered))
    mixed = lax.all_gather(mixed, ("row", "col"), axis=0, tiled=False).reshape(128, share, columns)
    gram = gather(gather(both_terms[:own], "y").reshape(columns // 2, columns), "core")

    inverse = inverse_factor(gram.reshape(columns, columns))
    basis = jnp.dot(inverse, sketched, precision=lax.Precision.HIGH, preferred_element_type=f32)
    projector = basis[:RANK].astype(bf16)
    turned_mixed = mixed_tokens(inverse, mixed)
    at = lax.axis_index("row").astype(jnp.int32).reshape(1)
    update, new_first, new_second = adam_step(
        at, turned_mixed, projector, grad_turned, gathered, first_moment, second_moment
    )
    return update.T, new_first, new_second


def solution(mesh):
    placed = (P(None, "row"), P(None, "col"), P("col", None), P("row", "col"), P("row", "col"))
    return jax.shard_map(
        local,
        mesh=mesh,
        in_specs=placed,
        out_specs=(P("row", "col"), P("row", "col"), P("row", "col")),
        check_vma=False,
    )
```

```python
import jax
import jax.numpy as jnp
from jax import lax
from jax.experimental import pallas as pl
from jax.experimental.pallas import tpu as pltpu
from jax.sharding import PartitionSpec as P

RANK = 512
ADAM_STEP = 10
BLOCK = 128
TILE = 1024
MIX_TILE = 768
PART, STEP = 24, 16

beta_one = 0.9
beta_two = 0.999
adam_epsilon = 1e-08

f32 = jnp.float32
bf16 = jnp.bfloat16
HIGHEST = lax.Precision.HIGHEST

EXTENT = {"x": 4, "z": 4, "y": 4, "core": 2}
HOME = {"x": ("row", 4), "z": ("row", 1), "y": ("col", 2), "core": ("col", 1)}


def place(sub):
    axis, stride = HOME[sub]
    return lax.axis_index(axis) // stride % EXTENT[sub]


def shift(value, sub, by):
    axis, stride = HOME[sub]
    n = EXTENT[sub]
    pairs = []
    for i in range(16 if axis == "row" else 8):
        at = i // stride % n
        pairs.append((i, i + ((at + by) % n - at) * stride))
    return lax.ppermute(value, axis, pairs)


def scatter_sum(value, sub):
    n, me = EXTENT[sub], place(sub)
    pick = lambda k: lax.dynamic_index_in_dim(value, (me + k) % n, 0, keepdims=False)
    got = [shift(pick(k), sub, k) for k in range(1, n)]
    total = pick(0)
    for term in got:
        total = total + term
    return total


def gather(value, sub):
    n, me = EXTENT[sub], place(sub)
    got = [value] + [shift(value, sub, k) for k in range(1, n)]
    out = jnp.zeros((n,) + value.shape, value.dtype)
    for k in range(n):
        out = lax.dynamic_update_index_in_dim(out, got[k], (me - k) % n, 0)
    return out


def full_sum(value, sub):
    total = value
    for k in range(1, EXTENT[sub]):
        total = total + shift(value, sub, k)
    return total


def lane_of(value, k):
    return jnp.take_along_axis(value, jnp.full(value.shape, k, jnp.int32), axis=1)


def row_of(value, k):
    return jnp.broadcast_to(value[k : k + 1], value.shape)


def reciprocal(value):
    guess = pl.reciprocal(value, approx=True)
    guess = guess * (2.0 - value * guess)
    return guess * (2.0 - value * guess)


def invert_block(rows, lane, sub):
    rows, scale = list(rows), []
    for g in range(len(rows)):
        group = (lane >= 8 * g) & (lane < 8 * g + 8)
        column = [lane_of(rows[g], 8 * g + m) for m in range(8)]
        now = jnp.where(group, jnp.where(lane == 8 * g + sub, 1.0, 0.0), rows[g])
        units, inverses, tops, diagonal = [], [], {}, None
        for k in range(8):
            pivot = row_of(column[k], k)
            inverses.append(reciprocal(pivot))
            units.append(row_of(now, k))
            factor = jnp.where(sub > k, column[k] * inverses[k], 0.0)
            for m in range(k + 1, 8):
                tops[k, m] = row_of(column[m], k)
                column[m] = column[m] - factor * tops[k, m]
            now = now - factor * units[k]
            diagonal = pivot if k == 0 else jnp.where(sub == k, pivot, diagonal)
        rows[g] = now
        scale.append(lax.rsqrt(diagonal))
        for h in range(g + 1, len(rows)):
            column = [lane_of(rows[h], 8 * g + m) for m in range(8)]
            now = jnp.where(group, 0.0, rows[h])
            for k in range(8):
                factor = column[k] * inverses[k]
                for m in range(k + 1, 8):
                    column[m] = column[m] - factor * tops[k, m]
                now = now - factor * units[k]
            rows[h] = now
    return [a * b for a, b in zip(rows, scale)]


def factor_kernel(gram_ref, out_ref, work):
    size, padded = gram_ref.shape[0], work.shape[0]
    work[...] = jnp.zeros_like(work)
    work[:size, :size] = gram_ref[...]
    lane = lax.broadcasted_iota(jnp.int32, (8, BLOCK), 1)
    sub = lax.broadcasted_iota(jnp.int32, (8, BLOCK), 0)
    lanes = lax.broadcasted_iota(jnp.int32, (BLOCK, padded), 1)

    def diagonal_inverse(o, n):
        rows = [work[pl.ds(pl.multiple_of(o + 8 * h, 8), 8), pl.ds(o, BLOCK)] for h in range(n // 8)]
        inverse = jnp.concatenate(invert_block(rows, lane, sub), axis=0)
        row_in = lax.broadcasted_iota(jnp.int32, (n, BLOCK), 0)
        lane_in = lax.broadcasted_iota(jnp.int32, (n, BLOCK), 1)
        return jnp.where(row_in >= lane_in, inverse, 0.0)

    def step(b, carry):
        o = pl.multiple_of(b * BLOCK, BLOCK)
        here = pl.ds(o, BLOCK)
        inverse = diagonal_inverse(o, BLOCK)
        panel = work[here, :]
        work[:, here] = jnp.zeros((padded, BLOCK), f32)
        solved = jnp.dot(inverse, panel, precision=HIGHEST, preferred_element_type=f32)
        work[here, :] = solved
        work[here, here] = inverse
        later = jnp.where(lanes >= o + BLOCK, solved, 0.0)
        work[...] -= lax.dot_general(
            later, work[here, :], (((0,), (0,)), ((), ())), precision=HIGHEST, preferred_element_type=f32
        )
        return carry

    lax.fori_loop(0, size // BLOCK, step, 0)
    o, n = size // BLOCK * BLOCK, size % BLOCK
    if n:
        inverse = diagonal_inverse(o, n)
        work[o:size, :] = jnp.dot(
            inverse[:, :n], work[o:size, :], precision=HIGHEST, preferred_element_type=f32
        )
        work[o:size, o:] = inverse
    row_at = lax.broadcasted_iota(jnp.int32, (padded, padded), 0)
    lane_at = lax.broadcasted_iota(jnp.int32, (padded, padded), 1)
    out_ref[...] = jnp.where(row_at >= lane_at, work[...], 0.0)[:size, :size]


def inverse_factor(gram):
    size = gram.shape[0]
    padded = pl.cdiv(size, BLOCK) * BLOCK
    return pl.pallas_call(
        factor_kernel,
        out_shape=jax.ShapeDtypeStruct((size, size), f32),
        in_specs=[pl.BlockSpec(memory_space=pltpu.VMEM)],
        out_specs=pl.BlockSpec(memory_space=pltpu.VMEM),
        scratch_shapes=[pltpu.VMEM((padded, padded), f32)],
        compiler_params=pltpu.CompilerParams(vmem_limit_bytes=32 << 20),
        cost_estimate=pl.CostEstimate(flops=12 * size**3, bytes_accessed=8 * size**2, transcendentals=0),
        name="inverse_factor",
    )(gram)


def two_parts(value):
    high = value.astype(bf16)
    return high, (value - high.astype(f32)).astype(bf16)


def pack_kernel(first_ref, second_ref, out_ref):
    owned = first_ref.shape[0]
    out_ref[:owned, :] = first_ref[...].astype(out_ref.dtype)
    out_ref[owned:, :] = second_ref[...].astype(out_ref.dtype)


def pack(first, second):
    owned, width = first.shape
    return pl.pallas_call(
        pack_kernel,
        out_shape=jax.ShapeDtypeStruct((2 * owned, width), bf16),
        name="pack",
    )(first, second)


def sketched_term(sketch_turned, grad_turned, layer_input):
    token_sketch = jnp.dot(sketch_turned, grad_turned, preferred_element_type=f32)
    high, low = two_parts(token_sketch)
    times = lambda part: jnp.dot(part, layer_input, preferred_element_type=f32)
    return times(high) + times(low)


def mix_kernel(inverse_ref, mixed_ref, out_ref):
    high, low = two_parts(mixed_ref[...])
    inverse_high, inverse_low = two_parts(inverse_ref[...])
    times = lambda a, b: lax.dot_general(a, b, (((1,), (1,)), ((), ())), preferred_element_type=f32)
    total = times(inverse_high, low) + times(inverse_low, high) + times(inverse_high, high)
    out_ref[...] = total.astype(out_ref.dtype)


def mixed_tokens(inverse, mixed):
    tokens, columns = mixed.shape
    return pl.pallas_call(
        mix_kernel,
        out_shape=jax.ShapeDtypeStruct((RANK, tokens), bf16),
        grid=(tokens // MIX_TILE,),
        in_specs=[
            pl.BlockSpec((RANK, columns), lambda i: (0, 0)),
            pl.BlockSpec((MIX_TILE, columns), lambda i: (i, 0)),
        ],
        out_specs=pl.BlockSpec((RANK, MIX_TILE), lambda i: (0, i)),
        compiler_params=pltpu.CompilerParams(vmem_limit_bytes=48 << 20),
        cost_estimate=pl.CostEstimate(
            flops=6 * RANK * columns * tokens,
            bytes_accessed=4 * tokens * columns + 2 * RANK * tokens,
            transcendentals=0,
        ),
        name="mixed_tokens",
    )(inverse, mixed)


def moments(first, second, projected):
    new_first = beta_one * first + (1.0 - beta_one) * projected
    new_second = beta_two * second + (1.0 - beta_two) * projected * projected
    return new_first, new_second


def step_kernel(
    at_ref, mixed_ref, projector_ref, grad_ref, gathered_ref, own_first_ref, own_second_ref,
    update_ref, new_first_ref, new_second_ref, projected_ref,
):
    projected_ref[...] = lax.dot_general(
        mixed_ref[...], grad_ref[...], (((1,), (1,)), ((), ())), preferred_element_type=f32
    )
    owned = own_first_ref.shape[0]
    first = gathered_ref[:, :owned, :].reshape(projected_ref.shape).astype(f32)
    second = gathered_ref[:, owned:, :].reshape(projected_ref.shape).astype(f32)
    new_first, new_second = moments(first, second, projected_ref[...])
    root = (1.0 - beta_two**ADAM_STEP) ** 0.5
    below = jnp.sqrt(new_second) + adam_epsilon * root
    normalized = (new_first * (root / (1.0 - beta_one**ADAM_STEP)) * pl.reciprocal(below)).astype(bf16)
    update_ref[...] = lax.dot_general(
        normalized, projector_ref[...], (((0,), (0,)), ((), ())), preferred_element_type=f32
    )
    mine = projected_ref[pl.ds(pl.multiple_of(at_ref[0] * owned, owned), owned), :]
    new_first_ref[...], new_second_ref[...] = moments(own_first_ref[...], own_second_ref[...], mine)


def adam_step(at, mixed, projector, grad_turned, gathered, own_first, own_second):
    width, tokens = grad_turned.shape
    rank, features = projector.shape
    owned = own_first.shape[0]
    whole = lambda shape: pl.BlockSpec(shape, lambda i, at: (0, 0))
    strip = lambda rows: pl.BlockSpec((rows, TILE), lambda i, at: (0, i))
    turned = lambda columns: pl.BlockSpec((TILE, columns), lambda i, at: (i, 0))
    return pl.pallas_call(
        step_kernel,
        out_shape=(
            jax.ShapeDtypeStruct((width, features), f32),
            jax.ShapeDtypeStruct((owned, width), f32),
            jax.ShapeDtypeStruct((owned, width), f32),
        ),
        grid_spec=pltpu.PrefetchScalarGridSpec(
            num_scalar_prefetch=1,
            grid=(pl.cdiv(width, TILE),),
            in_specs=[
                whole((rank, tokens)),
                whole((rank, features)),
                turned(tokens),
                pl.BlockSpec((rank // owned, 2 * owned, TILE), lambda i, at: (0, 0, i)),
                strip(owned),
                strip(owned),
            ],
            out_specs=[turned(features), strip(owned), strip(owned)],
            scratch_shapes=[pltpu.VMEM((rank, TILE), f32)],
        ),
        compiler_params=pltpu.CompilerParams(vmem_limit_bytes=48 << 20),
        cost_estimate=pl.CostEstimate(
            flops=2 * rank * width * (tokens + features),
            bytes_accessed=width * (2 * tokens + 4 * rank + 4 * features + 16 * owned),
            transcendentals=rank * width,
        ),
        name="adam_step",
    )(at, mixed, projector, grad_turned, gathered, own_first, own_second)


def local(layer_input, output_grad, sketch, first_moment, second_moment):
    tokens, features = layer_input.shape
    columns = sketch.shape[1]
    own = columns // 8
    share = tokens // 128
    grad_turned = output_grad.T
    gathered = lax.all_gather(pack(first_moment, second_moment), "row", axis=0, tiled=False)

    partial = sketched_term(sketch.T, grad_turned, layer_input)
    half = scatter_sum(partial.reshape(2, columns // 2, features), "core")
    owned_rows = scatter_sum(half.reshape(4, own, features), "y")
    sketched = gather(gather(owned_rows, "y").reshape(columns // 2, features), "core")
    sketched = sketched.reshape(columns, features)

    own_tokens = lax.dynamic_index_in_dim(
        layer_input.reshape(4, 4, 8, share, features), lax.axis_index("col"), 2, keepdims=False
    ).reshape(4, 4 * share, features)
    left = [[owned_rows[k * STEP : k * STEP + PART], own_tokens[k].astype(f32)] for k in range(4)]
    terms = lax.dot_general(
        jnp.concatenate(sum(left, []), axis=0), sketched, (((1,), (1,)), ((), ())),
        precision=HIGHEST, preferred_element_type=f32,
    )
    terms = scatter_sum(terms.reshape(4, PART + 4 * share, columns), "x")
    terms = jnp.concatenate(
        [
            jnp.broadcast_to(terms[:PART], (4, PART, columns)),
            terms[PART:].reshape(4, share, columns),
        ],
        axis=1,
    )
    terms = scatter_sum(terms, "z")
    mixed = gather(gather(terms[PART:], "core"), "y").reshape(8 * share, columns)
    mixed, gathered = lax.optimization_barrier((mixed, gathered))
    mixed = lax.all_gather(mixed, "row", axis=0, tiled=True)
    gram = gather(terms[:PART], "x")
    gram = jnp.concatenate([gram[0, :STEP], gram[1, :STEP], gram[2, :STEP], gram[3]], axis=0)
    gram = gather(gather(gram, "y").reshape(columns // 2, columns), "core")

    inverse = inverse_factor(gram.reshape(columns, columns))
    basis = jnp.dot(inverse, sketched, precision=lax.Precision.HIGH, preferred_element_type=f32)
    projector = basis[:RANK].astype(bf16)
    turned_mixed = mixed_tokens(inverse, mixed)
    at = lax.axis_index("row").astype(jnp.int32).reshape(1)
    update, new_first, new_second = adam_step(
        at, turned_mixed, projector, grad_turned, gathered, first_moment, second_moment
    )
    return update.T, new_first, new_second


def solution(mesh):
    placed = (P(None, "row"), P(None, "col"), P("col", None), P("row", "col"), P("row", "col"))
    return jax.shard_map(
        local,
        mesh=mesh,
        in_specs=placed,
        out_specs=(P("row", "col"), P("row", "col"), P("row", "col")),
        check_vma=False,
    )
```

```python
import jax
import jax.numpy as jnp
from jax import lax
from jax.experimental import pallas as pl
from jax.experimental.pallas import tpu as pltpu
from jax.sharding import PartitionSpec as P

RANK = 512
ADAM_STEP = 10
BLOCK = 128
TILE = 512
MIX_TILE = 512
STEP_VMEM = 30 << 20
PART, STEP = 24, 16

beta_one = 0.9
beta_two = 0.999
adam_epsilon = 1e-08

f32 = jnp.float32
bf16 = jnp.bfloat16
HIGHEST = lax.Precision.HIGHEST

EXTENT = {"x": 4, "z": 4, "y": 4, "core": 2}
HOME = {"x": ("row", 4), "z": ("row", 1), "y": ("col", 2), "core": ("col", 1)}


def place(sub):
    axis, stride = HOME[sub]
    return lax.axis_index(axis) // stride % EXTENT[sub]


def shift(value, sub, by):
    axis, stride = HOME[sub]
    n = EXTENT[sub]
    pairs = []
    for i in range(16 if axis == "row" else 8):
        at = i // stride % n
        pairs.append((i, i + ((at + by) % n - at) * stride))
    return lax.ppermute(value, axis, pairs)


def scatter_sum(value, sub, wire=f32):
    n, me = EXTENT[sub], place(sub)
    pick = lambda k: lax.dynamic_index_in_dim(value, (me + k) % n, 0, keepdims=False)
    got = [shift(pick(k).astype(wire), sub, k) for k in range(1, n)]
    total = pick(0)
    for term in got:
        total = total + term.astype(value.dtype)
    return total


def gather(value, sub):
    n, me = EXTENT[sub], place(sub)
    got = [value] + [shift(value, sub, k) for k in range(1, n)]
    out = jnp.zeros((n,) + value.shape, value.dtype)
    for k in range(n):
        out = lax.dynamic_update_index_in_dim(out, got[k], (me - k) % n, 0)
    return out


def lane_of(value, k):
    return jnp.take_along_axis(value, jnp.full(value.shape, k, jnp.int32), axis=1)


def row_of(value, k):
    return jnp.broadcast_to(value[k : k + 1], value.shape)


def reciprocal(value):
    guess = pl.reciprocal(value, approx=True)
    guess = guess * (2.0 - value * guess)
    return guess * (2.0 - value * guess)


def invert_block(rows, lane, sub):
    rows, scale = list(rows), []
    for g in range(len(rows)):
        group = (lane >= 8 * g) & (lane < 8 * g + 8)
        column = [lane_of(rows[g], 8 * g + m) for m in range(8)]
        now = jnp.where(group, jnp.where(lane == 8 * g + sub, 1.0, 0.0), rows[g])
        units, inverses, tops, diagonal = [], [], {}, None
        for k in range(8):
            pivot = row_of(column[k], k)
            inverses.append(reciprocal(pivot))
            units.append(row_of(now, k))
            factor = jnp.where(sub > k, column[k] * inverses[k], 0.0)
            for m in range(k + 1, 8):
                tops[k, m] = row_of(column[m], k)
                column[m] = column[m] - factor * tops[k, m]
            now = now - factor * units[k]
            diagonal = pivot if k == 0 else jnp.where(sub == k, pivot, diagonal)
        rows[g] = now
        scale.append(lax.rsqrt(diagonal))
        for h in range(g + 1, len(rows)):
            column = [lane_of(rows[h], 8 * g + m) for m in range(8)]
            now = jnp.where(group, 0.0, rows[h])
            for k in range(8):
                factor = column[k] * inverses[k]
                for m in range(k + 1, 8):
                    column[m] = column[m] - factor * tops[k, m]
                now = now - factor * units[k]
            rows[h] = now
    return [a * b for a, b in zip(rows, scale)]


def factor_kernel(gram_ref, out_ref, work):
    size, padded = gram_ref.shape[0], work.shape[0]
    work[...] = jnp.zeros_like(work)
    work[:size, :size] = gram_ref[...]
    lane = lax.broadcasted_iota(jnp.int32, (8, BLOCK), 1)
    sub = lax.broadcasted_iota(jnp.int32, (8, BLOCK), 0)
    lanes = lax.broadcasted_iota(jnp.int32, (BLOCK, padded), 1)

    def diagonal_inverse(o, n):
        rows = [work[pl.ds(pl.multiple_of(o + 8 * h, 8), 8), pl.ds(o, BLOCK)] for h in range(n // 8)]
        inverse = jnp.concatenate(invert_block(rows, lane, sub), axis=0)
        row_in = lax.broadcasted_iota(jnp.int32, (n, BLOCK), 0)
        lane_in = lax.broadcasted_iota(jnp.int32, (n, BLOCK), 1)
        return jnp.where(row_in >= lane_in, inverse, 0.0)

    def step(b, carry):
        o = pl.multiple_of(b * BLOCK, BLOCK)
        here = pl.ds(o, BLOCK)
        inverse = diagonal_inverse(o, BLOCK)
        panel = work[here, :]
        work[:, here] = jnp.zeros((padded, BLOCK), f32)
        solved = jnp.dot(inverse, panel, precision=HIGHEST, preferred_element_type=f32)
        work[here, :] = solved
        work[here, here] = inverse
        later = jnp.where(lanes >= o + BLOCK, solved, 0.0)
        work[...] -= lax.dot_general(
            later, work[here, :], (((0,), (0,)), ((), ())), precision=HIGHEST, preferred_element_type=f32
        )
        return carry

    lax.fori_loop(0, size // BLOCK, step, 0)
    o, n = size // BLOCK * BLOCK, size % BLOCK
    if n:
        inverse = diagonal_inverse(o, n)
        work[o:size, :] = jnp.dot(
            inverse[:, :n], work[o:size, :], precision=HIGHEST, preferred_element_type=f32
        )
        work[o:size, o:] = inverse
    row_at = lax.broadcasted_iota(jnp.int32, (padded, padded), 0)
    lane_at = lax.broadcasted_iota(jnp.int32, (padded, padded), 1)
    out_ref[...] = jnp.where(row_at >= lane_at, work[...], 0.0)[:size, :size]


def inverse_factor(gram):
    size = gram.shape[0]
    padded = pl.cdiv(size, BLOCK) * BLOCK
    return pl.pallas_call(
        factor_kernel,
        out_shape=jax.ShapeDtypeStruct((size, size), f32),
        in_specs=[pl.BlockSpec(memory_space=pltpu.VMEM)],
        out_specs=pl.BlockSpec(memory_space=pltpu.VMEM),
        scratch_shapes=[pltpu.VMEM((padded, padded), f32)],
        compiler_params=pltpu.CompilerParams(vmem_limit_bytes=32 << 20),
        cost_estimate=pl.CostEstimate(flops=12 * size**3, bytes_accessed=8 * size**2, transcendentals=0),
        name="inverse_factor",
    )(gram)


def two_parts(value):
    high = value.astype(bf16)
    return high, (value - high.astype(f32)).astype(bf16)


def pack_kernel(first_ref, second_ref, out_ref):
    owned = first_ref.shape[0]
    out_ref[:owned, :] = first_ref[...].astype(out_ref.dtype)
    out_ref[owned:, :] = second_ref[...].astype(out_ref.dtype)


def pack(first, second):
    owned, width = first.shape
    return pl.pallas_call(
        pack_kernel,
        out_shape=jax.ShapeDtypeStruct((2 * owned, width), bf16),
        name="pack",
    )(first, second)


def sketched_term(sketch_turned, grad_turned, layer_input):
    token_sketch = jnp.dot(sketch_turned, grad_turned, preferred_element_type=f32)
    rounded = lax.reduce_precision(token_sketch, 8, 7)
    high, low = rounded.astype(bf16), (token_sketch - rounded).astype(bf16)
    times = lambda part: jnp.dot(part, layer_input, preferred_element_type=f32)
    return times(high) + times(low)


def moments(first, second, projected):
    new_first = beta_one * first + (1.0 - beta_one) * projected
    new_second = beta_two * second + (1.0 - beta_two) * projected * projected
    return new_first, new_second


def step_kernel(
    at_ref, inverse_ref, sketched_ref, mixed_ref, grad_ref, gathered_ref, own_first_ref, own_second_ref,
    update_ref, new_first_ref, new_second_ref, projector_ref, turned_ref, projected_ref,
):
    @pl.when(pl.program_id(0) == 0)
    def _():
        high, low = two_parts(inverse_ref[...])
        values = sketched_ref[...]
        projector_ref[...] = (
            jnp.dot(low, values, preferred_element_type=f32)
            + jnp.dot(high, values, preferred_element_type=f32)
        ).astype(bf16)
        times = lambda a, b: lax.dot_general(a, b, (((1,), (1,)), ((), ())), preferred_element_type=f32)
        for o in range(0, mixed_ref.shape[0], MIX_TILE):
            here = pl.ds(o, MIX_TILE)
            mixed_high, mixed_low = two_parts(mixed_ref[here, :])
            turned_ref[:, here] = (
                times(high, mixed_low) + times(low, mixed_high) + times(high, mixed_high)
            ).astype(bf16)

    projected_ref[...] = lax.dot_general(
        turned_ref[...], grad_ref[...], (((1,), (1,)), ((), ())), preferred_element_type=f32
    )
    owned = own_first_ref.shape[0]
    first = gathered_ref[:, :owned, :].reshape(projected_ref.shape).astype(f32)
    second = gathered_ref[:, owned:, :].reshape(projected_ref.shape).astype(f32)
    new_first, new_second = moments(first, second, projected_ref[...])
    root = (1.0 - beta_two**ADAM_STEP) ** 0.5
    below = jnp.sqrt(new_second) + adam_epsilon * root
    normalized = (new_first * (root / (1.0 - beta_one**ADAM_STEP)) * pl.reciprocal(below)).astype(bf16)
    update_ref[...] = lax.dot_general(
        normalized, projector_ref[...], (((0,), (0,)), ((), ())), preferred_element_type=f32
    )
    mine = projected_ref[pl.ds(pl.multiple_of(at_ref[0] * owned, owned), owned), :]
    new_first_ref[...], new_second_ref[...] = moments(own_first_ref[...], own_second_ref[...], mine)


def adam_step(at, inverse, sketched, mixed, grad_turned, gathered, own_first, own_second):
    width, tokens = grad_turned.shape
    columns, features = sketched.shape
    owned = own_first.shape[0]
    whole = lambda shape: pl.BlockSpec(shape, lambda i, at: (0, 0), pipeline_mode=pl.Buffered(1))
    strip = lambda rows: pl.BlockSpec((rows, TILE), lambda i, at: (0, i))
    turned = lambda across: pl.BlockSpec((TILE, across), lambda i, at: (i, 0))
    return pl.pallas_call(
        step_kernel,
        out_shape=(
            jax.ShapeDtypeStruct((width, features), f32),
            jax.ShapeDtypeStruct((owned, width), f32),
            jax.ShapeDtypeStruct((owned, width), f32),
        ),
        grid_spec=pltpu.PrefetchScalarGridSpec(
            num_scalar_prefetch=1,
            grid=(pl.cdiv(width, TILE),),
            in_specs=[
                whole((RANK, columns)),
                whole((columns, features)),
                whole((tokens, columns)),
                turned(tokens),
                pl.BlockSpec((RANK // owned, 2 * owned, TILE), lambda i, at: (0, 0, i)),
                strip(owned),
                strip(owned),
            ],
            out_specs=[turned(features), strip(owned), strip(owned)],
            scratch_shapes=[
                pltpu.VMEM((RANK, features), bf16),
                pltpu.VMEM((RANK, tokens), bf16),
                pltpu.VMEM((RANK, TILE), f32),
            ],
        ),
        compiler_params=pltpu.CompilerParams(vmem_limit_bytes=STEP_VMEM),
        cost_estimate=pl.CostEstimate(
            flops=2 * RANK * width * (tokens + features) + 6 * RANK * columns * tokens,
            bytes_accessed=width * (2 * tokens + 4 * RANK + 4 * features + 16 * owned) + 4 * tokens * columns,
            transcendentals=RANK * width,
        ),
        name="adam_step",
    )(at, inverse, sketched, mixed, grad_turned, gathered, own_first, own_second)


def local(layer_input, output_grad, sketch, first_moment, second_moment):
    tokens, features = layer_input.shape
    columns = sketch.shape[1]
    own = columns // 8
    share = tokens // 128
    grad_turned = output_grad.T
    gathered = lax.all_gather(pack(first_moment, second_moment), "row", axis=0, tiled=False)

    partial = sketched_term(sketch.T, grad_turned, layer_input)
    half = scatter_sum(partial.reshape(2, columns // 2, features), "core", bf16)
    owned_rows = scatter_sum(half.reshape(4, own, features), "y", bf16).astype(bf16)
    sketched = gather(gather(owned_rows, "y").reshape(columns // 2, features), "core")
    sketched = sketched.reshape(columns, features)

    own_tokens = lax.dynamic_index_in_dim(
        layer_input.reshape(4, 4, 8, share, features), lax.axis_index("col"), 2, keepdims=False
    ).reshape(4, 4 * share, features)
    left = [[owned_rows[k * STEP : k * STEP + PART], own_tokens[k]] for k in range(4)]
    terms = lax.dot_general(
        jnp.concatenate(sum(left, []), axis=0), sketched, (((1,), (1,)), ((), ())),
        preferred_element_type=f32,
    )
    terms = scatter_sum(terms.reshape(4, PART + 4 * share, columns), "x")
    terms = jnp.concatenate(
        [
            jnp.broadcast_to(terms[:PART], (4, PART, columns)),
            terms[PART:].reshape(4, share, columns),
        ],
        axis=1,
    )
    terms = scatter_sum(terms, "z")
    mixed = gather(gather(terms[PART:], "core"), "y").reshape(8 * share, columns)
    mixed, gathered = lax.optimization_barrier((mixed, gathered))
    mixed = lax.all_gather(mixed, "row", axis=0, tiled=True)
    gram = gather(terms[:PART], "x")
    gram = jnp.concatenate([gram[0, :STEP], gram[1, :STEP], gram[2, :STEP], gram[3]], axis=0)
    gram = gather(gather(gram, "y").reshape(columns // 2, columns), "core")

    inverse = inverse_factor(gram.reshape(columns, columns))
    at = lax.axis_index("row").astype(jnp.int32).reshape(1)
    update, new_first, new_second = adam_step(
        at, inverse, sketched, mixed, grad_turned, gathered, first_moment, second_moment
    )
    return update.T, new_first, new_second


def solution(mesh):
    placed = (P(None, "row"), P(None, "col"), P("col", None), P("row", "col"), P("row", "col"))
    return jax.shard_map(
        local,
        mesh=mesh,
        in_specs=placed,
        out_specs=(P("row", "col"), P("row", "col"), P("row", "col")),
        check_vma=False,
    )
```

```python
import jax
import jax.numpy as jnp
from jax import lax
from jax.experimental import pallas as pl
from jax.experimental.pallas import tpu as pltpu
from jax.sharding import PartitionSpec as P

RANK = 512
ADAM_STEP = 10
BLOCK = 128
TILE = 1024
MIX_TILE = 512
STEP_VMEM = 50 << 20
PART, STEP = 24, 16

beta_one = 0.9
beta_two = 0.999
adam_epsilon = 1e-08

f32 = jnp.float32
bf16 = jnp.bfloat16
HIGHEST = lax.Precision.HIGHEST

EXTENT = {"x": 4, "z": 4, "y": 4, "core": 2}
HOME = {"x": ("row", 4), "z": ("row", 1), "y": ("col", 2), "core": ("col", 1)}


def place(sub):
    axis, stride = HOME[sub]
    return lax.axis_index(axis) // stride % EXTENT[sub]


def shift(value, sub, by):
    axis, stride = HOME[sub]
    n = EXTENT[sub]
    pairs = []
    for i in range(16 if axis == "row" else 8):
        at = i // stride % n
        pairs.append((i, i + ((at + by) % n - at) * stride))
    return lax.ppermute(value, axis, pairs)


def scatter_sum(value, sub, wire=f32):
    n, me = EXTENT[sub], place(sub)
    pick = lambda k: lax.dynamic_index_in_dim(value, (me + k) % n, 0, keepdims=False)
    got = [shift(pick(k).astype(wire), sub, k) for k in range(1, n)]
    total = pick(0)
    for term in got:
        total = total + term.astype(value.dtype)
    return total


def gather(value, sub):
    n, me = EXTENT[sub], place(sub)
    got = [value] + [shift(value, sub, k) for k in range(1, n)]
    out = jnp.zeros((n,) + value.shape, value.dtype)
    for k in range(n):
        out = lax.dynamic_update_index_in_dim(out, got[k], (me - k) % n, 0)
    return out


def lane_of(value, k):
    return jnp.take_along_axis(value, jnp.full(value.shape, k, jnp.int32), axis=1)


def row_of(value, k):
    return jnp.broadcast_to(value[k : k + 1], value.shape)


def reciprocal(value):
    guess = pl.reciprocal(value, approx=True)
    guess = guess * (2.0 - value * guess)
    return guess * (2.0 - value * guess)


def invert_block(rows, lane, sub):
    rows, scale = list(rows), []
    for g in range(len(rows)):
        group = (lane >= 8 * g) & (lane < 8 * g + 8)
        column = [lane_of(rows[g], 8 * g + m) for m in range(8)]
        now = jnp.where(group, jnp.where(lane == 8 * g + sub, 1.0, 0.0), rows[g])
        units, inverses, tops, diagonal = [], [], {}, None
        for k in range(8):
            pivot = row_of(column[k], k)
            inverses.append(reciprocal(pivot))
            units.append(row_of(now, k))
            factor = jnp.where(sub > k, column[k] * inverses[k], 0.0)
            for m in range(k + 1, 8):
                tops[k, m] = row_of(column[m], k)
                column[m] = column[m] - factor * tops[k, m]
            now = now - factor * units[k]
            diagonal = pivot if k == 0 else jnp.where(sub == k, pivot, diagonal)
        rows[g] = now
        scale.append(lax.rsqrt(diagonal))
        for h in range(g + 1, len(rows)):
            column = [lane_of(rows[h], 8 * g + m) for m in range(8)]
            now = jnp.where(group, 0.0, rows[h])
            for k in range(8):
                factor = column[k] * inverses[k]
                for m in range(k + 1, 8):
                    column[m] = column[m] - factor * tops[k, m]
                now = now - factor * units[k]
            rows[h] = now
    return [a * b for a, b in zip(rows, scale)]


def factor_kernel(gram_ref, out_ref, work):
    size, padded = gram_ref.shape[0], work.shape[0]
    work[...] = jnp.zeros_like(work)
    work[:size, :size] = gram_ref[...]
    lane = lax.broadcasted_iota(jnp.int32, (8, BLOCK), 1)
    sub = lax.broadcasted_iota(jnp.int32, (8, BLOCK), 0)
    lanes = lax.broadcasted_iota(jnp.int32, (BLOCK, padded), 1)

    def diagonal_inverse(o, n):
        rows = [work[pl.ds(pl.multiple_of(o + 8 * h, 8), 8), pl.ds(o, BLOCK)] for h in range(n // 8)]
        inverse = jnp.concatenate(invert_block(rows, lane, sub), axis=0)
        row_in = lax.broadcasted_iota(jnp.int32, (n, BLOCK), 0)
        lane_in = lax.broadcasted_iota(jnp.int32, (n, BLOCK), 1)
        return jnp.where(row_in >= lane_in, inverse, 0.0)

    def step(b, carry):
        o = pl.multiple_of(b * BLOCK, BLOCK)
        here = pl.ds(o, BLOCK)
        inverse = diagonal_inverse(o, BLOCK)
        panel = work[here, :]
        work[:, here] = jnp.zeros((padded, BLOCK), f32)
        solved = jnp.dot(inverse, panel, precision=HIGHEST, preferred_element_type=f32)
        work[here, :] = solved
        work[here, here] = inverse
        later = jnp.where(lanes >= o + BLOCK, solved, 0.0)
        work[...] -= lax.dot_general(
            later, work[here, :], (((0,), (0,)), ((), ())), precision=HIGHEST, preferred_element_type=f32
        )
        return carry

    lax.fori_loop(0, size // BLOCK, step, 0)
    o, n = size // BLOCK * BLOCK, size % BLOCK
    if n:
        inverse = diagonal_inverse(o, n)
        work[o:size, :] = jnp.dot(
            inverse[:, :n], work[o:size, :], precision=HIGHEST, preferred_element_type=f32
        )
        work[o:size, o:] = inverse
    row_at = lax.broadcasted_iota(jnp.int32, (padded, padded), 0)
    lane_at = lax.broadcasted_iota(jnp.int32, (padded, padded), 1)
    out_ref[...] = jnp.where(row_at >= lane_at, work[...], 0.0)[:size, :size]


def inverse_factor(gram):
    size = gram.shape[0]
    padded = pl.cdiv(size, BLOCK) * BLOCK
    return pl.pallas_call(
        factor_kernel,
        out_shape=jax.ShapeDtypeStruct((size, size), f32),
        in_specs=[pl.BlockSpec(memory_space=pltpu.VMEM)],
        out_specs=pl.BlockSpec(memory_space=pltpu.VMEM),
        scratch_shapes=[pltpu.VMEM((padded, padded), f32)],
        compiler_params=pltpu.CompilerParams(vmem_limit_bytes=16 << 20),
        cost_estimate=pl.CostEstimate(flops=160 * size**3, bytes_accessed=8 * size**2, transcendentals=0),
        name="inverse_factor",
    )(gram)


def two_parts(value):
    high = value.astype(bf16)
    return high, (value - high.astype(f32)).astype(bf16)


def pack_kernel(first_ref, second_ref, out_ref):
    owned = first_ref.shape[0]
    out_ref[:owned, :] = first_ref[...].astype(out_ref.dtype)
    out_ref[owned:, :] = second_ref[...].astype(out_ref.dtype)


def pack(first, second):
    owned, width = first.shape
    return pl.pallas_call(
        pack_kernel,
        out_shape=jax.ShapeDtypeStruct((2 * owned, width), bf16),
        name="pack",
    )(first, second)


def sketched_term(sketch_turned, grad_turned, layer_input):
    token_sketch = jnp.dot(sketch_turned, grad_turned, preferred_element_type=f32)
    rounded = lax.reduce_precision(token_sketch, 8, 7)
    high, low = rounded.astype(bf16), (token_sketch - rounded).astype(bf16)
    times = lambda part: jnp.dot(part, layer_input, preferred_element_type=f32)
    return times(high) + times(low)


def moments(first, second, projected):
    new_first = beta_one * first + (1.0 - beta_one) * projected
    new_second = beta_two * second + (1.0 - beta_two) * projected * projected
    return new_first, new_second


def step_kernel(
    at_ref, inverse_ref, sketched_ref, mixed_ref, grad_ref, gathered_ref, own_first_ref, own_second_ref,
    update_ref, new_first_ref, new_second_ref,
    projector, turned, projected, ready, mixed, grad, gathered, arrived, sent,
):
    width, owned = grad_ref.shape[0], own_first_ref.shape[0]
    tiles = [(o, min(TILE, width - o)) for o in range(0, width, TILE)]
    fetch_mixed = pltpu.make_async_copy(mixed_ref, mixed, arrived.at[0])
    fetch_gathered = pltpu.make_async_copy(gathered_ref, gathered, arrived.at[1])
    fetch_grad = [
        pltpu.make_async_copy(grad_ref.at[pl.ds(o, n)], grad.at[pl.ds(o, n)], arrived.at[2 + i])
        for i, (o, n) in enumerate(tiles)
    ]
    fetch_mixed.start()

    high, low = two_parts(inverse_ref[:RANK, :])
    values = sketched_ref[...]
    projector[...] = (
        jnp.dot(low, values, preferred_element_type=f32) + jnp.dot(high, values, preferred_element_type=f32)
    ).astype(bf16)
    times = lambda a, b: lax.dot_general(a, b, (((1,), (1,)), ((), ())), preferred_element_type=f32)
    fetch_mixed.wait()
    fetch_grad[0].start()
    fetch_gathered.start()
    for o in range(0, mixed.shape[0], MIX_TILE):
        here = pl.ds(o, MIX_TILE)
        mixed_high, mixed_low = two_parts(mixed[here, :])
        turned[:, here] = (
            times(high, mixed_low) + times(low, mixed_high) + times(high, mixed_high)
        ).astype(bf16)

    mine = pl.ds(pl.multiple_of(at_ref[0] * owned, owned), owned)
    send = [
        pltpu.make_async_copy(ready.at[i % 2, :n], update_ref.at[pl.ds(o, n)], sent.at[i % 2])
        for i, (o, n) in enumerate(tiles)
    ]
    for i, (o, n) in enumerate(tiles):
        here = pl.ds(o, n)
        fetch_grad[i].wait()
        if i + 1 < len(tiles):
            fetch_grad[i + 1].start()
        projected[:, :n] = times(turned[...], grad[here, :])
        if i == 0:
            fetch_gathered.wait()
        first = gathered[:, :owned, here].reshape(RANK, n).astype(f32)
        second = gathered[:, owned:, here].reshape(RANK, n).astype(f32)
        new_first, new_second = moments(first, second, projected[:, :n])
        root = (1.0 - beta_two**ADAM_STEP) ** 0.5
        below = new_second * lax.rsqrt(new_second) + adam_epsilon * root
        scaled = new_first * (root / (1.0 - beta_one**ADAM_STEP))
        normalized = (scaled * pltpu.reciprocal(below)).astype(bf16)
        if i >= 2:
            send[i - 2].wait()
        ready[i % 2, :n] = lax.dot_general(
            normalized, projector[...], (((0,), (0,)), ((), ())), preferred_element_type=f32
        )
        send[i].start()
        new_first_ref[:, here], new_second_ref[:, here] = moments(
            own_first_ref[:, here], own_second_ref[:, here], projected[mine, :n]
        )
    for copy in send[-2:]:
        copy.wait()


def adam_step(at, inverse, sketched, mixed, grad_turned, gathered, own_first, own_second):
    width, tokens = grad_turned.shape
    columns, features = sketched.shape
    owned = own_first.shape[0]
    inside = pl.BlockSpec(memory_space=pltpu.VMEM)
    outside = pl.BlockSpec(memory_space=pl.ANY)
    return pl.pallas_call(
        step_kernel,
        out_shape=(
            jax.ShapeDtypeStruct((width, features), f32),
            jax.ShapeDtypeStruct((owned, width), f32),
            jax.ShapeDtypeStruct((owned, width), f32),
        ),
        in_specs=[pl.BlockSpec(memory_space=pltpu.SMEM), inside, inside]
        + [outside, outside, outside, inside, inside],
        out_specs=(outside, inside, inside),
        scratch_shapes=[
            pltpu.VMEM((RANK, features), bf16),
            pltpu.VMEM((RANK, tokens), bf16),
            pltpu.VMEM((RANK, TILE), f32),
            pltpu.VMEM((2, TILE, features), f32),
            pltpu.VMEM(mixed.shape, f32),
            pltpu.VMEM(grad_turned.shape, bf16),
            pltpu.VMEM(gathered.shape, bf16),
            pltpu.SemaphoreType.DMA((2 + pl.cdiv(width, TILE),)),
            pltpu.SemaphoreType.DMA((2,)),
        ],
        compiler_params=pltpu.CompilerParams(vmem_limit_bytes=STEP_VMEM),
        cost_estimate=pl.CostEstimate(
            flops=2 * RANK * width * (tokens + features) + 6 * RANK * columns * tokens,
            bytes_accessed=width * (2 * tokens + 4 * RANK + 4 * features + 16 * owned) + 4 * tokens * columns,
            transcendentals=RANK * width,
        ),
        name="adam_step",
    )(at, inverse, sketched, mixed, grad_turned, gathered, own_first, own_second)


def local(layer_input, output_grad, sketch, first_moment, second_moment):
    tokens, features = layer_input.shape
    columns = sketch.shape[1]
    own = columns // 8
    share = tokens // 128
    grad_turned = output_grad.T
    gathered = lax.all_gather(pack(first_moment, second_moment), "row", axis=0, tiled=False)

    partial = sketched_term(sketch.T, grad_turned, layer_input)
    half = scatter_sum(partial.reshape(2, columns // 2, features), "core", bf16)
    owned_rows = scatter_sum(half.reshape(4, own, features), "y", bf16).astype(bf16)
    sketched = gather(gather(owned_rows, "y").reshape(columns // 2, features), "core")
    sketched = sketched.reshape(columns, features)

    own_tokens = lax.dynamic_index_in_dim(
        layer_input.reshape(4, 4, 8, share, features), lax.axis_index("col"), 2, keepdims=False
    ).reshape(4, 4 * share, features)
    left = [[owned_rows[k * STEP : k * STEP + PART], own_tokens[k]] for k in range(4)]
    terms = lax.dot_general(
        jnp.concatenate(sum(left, []), axis=0), sketched, (((1,), (1,)), ((), ())),
        preferred_element_type=f32,
    )
    terms = scatter_sum(terms.reshape(4, PART + 4 * share, columns), "x")
    terms = jnp.concatenate(
        [
            jnp.broadcast_to(terms[:PART], (4, PART, columns)),
            terms[PART:].reshape(4, share, columns),
        ],
        axis=1,
    )
    terms = scatter_sum(terms, "z")
    mixed = gather(gather(terms[PART:], "core"), "y").reshape(8 * share, columns)
    mixed, gathered = lax.optimization_barrier((mixed, gathered))
    mixed = lax.all_gather(mixed, "row", axis=0, tiled=True)
    gram = gather(terms[:PART], "x")
    gram = jnp.concatenate([gram[0, :STEP], gram[1, :STEP], gram[2, :STEP], gram[3]], axis=0)
    gram = gather(gather(gram, "y").reshape(columns // 2, columns), "core")

    inverse = inverse_factor(gram.reshape(columns, columns))
    at = lax.axis_index("row").astype(jnp.int32).reshape(1)
    update, new_first, new_second = adam_step(
        at, inverse, sketched, mixed, grad_turned, gathered, first_moment, second_moment
    )
    return update.T, new_first, new_second


def solution(mesh):
    placed = (P(None, "row"), P(None, "col"), P("col", None), P("row", "col"), P("row", "col"))
    return jax.shard_map(
        local,
        mesh=mesh,
        in_specs=placed,
        out_specs=(P("row", "col"), P("row", "col"), P("row", "col")),
        check_vma=False,
    )
```

```python
import jax
import jax.numpy as jnp
from jax import lax
from jax.experimental import pallas as pl
from jax.experimental.pallas import tpu as pltpu
from jax.sharding import PartitionSpec as P

RANK = 512
ADAM_STEP = 10
BLOCK = 128
TILE = 1024
MIX_TILE = 512
STEP_VMEM = 50 << 20
PART = 40

beta_one = 0.9
beta_two = 0.999
adam_epsilon = 1e-08

f32 = jnp.float32
bf16 = jnp.bfloat16
HIGHEST = lax.Precision.HIGHEST

EXTENT = {"x": 4, "z": 4, "y": 4, "core": 2}
HOME = {"x": ("row", 4), "z": ("row", 1), "y": ("col", 2), "core": ("col", 1)}


def place(sub):
    axis, stride = HOME[sub]
    return lax.axis_index(axis) // stride % EXTENT[sub]


def shift(value, sub, by):
    axis, stride = HOME[sub]
    n = EXTENT[sub]
    pairs = []
    for i in range(16 if axis == "row" else 8):
        at = i // stride % n
        pairs.append((i, i + ((at + by) % n - at) * stride))
    return lax.ppermute(value, axis, pairs)


def scatter_sum(value, sub, wire=f32):
    n, me = EXTENT[sub], place(sub)
    pick = lambda k: lax.dynamic_index_in_dim(value, (me + k) % n, 0, keepdims=False)
    got = [shift(pick(k).astype(wire), sub, k) for k in range(1, n)]
    total = pick(0)
    for term in got:
        total = total + term.astype(value.dtype)
    return total


def gather(value, sub):
    n, me = EXTENT[sub], place(sub)
    got = [value] + [shift(value, sub, k) for k in range(1, n)]
    out = jnp.zeros((n,) + value.shape, value.dtype)
    for k in range(n):
        out = lax.dynamic_update_index_in_dim(out, got[k], (me - k) % n, 0)
    return out


def swap(value, sub, turn):
    axis, stride = HOME[sub]
    pairs = []
    for i in range(16 if axis == "row" else 8):
        at = i // stride % 4
        pairs.append((i, i + ((at ^ turn) - at) * stride))
    return lax.ppermute(value, axis, pairs)


def halving_sum(value, sub):
    me = place(sub)
    pick = lambda k: lax.dynamic_index_in_dim(value, k, 0, keepdims=False)
    kept = jnp.stack([pick(me), pick(3 - me)])
    kept = kept + swap(jnp.stack([pick(me ^ 1), pick(3 - (me ^ 1))]), sub, 1)
    return kept[0] + swap(kept[1], sub, 3)


def doubling_gather(value, sub):
    me = place(sub)
    near = jnp.stack([value, swap(value, sub, 3)])
    far = swap(near, sub, 1)
    out = jnp.zeros((4,) + value.shape, value.dtype)
    for k, piece in ((me, near[0]), (3 - me, near[1]), (me ^ 1, far[0]), (3 - (me ^ 1), far[1])):
        out = lax.dynamic_update_index_in_dim(out, piece, k, 0)
    return out


def row_total(rows):
    upper = (place("x") == 1) | (place("x") == 2)
    lo, hi = rows[:PART], rows[-PART:]
    part = jnp.where(upper, hi, lo) + swap(jnp.where(upper, lo, hi), "x", 1)
    for sub, turn in (("x", 3), ("z", 1), ("z", 3)):
        part = part + swap(part, sub, turn)
    other = swap(part, "x", 1)
    lo, hi = jnp.where(upper, other, part), jnp.where(upper, part, other)
    return jnp.concatenate([lo, hi[2 * PART - rows.shape[0] :]], axis=0)


def lane_of(value, k):
    return jnp.take_along_axis(value, jnp.full(value.shape, k, jnp.int32), axis=1)


def row_of(value, k):
    return jnp.broadcast_to(value[k : k + 1], value.shape)


def reciprocal(value):
    guess = pl.reciprocal(value, approx=True)
    guess = guess * (2.0 - value * guess)
    return guess * (2.0 - value * guess)


def invert_block(rows, lane, sub):
    rows, scale = list(rows), []
    for g in range(len(rows)):
        group = (lane >= 8 * g) & (lane < 8 * g + 8)
        column = [lane_of(rows[g], 8 * g + m) for m in range(8)]
        now = jnp.where(group, jnp.where(lane == 8 * g + sub, 1.0, 0.0), rows[g])
        units, inverses, tops, diagonal = [], [], {}, None
        for k in range(8):
            pivot = row_of(column[k], k)
            inverses.append(reciprocal(pivot))
            units.append(row_of(now, k))
            factor = jnp.where(sub > k, column[k] * inverses[k], 0.0)
            for m in range(k + 1, 8):
                tops[k, m] = row_of(column[m], k)
                column[m] = column[m] - factor * tops[k, m]
            now = now - factor * units[k]
            diagonal = pivot if k == 0 else jnp.where(sub == k, pivot, diagonal)
        rows[g] = now
        scale.append(lax.rsqrt(diagonal))
        for h in range(g + 1, len(rows)):
            column = [lane_of(rows[h], 8 * g + m) for m in range(8)]
            now = jnp.where(group, 0.0, rows[h])
            for k in range(8):
                factor = column[k] * inverses[k]
                for m in range(k + 1, 8):
                    column[m] = column[m] - factor * tops[k, m]
                now = now - factor * units[k]
            rows[h] = now
    return [a * b for a, b in zip(rows, scale)]


def factor_kernel(gram_ref, out_ref, work):
    size, padded = gram_ref.shape[0], work.shape[0]
    work[...] = jnp.zeros_like(work)
    work[:size, :size] = gram_ref[...]
    lane = lax.broadcasted_iota(jnp.int32, (8, BLOCK), 1)
    sub = lax.broadcasted_iota(jnp.int32, (8, BLOCK), 0)
    lanes = lax.broadcasted_iota(jnp.int32, (BLOCK, padded), 1)

    def diagonal_inverse(o, n):
        rows = [work[pl.ds(pl.multiple_of(o + 8 * h, 8), 8), pl.ds(o, BLOCK)] for h in range(n // 8)]
        inverse = jnp.concatenate(invert_block(rows, lane, sub), axis=0)
        row_in = lax.broadcasted_iota(jnp.int32, (n, BLOCK), 0)
        lane_in = lax.broadcasted_iota(jnp.int32, (n, BLOCK), 1)
        return jnp.where(row_in >= lane_in, inverse, 0.0)

    def step(b, carry):
        o = pl.multiple_of(b * BLOCK, BLOCK)
        here = pl.ds(o, BLOCK)
        inverse = diagonal_inverse(o, BLOCK)
        panel = work[here, :]
        work[:, here] = jnp.zeros((padded, BLOCK), f32)
        solved = jnp.dot(inverse, panel, precision=HIGHEST, preferred_element_type=f32)
        work[here, :] = solved
        work[here, here] = inverse
        later = jnp.where(lanes >= o + BLOCK, solved, 0.0)
        work[...] -= lax.dot_general(
            later, work[here, :], (((0,), (0,)), ((), ())), precision=HIGHEST, preferred_element_type=f32
        )
        return carry

    lax.fori_loop(0, size // BLOCK, step, 0)
    o, n = size // BLOCK * BLOCK, size % BLOCK
    if n:
        inverse = diagonal_inverse(o, n)
        work[o:size, :] = jnp.dot(
            inverse[:, :n], work[o:size, :], precision=HIGHEST, preferred_element_type=f32
        )
        work[o:size, o:] = inverse
    row_at = lax.broadcasted_iota(jnp.int32, (padded, padded), 0)
    lane_at = lax.broadcasted_iota(jnp.int32, (padded, padded), 1)
    out_ref[...] = jnp.where(row_at >= lane_at, work[...], 0.0)[:size, :size]


def inverse_factor(gram):
    size = gram.shape[0]
    padded = pl.cdiv(size, BLOCK) * BLOCK
    return pl.pallas_call(
        factor_kernel,
        out_shape=jax.ShapeDtypeStruct((size, size), f32),
        in_specs=[pl.BlockSpec(memory_space=pltpu.VMEM)],
        out_specs=pl.BlockSpec(memory_space=pltpu.VMEM),
        scratch_shapes=[pltpu.VMEM((padded, padded), f32)],
        compiler_params=pltpu.CompilerParams(vmem_limit_bytes=16 << 20),
        cost_estimate=pl.CostEstimate(flops=160 * size**3, bytes_accessed=8 * size**2, transcendentals=0),
        name="inverse_factor",
    )(gram)


def two_parts(value):
    high = value.astype(bf16)
    return high, (value - high.astype(f32)).astype(bf16)


def pack_kernel(first_ref, second_ref, out_ref):
    owned = first_ref.shape[0]
    out_ref[:owned, :] = first_ref[...].astype(out_ref.dtype)
    out_ref[owned:, :] = second_ref[...].astype(out_ref.dtype)


def pack(first, second):
    owned, width = first.shape
    return pl.pallas_call(
        pack_kernel,
        out_shape=jax.ShapeDtypeStruct((2 * owned, width), bf16),
        name="pack",
    )(first, second)


def sketched_term(sketch_turned, grad_turned, layer_input):
    token_sketch = jnp.dot(sketch_turned, grad_turned, preferred_element_type=f32)
    rounded = lax.reduce_precision(token_sketch, 8, 7)
    high, low = rounded.astype(bf16), (token_sketch - rounded).astype(bf16)
    times = lambda part: jnp.dot(part, layer_input, preferred_element_type=f32)
    return times(high) + times(low)


def moments(first, second, projected):
    new_first = beta_one * first + (1.0 - beta_one) * projected
    new_second = beta_two * second + (1.0 - beta_two) * projected * projected
    return new_first, new_second


def step_kernel(
    at_ref, inverse_ref, sketched_ref, mixed_ref, grad_ref, gathered_ref, own_first_ref, own_second_ref,
    update_ref, new_first_ref, new_second_ref,
    projector, turned, projected, ready, mixed, grad, gathered, arrived, sent,
):
    width, owned = grad_ref.shape[0], own_first_ref.shape[0]
    tiles = [(o, min(TILE, width - o)) for o in range(0, width, TILE)]
    fetch_mixed = pltpu.make_async_copy(mixed_ref, mixed, arrived.at[0])
    fetch_gathered = pltpu.make_async_copy(gathered_ref, gathered, arrived.at[1])
    fetch_grad = [
        pltpu.make_async_copy(grad_ref.at[pl.ds(o, n)], grad.at[pl.ds(o, n)], arrived.at[2 + i])
        for i, (o, n) in enumerate(tiles)
    ]
    fetch_mixed.start()

    high, low = two_parts(inverse_ref[:RANK, :RANK])
    values = sketched_ref[:RANK, :]
    projector[...] = (
        jnp.dot(low, values, preferred_element_type=f32) + jnp.dot(high, values, preferred_element_type=f32)
    ).astype(bf16)
    times = lambda a, b: lax.dot_general(a, b, (((1,), (1,)), ((), ())), preferred_element_type=f32)
    fetch_mixed.wait()
    fetch_grad[0].start()
    fetch_gathered.start()
    for o in range(0, mixed.shape[0], MIX_TILE):
        here = pl.ds(o, MIX_TILE)
        mixed_high, mixed_low = two_parts(mixed[here, :])
        turned[:, here] = (
            times(high, mixed_low) + times(low, mixed_high) + times(high, mixed_high)
        ).astype(bf16)

    mine = pl.ds(pl.multiple_of(at_ref[0] * owned, owned), owned)
    send = [
        pltpu.make_async_copy(ready.at[i % 2, :n], update_ref.at[pl.ds(o, n)], sent.at[i % 2])
        for i, (o, n) in enumerate(tiles)
    ]
    for i, (o, n) in enumerate(tiles):
        here = pl.ds(o, n)
        fetch_grad[i].wait()
        if i + 1 < len(tiles):
            fetch_grad[i + 1].start()
        projected[:, :n] = times(turned[...], grad[here, :])
        if i == 0:
            fetch_gathered.wait()
        first = gathered[:, :owned, here].reshape(RANK, n).astype(f32)
        second = gathered[:, owned:, here].reshape(RANK, n).astype(f32)
        new_first, new_second = moments(first, second, projected[:, :n])
        root = (1.0 - beta_two**ADAM_STEP) ** 0.5
        below = new_second * lax.rsqrt(new_second) + adam_epsilon * root
        scaled = new_first * (root / (1.0 - beta_one**ADAM_STEP))
        normalized = (scaled * pltpu.reciprocal(below)).astype(bf16)
        if i >= 2:
            send[i - 2].wait()
        ready[i % 2, :n] = lax.dot_general(
            normalized, projector[...], (((0,), (0,)), ((), ())), preferred_element_type=f32
        )
        send[i].start()
        new_first_ref[:, here], new_second_ref[:, here] = moments(
            own_first_ref[:, here], own_second_ref[:, here], projected[mine, :n]
        )
    for copy in send[-2:]:
        copy.wait()


def adam_step(at, inverse, sketched, mixed, grad_turned, gathered, own_first, own_second):
    width, tokens = grad_turned.shape
    features = sketched.shape[1]
    owned = own_first.shape[0]
    inside = pl.BlockSpec(memory_space=pltpu.VMEM)
    outside = pl.BlockSpec(memory_space=pl.ANY)
    return pl.pallas_call(
        step_kernel,
        out_shape=(
            jax.ShapeDtypeStruct((width, features), f32),
            jax.ShapeDtypeStruct((owned, width), f32),
            jax.ShapeDtypeStruct((owned, width), f32),
        ),
        in_specs=[pl.BlockSpec(memory_space=pltpu.SMEM), inside, inside]
        + [outside, outside, outside, inside, inside],
        out_specs=(outside, inside, inside),
        scratch_shapes=[
            pltpu.VMEM((RANK, features), bf16),
            pltpu.VMEM((RANK, tokens), bf16),
            pltpu.VMEM((RANK, TILE), f32),
            pltpu.VMEM((2, TILE, features), f32),
            pltpu.VMEM(mixed.shape, f32),
            pltpu.VMEM(grad_turned.shape, bf16),
            pltpu.VMEM(gathered.shape, bf16),
            pltpu.SemaphoreType.DMA((2 + pl.cdiv(width, TILE),)),
            pltpu.SemaphoreType.DMA((2,)),
        ],
        compiler_params=pltpu.CompilerParams(vmem_limit_bytes=STEP_VMEM),
        cost_estimate=pl.CostEstimate(
            flops=2 * RANK * width * (tokens + features) + 6 * RANK * RANK * tokens,
            bytes_accessed=width * (2 * tokens + 4 * RANK + 4 * features + 16 * owned) + 4 * tokens * RANK,
            transcendentals=RANK * width,
        ),
        name="adam_step",
    )(at, inverse, sketched, mixed, grad_turned, gathered, own_first, own_second)


def local(layer_input, output_grad, sketch, first_moment, second_moment):
    tokens, features = layer_input.shape
    columns = sketch.shape[1]
    own = columns // 8
    share = tokens // 128
    grad_turned = output_grad.T
    gathered = lax.all_gather(pack(first_moment, second_moment), "row", axis=0, tiled=False)

    partial = sketched_term(sketch.T, grad_turned, layer_input)
    half = scatter_sum(partial.reshape(2, columns // 2, features), "core", bf16)
    owned_rows = scatter_sum(half.reshape(4, own, features), "y", bf16).astype(bf16)
    sketched = gather(gather(owned_rows, "y").reshape(columns // 2, features), "core")
    sketched = sketched.reshape(columns, features)

    own_tokens = lax.dynamic_index_in_dim(
        layer_input.reshape(16, 8, share, features), lax.axis_index("col"), 1, keepdims=False
    ).reshape(tokens // 8, features)
    times = lambda a, b: lax.dot_general(a, b, (((1,), (1,)), ((), ())), preferred_element_type=f32)
    mixed = times(own_tokens, sketched[:RANK])
    mixed = halving_sum(mixed.reshape(4, 4 * share, RANK), "x")
    mixed = halving_sum(mixed.reshape(4, share, RANK), "z")
    mixed = doubling_gather(gather(mixed, "core"), "y").reshape(8 * share, RANK)
    mixed, gathered = lax.optimization_barrier((mixed, gathered))
    mixed = lax.all_gather(mixed, "row", axis=0, tiled=True)

    gram = row_total(times(owned_rows, sketched))
    gram = gather(gather(gram, "y").reshape(columns // 2, columns), "core")

    inverse = inverse_factor(gram.reshape(columns, columns))
    at = lax.axis_index("row").astype(jnp.int32).reshape(1)
    update, new_first, new_second = adam_step(
        at, inverse, sketched, mixed, grad_turned, gathered, first_moment, second_moment
    )
    return update.T, new_first, new_second


def solution(mesh):
    placed = (P(None, "row"), P(None, "col"), P("col", None), P("row", "col"), P("row", "col"))
    return jax.shard_map(
        local,
        mesh=mesh,
        in_specs=placed,
        out_specs=(P("row", "col"), P("row", "col"), P("row", "col")),
        check_vma=False,
    )
```

```python
import jax
import jax.numpy as jnp
from jax import lax
from jax.experimental import pallas as pl
from jax.experimental.pallas import tpu as pltpu
from jax.sharding import PartitionSpec as P

RANK = 512
ADAM_STEP = 10
BLOCK = 128
TILE = 1024
MIX_TILE = 512
STEP_VMEM = 50 << 20

beta_one = 0.9
beta_two = 0.999
adam_epsilon = 1e-08

f32 = jnp.float32
bf16 = jnp.bfloat16
HIGHEST = lax.Precision.HIGHEST

EXTENT = {"x": 4, "z": 4, "y": 4, "core": 2}
HOME = {"x": ("row", 4), "z": ("row", 1), "y": ("col", 2), "core": ("col", 1)}


def place(sub):
    axis, stride = HOME[sub]
    return lax.axis_index(axis) // stride % EXTENT[sub]


def shift(value, sub, by):
    axis, stride = HOME[sub]
    n = EXTENT[sub]
    pairs = []
    for i in range(16 if axis == "row" else 8):
        at = i // stride % n
        pairs.append((i, i + ((at + by) % n - at) * stride))
    return lax.ppermute(value, axis, pairs)


def scatter_sum(value, sub, wire=f32):
    n, me = EXTENT[sub], place(sub)
    pick = lambda k: lax.dynamic_index_in_dim(value, (me + k) % n, 0, keepdims=False)
    got = [shift(pick(k).astype(wire), sub, k) for k in range(1, n)]
    total = pick(0)
    for term in got:
        total = total + term.astype(value.dtype)
    return total


def gather(value, sub):
    n, me = EXTENT[sub], place(sub)
    got = [value] + [shift(value, sub, k) for k in range(1, n)]
    out = jnp.zeros((n,) + value.shape, value.dtype)
    for k in range(n):
        out = lax.dynamic_update_index_in_dim(out, got[k], (me - k) % n, 0)
    return out


def lane_of(value, k):
    return jnp.take_along_axis(value, jnp.full(value.shape, k, jnp.int32), axis=1)


def row_of(value, k):
    return jnp.broadcast_to(value[k : k + 1], value.shape)


def reciprocal(value):
    guess = pl.reciprocal(value, approx=True)
    guess = guess * (2.0 - value * guess)
    return guess * (2.0 - value * guess)


def invert_block(rows, lane, sub):
    rows, scale = list(rows), []
    for g in range(len(rows)):
        group = (lane >= 8 * g) & (lane < 8 * g + 8)
        column = [lane_of(rows[g], 8 * g + m) for m in range(8)]
        now = jnp.where(group, jnp.where(lane == 8 * g + sub, 1.0, 0.0), rows[g])
        units, inverses, tops, diagonal = [], [], {}, None
        for k in range(8):
            pivot = row_of(column[k], k)
            inverses.append(reciprocal(pivot))
            units.append(row_of(now, k))
            factor = jnp.where(sub > k, column[k] * inverses[k], 0.0)
            for m in range(k + 1, 8):
                tops[k, m] = row_of(column[m], k)
                column[m] = column[m] - factor * tops[k, m]
            now = now - factor * units[k]
            diagonal = pivot if k == 0 else jnp.where(sub == k, pivot, diagonal)
        rows[g] = now
        scale.append(lax.rsqrt(diagonal))
        for h in range(g + 1, len(rows)):
            column = [lane_of(rows[h], 8 * g + m) for m in range(8)]
            now = jnp.where(group, 0.0, rows[h])
            for k in range(8):
                factor = column[k] * inverses[k]
                for m in range(k + 1, 8):
                    column[m] = column[m] - factor * tops[k, m]
                now = now - factor * units[k]
            rows[h] = now
    return [a * b for a, b in zip(rows, scale)]


def factor_kernel(gram_ref, out_ref, work):
    size, padded = gram_ref.shape[0], work.shape[0]
    work[...] = jnp.zeros_like(work)
    work[:size, :size] = gram_ref[...]
    lane = lax.broadcasted_iota(jnp.int32, (8, BLOCK), 1)
    sub = lax.broadcasted_iota(jnp.int32, (8, BLOCK), 0)
    lanes = lax.broadcasted_iota(jnp.int32, (BLOCK, padded), 1)

    def diagonal_inverse(o, n):
        rows = [work[pl.ds(pl.multiple_of(o + 8 * h, 8), 8), pl.ds(o, BLOCK)] for h in range(n // 8)]
        inverse = jnp.concatenate(invert_block(rows, lane, sub), axis=0)
        row_in = lax.broadcasted_iota(jnp.int32, (n, BLOCK), 0)
        lane_in = lax.broadcasted_iota(jnp.int32, (n, BLOCK), 1)
        return jnp.where(row_in >= lane_in, inverse, 0.0)

    def step(b, carry):
        o = pl.multiple_of(b * BLOCK, BLOCK)
        here = pl.ds(o, BLOCK)
        inverse = diagonal_inverse(o, BLOCK)
        panel = work[here, :]
        work[:, here] = jnp.zeros((padded, BLOCK), f32)
        solved = jnp.dot(inverse, panel, precision=HIGHEST, preferred_element_type=f32)
        work[here, :] = solved
        work[here, here] = inverse
        later = jnp.where(lanes >= o + BLOCK, solved, 0.0)
        work[...] -= lax.dot_general(
            later, work[here, :], (((0,), (0,)), ((), ())), precision=HIGHEST, preferred_element_type=f32
        )
        return carry

    lax.fori_loop(0, size // BLOCK, step, 0)
    o, n = size // BLOCK * BLOCK, size % BLOCK
    if n:
        inverse = diagonal_inverse(o, n)
        work[o:size, :] = jnp.dot(
            inverse[:, :n], work[o:size, :], precision=HIGHEST, preferred_element_type=f32
        )
        work[o:size, o:] = inverse
    row_at = lax.broadcasted_iota(jnp.int32, (padded, padded), 0)
    lane_at = lax.broadcasted_iota(jnp.int32, (padded, padded), 1)
    out_ref[...] = jnp.where(row_at >= lane_at, work[...], 0.0)[:size, :size]


def inverse_factor(gram):
    size = gram.shape[0]
    padded = pl.cdiv(size, BLOCK) * BLOCK
    return pl.pallas_call(
        factor_kernel,
        out_shape=jax.ShapeDtypeStruct((size, size), f32),
        in_specs=[pl.BlockSpec(memory_space=pltpu.VMEM)],
        out_specs=pl.BlockSpec(memory_space=pltpu.VMEM),
        scratch_shapes=[pltpu.VMEM((padded, padded), f32)],
        compiler_params=pltpu.CompilerParams(vmem_limit_bytes=16 << 20),
        cost_estimate=pl.CostEstimate(flops=160 * size**3, bytes_accessed=8 * size**2, transcendentals=0),
        name="inverse_factor",
    )(gram)


def two_parts(value):
    high = value.astype(bf16)
    return high, (value - high.astype(f32)).astype(bf16)


def pack_kernel(first_ref, second_ref, out_ref):
    owned = first_ref.shape[0]
    out_ref[:owned, :] = first_ref[...].astype(out_ref.dtype)
    out_ref[owned:, :] = second_ref[...].astype(out_ref.dtype)


def pack(first, second):
    owned, width = first.shape
    return pl.pallas_call(
        pack_kernel,
        out_shape=jax.ShapeDtypeStruct((2 * owned, width), bf16),
        name="pack",
    )(first, second)


def sketched_term(sketch_turned, grad_turned, layer_input):
    token_sketch = jnp.dot(sketch_turned, grad_turned, preferred_element_type=f32)
    rounded = lax.reduce_precision(token_sketch, 8, 7)
    high, low = rounded.astype(bf16), (token_sketch - rounded).astype(bf16)
    times = lambda part: jnp.dot(part, layer_input, preferred_element_type=f32)
    return times(high) + times(low)


def moments(first, second, projected):
    new_first = beta_one * first + (1.0 - beta_one) * projected
    new_second = beta_two * second + (1.0 - beta_two) * projected * projected
    return new_first, new_second


def step_kernel(
    at_ref, inverse_ref, sketched_ref, mixed_ref, grad_ref, gathered_ref, own_first_ref, own_second_ref,
    update_ref, new_first_ref, new_second_ref,
    projector, turned, projected, ready, mixed, grad, gathered, arrived, sent,
):
    width, owned = grad_ref.shape[0], own_first_ref.shape[0]
    tiles = [(o, min(TILE, width - o)) for o in range(0, width, TILE)]
    fetch_mixed = pltpu.make_async_copy(mixed_ref, mixed, arrived.at[0])
    fetch_gathered = pltpu.make_async_copy(gathered_ref, gathered, arrived.at[1])
    fetch_grad = [
        pltpu.make_async_copy(grad_ref.at[pl.ds(o, n)], grad.at[pl.ds(o, n)], arrived.at[2 + i])
        for i, (o, n) in enumerate(tiles)
    ]
    fetch_mixed.start()

    high, low = two_parts(inverse_ref[:RANK, :RANK])
    values = sketched_ref[:RANK, :]
    projector[...] = (
        jnp.dot(low, values, preferred_element_type=f32) + jnp.dot(high, values, preferred_element_type=f32)
    ).astype(bf16)
    times = lambda a, b: lax.dot_general(a, b, (((1,), (1,)), ((), ())), preferred_element_type=f32)
    fetch_mixed.wait()
    fetch_grad[0].start()
    fetch_gathered.start()
    for o in range(0, mixed.shape[0], MIX_TILE):
        here = pl.ds(o, MIX_TILE)
        mixed_high, mixed_low = two_parts(mixed[here, :])
        turned[:, here] = (
            times(high, mixed_low) + times(low, mixed_high) + times(high, mixed_high)
        ).astype(bf16)

    mine = pl.ds(pl.multiple_of(at_ref[0] * owned, owned), owned)
    send = [
        pltpu.make_async_copy(ready.at[i % 2, :n], update_ref.at[pl.ds(o, n)], sent.at[i % 2])
        for i, (o, n) in enumerate(tiles)
    ]
    for i, (o, n) in enumerate(tiles):
        here = pl.ds(o, n)
        fetch_grad[i].wait()
        if i + 1 < len(tiles):
            fetch_grad[i + 1].start()
        projected[:, :n] = times(turned[...], grad[here, :])
        if i == 0:
            fetch_gathered.wait()
        first = gathered[:, :owned, here].reshape(RANK, n).astype(f32)
        second = gathered[:, owned:, here].reshape(RANK, n).astype(f32)
        new_first, new_second = moments(first, second, projected[:, :n])
        root = (1.0 - beta_two**ADAM_STEP) ** 0.5
        below = new_second * lax.rsqrt(new_second) + adam_epsilon * root
        scaled = new_first * (root / (1.0 - beta_one**ADAM_STEP))
        normalized = (scaled * pltpu.reciprocal(below)).astype(bf16)
        if i >= 2:
            send[i - 2].wait()
        ready[i % 2, :n] = lax.dot_general(
            normalized, projector[...], (((0,), (0,)), ((), ())), preferred_element_type=f32
        )
        send[i].start()
        new_first_ref[:, here], new_second_ref[:, here] = moments(
            own_first_ref[:, here], own_second_ref[:, here], projected[mine, :n]
        )
    for copy in send[-2:]:
        copy.wait()


def adam_step(at, inverse, sketched, mixed, grad_turned, gathered, own_first, own_second):
    width, tokens = grad_turned.shape
    features = sketched.shape[1]
    owned = own_first.shape[0]
    inside = pl.BlockSpec(memory_space=pltpu.VMEM)
    outside = pl.BlockSpec(memory_space=pl.ANY)
    return pl.pallas_call(
        step_kernel,
        out_shape=(
            jax.ShapeDtypeStruct((width, features), f32),
            jax.ShapeDtypeStruct((owned, width), f32),
            jax.ShapeDtypeStruct((owned, width), f32),
        ),
        in_specs=[pl.BlockSpec(memory_space=pltpu.SMEM), inside, inside]
        + [outside, outside, outside, inside, inside],
        out_specs=(outside, inside, inside),
        scratch_shapes=[
            pltpu.VMEM((RANK, features), bf16),
            pltpu.VMEM((RANK, tokens), bf16),
            pltpu.VMEM((RANK, TILE), f32),
            pltpu.VMEM((2, TILE, features), f32),
            pltpu.VMEM(mixed.shape, f32),
            pltpu.VMEM(grad_turned.shape, bf16),
            pltpu.VMEM(gathered.shape, bf16),
            pltpu.SemaphoreType.DMA((2 + pl.cdiv(width, TILE),)),
            pltpu.SemaphoreType.DMA((2,)),
        ],
        compiler_params=pltpu.CompilerParams(vmem_limit_bytes=STEP_VMEM),
        cost_estimate=pl.CostEstimate(
            flops=2 * RANK * width * (tokens + features) + 6 * RANK * RANK * tokens,
            bytes_accessed=width * (2 * tokens + 4 * RANK + 4 * features + 16 * owned) + 4 * tokens * RANK,
            transcendentals=RANK * width,
        ),
        name="adam_step",
    )(at, inverse, sketched, mixed, grad_turned, gathered, own_first, own_second)


def local(layer_input, output_grad, sketch, first_moment, second_moment):
    tokens, features = layer_input.shape
    columns = sketch.shape[1]
    own = columns // 8
    share = tokens // 128
    grad_turned = output_grad.T
    gathered = lax.all_gather(pack(first_moment, second_moment), "row", axis=0, tiled=False)

    partial = sketched_term(sketch.T, grad_turned, layer_input)
    half = scatter_sum(partial.reshape(2, columns // 2, features), "core", bf16)
    owned_rows = scatter_sum(half.reshape(4, own, features), "y", bf16).astype(bf16)
    sketched = gather(gather(owned_rows, "y").reshape(columns // 2, features), "core")
    sketched = sketched.reshape(columns, features)

    own_tokens = lax.dynamic_index_in_dim(
        layer_input.reshape(16, 8, share, features), lax.axis_index("col"), 1, keepdims=False
    )
    chunks = [owned_rows[8 * (i % (own // 8)) : 8 * (i % (own // 8)) + 8] for i in range(16)]
    left = jnp.concatenate([jnp.stack(chunks), own_tokens], axis=1)
    terms = lax.dot_general(
        left.reshape(16 * (8 + share), features), sketched, (((1,), (1,)), ((), ())),
        preferred_element_type=f32,
    )
    terms = lax.all_to_all(terms.reshape(16, 8 + share, columns), "row", 0, 0, tiled=False)
    terms = terms.sum(axis=0)

    mixed = gather(terms[8:, :RANK], "core")
    gram = gather(terms[:8], "z")
    mixed, gram = lax.optimization_barrier((mixed, gram))
    mixed = gather(mixed, "y").reshape(8 * share, RANK)
    gram = gather(gram.reshape(32, columns), "x").reshape(128, columns)[:own]
    mixed, gathered = lax.optimization_barrier((mixed, gathered))
    mixed = lax.all_gather(mixed, "row", axis=0, tiled=True)
    gram = gather(gather(gram, "y").reshape(columns // 2, columns), "core")

    inverse = inverse_factor(gram.reshape(columns, columns))
    at = lax.axis_index("row").astype(jnp.int32).reshape(1)
    update, new_first, new_second = adam_step(
        at, inverse, sketched, mixed, grad_turned, gathered, first_moment, second_moment
    )
    return update.T, new_first, new_second


def solution(mesh):
    placed = (P(None, "row"), P(None, "col"), P("col", None), P("row", "col"), P("row", "col"))
    return jax.shard_map(
        local,
        mesh=mesh,
        in_specs=placed,
        out_specs=(P("row", "col"), P("row", "col"), P("row", "col")),
        check_vma=False,
    )
```

```python
import jax
import jax.numpy as jnp
from jax import lax
from jax.experimental import pallas as pl
from jax.experimental.pallas import tpu as pltpu
from jax.sharding import PartitionSpec as P

RANK = 512
ADAM_STEP = 10
BLOCK = 128
TILE = 1024
MIX_TILE = 512
STEP_VMEM = 50 << 20
PART, STEP = 24, 16

beta_one = 0.9
beta_two = 0.999
adam_epsilon = 1e-08

f32 = jnp.float32
bf16 = jnp.bfloat16
HIGHEST = lax.Precision.HIGHEST

EXTENT = {"x": 4, "z": 4, "y": 4, "core": 2}
HOME = {"x": ("row", 4), "z": ("row", 1), "y": ("col", 2), "core": ("col", 1)}


def place(sub):
    axis, stride = HOME[sub]
    return lax.axis_index(axis) // stride % EXTENT[sub]


def shift(value, sub, by):
    axis, stride = HOME[sub]
    n = EXTENT[sub]
    pairs = []
    for i in range(16 if axis == "row" else 8):
        at = i // stride % n
        pairs.append((i, i + ((at + by) % n - at) * stride))
    return lax.ppermute(value, axis, pairs)


def scatter_sum(value, sub, wire=f32):
    n, me = EXTENT[sub], place(sub)
    pick = lambda k: lax.dynamic_index_in_dim(value, (me + k) % n, 0, keepdims=False)
    got = [shift(pick(k).astype(wire), sub, k) for k in range(1, n)]
    total = pick(0)
    for term in got:
        total = total + term.astype(value.dtype)
    return total


def gather(value, sub):
    n, me = EXTENT[sub], place(sub)
    got = [value] + [shift(value, sub, k) for k in range(1, n)]
    out = jnp.zeros((n,) + value.shape, value.dtype)
    for k in range(n):
        out = lax.dynamic_update_index_in_dim(out, got[k], (me - k) % n, 0)
    return out


def full_sum(value, sub):
    got = [shift(value, sub, k) for k in range(1, EXTENT[sub])]
    return (value + got[1]) + (got[0] + got[2])


def lane_of(value, k):
    return jnp.take_along_axis(value, jnp.full(value.shape, k, jnp.int32), axis=1)


def row_of(value, k):
    return jnp.broadcast_to(value[k : k + 1], value.shape)


def reciprocal(value):
    guess = pl.reciprocal(value, approx=True)
    guess = guess * (2.0 - value * guess)
    return guess * (2.0 - value * guess)


def invert_block(rows, lane, sub):
    rows, scale = list(rows), []
    for g in range(len(rows)):
        group = (lane >= 8 * g) & (lane < 8 * g + 8)
        column = [lane_of(rows[g], 8 * g + m) for m in range(8)]
        now = jnp.where(group, jnp.where(lane == 8 * g + sub, 1.0, 0.0), rows[g])
        units, inverses, tops, diagonal = [], [], {}, None
        for k in range(8):
            pivot = row_of(column[k], k)
            inverses.append(reciprocal(pivot))
            units.append(row_of(now, k))
            factor = jnp.where(sub > k, column[k] * inverses[k], 0.0)
            for m in range(k + 1, 8):
                tops[k, m] = row_of(column[m], k)
                column[m] = column[m] - factor * tops[k, m]
            now = now - factor * units[k]
            diagonal = pivot if k == 0 else jnp.where(sub == k, pivot, diagonal)
        rows[g] = now
        scale.append(lax.rsqrt(diagonal))
        for h in range(g + 1, len(rows)):
            column = [lane_of(rows[h], 8 * g + m) for m in range(8)]
            now = jnp.where(group, 0.0, rows[h])
            for k in range(8):
                factor = column[k] * inverses[k]
                for m in range(k + 1, 8):
                    column[m] = column[m] - factor * tops[k, m]
                now = now - factor * units[k]
            rows[h] = now
    return [a * b for a, b in zip(rows, scale)]


def factor_kernel(gram_ref, out_ref, work):
    size, padded = gram_ref.shape[0], work.shape[0]
    work[...] = jnp.zeros_like(work)
    work[:size, :size] = gram_ref[...]
    lane = lax.broadcasted_iota(jnp.int32, (8, BLOCK), 1)
    sub = lax.broadcasted_iota(jnp.int32, (8, BLOCK), 0)

    def diagonal_inverse(o, n):
        rows = [work[pl.ds(pl.multiple_of(o + 8 * h, 8), 8), pl.ds(o, BLOCK)] for h in range(n // 8)]
        inverse = jnp.concatenate(invert_block(rows, lane, sub), axis=0)
        row_in = lax.broadcasted_iota(jnp.int32, (n, BLOCK), 0)
        lane_in = lax.broadcasted_iota(jnp.int32, (n, BLOCK), 1)
        return jnp.where(row_in >= lane_in, inverse, 0.0)

    def step(b, carry):
        o = pl.multiple_of(b * BLOCK, BLOCK)
        here = pl.ds(o, BLOCK)
        inverse = diagonal_inverse(o, BLOCK)
        panel = work[here, :]
        work[:, here] = jnp.zeros((padded, BLOCK), f32)
        solved = jnp.dot(inverse, panel, precision=HIGHEST, preferred_element_type=f32)
        work[here, :] = solved
        work[here, here] = inverse
        for later in range(1, padded // BLOCK):
            there = pl.ds(later * BLOCK, BLOCK)

            @pl.when(later > b)
            def _():
                work[there, :] -= lax.dot_general(
                    work[here, there], work[here, :], (((0,), (0,)), ((), ())),
                    precision=HIGHEST, preferred_element_type=f32,
                )

        return carry

    lax.fori_loop(0, size // BLOCK, step, 0)
    o, n = size // BLOCK * BLOCK, size % BLOCK
    if n:
        inverse = diagonal_inverse(o, n)
        work[o:size, :] = jnp.dot(
            inverse[:, :n], work[o:size, :], precision=HIGHEST, preferred_element_type=f32
        )
        work[o:size, o:] = inverse
    row_at = lax.broadcasted_iota(jnp.int32, (padded, padded), 0)
    lane_at = lax.broadcasted_iota(jnp.int32, (padded, padded), 1)
    out_ref[...] = jnp.where(row_at >= lane_at, work[...], 0.0)[:size, :size]


def inverse_factor(gram):
    size = gram.shape[0]
    padded = pl.cdiv(size, BLOCK) * BLOCK
    return pl.pallas_call(
        factor_kernel,
        out_shape=jax.ShapeDtypeStruct((size, size), f32),
        in_specs=[pl.BlockSpec(memory_space=pltpu.VMEM)],
        out_specs=pl.BlockSpec(memory_space=pltpu.VMEM),
        scratch_shapes=[pltpu.VMEM((padded, padded), f32)],
        compiler_params=pltpu.CompilerParams(vmem_limit_bytes=16 << 20),
        cost_estimate=pl.CostEstimate(flops=160 * size**3, bytes_accessed=8 * size**2, transcendentals=0),
        name="inverse_factor",
    )(gram)


def two_parts(value):
    high = value.astype(bf16)
    return high, (value - high.astype(f32)).astype(bf16)


def pack_kernel(first_ref, second_ref, out_ref):
    owned = first_ref.shape[0]
    out_ref[:owned, :] = first_ref[...].astype(out_ref.dtype)
    out_ref[owned:, :] = second_ref[...].astype(out_ref.dtype)


def pack(first, second):
    owned, width = first.shape
    return pl.pallas_call(
        pack_kernel,
        out_shape=jax.ShapeDtypeStruct((2 * owned, width), bf16),
        name="pack",
    )(first, second)


def sketched_term(sketch_turned, grad_turned, layer_input):
    token_sketch = jnp.dot(sketch_turned, grad_turned, preferred_element_type=f32).astype(bf16)
    return jnp.dot(lax.optimization_barrier(token_sketch), layer_input, preferred_element_type=f32)


def moments(first, second, projected):
    new_first = beta_one * first + (1.0 - beta_one) * projected
    new_second = beta_two * second + (1.0 - beta_two) * projected * projected
    return new_first, new_second


def step_kernel(
    at_ref, inverse_ref, sketched_ref, mixed_ref, grad_ref, gathered_ref, own_first_ref, own_second_ref,
    update_ref, new_first_ref, new_second_ref,
    projector, turned, projected, ready, mixed, grad, gathered, arrived, sent,
):
    width, owned = grad_ref.shape[0], own_first_ref.shape[0]
    tiles = [(o, min(TILE, width - o)) for o in range(0, width, TILE)]
    fetch_mixed = pltpu.make_async_copy(mixed_ref, mixed, arrived.at[0])
    fetch_gathered = pltpu.make_async_copy(gathered_ref, gathered, arrived.at[1])
    fetch_grad = [
        pltpu.make_async_copy(grad_ref.at[pl.ds(o, n)], grad.at[pl.ds(o, n)], arrived.at[2 + i])
        for i, (o, n) in enumerate(tiles)
    ]
    fetch_mixed.start()

    high, low = two_parts(inverse_ref[:RANK, :RANK])
    values = sketched_ref[:RANK, :]
    projector[...] = (
        jnp.dot(low, values, preferred_element_type=f32) + jnp.dot(high, values, preferred_element_type=f32)
    ).astype(bf16)
    times = lambda a, b: lax.dot_general(a, b, (((1,), (1,)), ((), ())), preferred_element_type=f32)
    fetch_mixed.wait()
    fetch_grad[0].start()
    fetch_gathered.start()
    for o in range(0, mixed.shape[0], MIX_TILE):
        here = pl.ds(o, MIX_TILE)
        mixed_high, mixed_low = two_parts(mixed[here, :])
        turned[:, here] = (
            times(high, mixed_low) + times(low, mixed_high) + times(high, mixed_high)
        ).astype(bf16)

    mine = pl.ds(pl.multiple_of(at_ref[0] * owned, owned), owned)
    send = [
        pltpu.make_async_copy(ready.at[i % 2, :n], update_ref.at[pl.ds(o, n)], sent.at[i % 2])
        for i, (o, n) in enumerate(tiles)
    ]
    for i, (o, n) in enumerate(tiles):
        here = pl.ds(o, n)
        fetch_grad[i].wait()
        if i + 1 < len(tiles):
            fetch_grad[i + 1].start()
        projected[:, :n] = times(turned[...], grad[here, :])
        if i == 0:
            fetch_gathered.wait()
        first = gathered[:, :owned, here].reshape(RANK, n).astype(f32)
        second = gathered[:, owned:, here].reshape(RANK, n).astype(f32)
        new_first, new_second = moments(first, second, projected[:, :n])
        root = (1.0 - beta_two**ADAM_STEP) ** 0.5
        below = new_second * lax.rsqrt(new_second) + adam_epsilon * root
        scaled = new_first * (root / (1.0 - beta_one**ADAM_STEP))
        normalized = (scaled * pltpu.reciprocal(below)).astype(bf16)
        if i >= 2:
            send[i - 2].wait()
        ready[i % 2, :n] = lax.dot_general(
            normalized, projector[...], (((0,), (0,)), ((), ())), preferred_element_type=f32
        )
        send[i].start()
        new_first_ref[:, here], new_second_ref[:, here] = moments(
            own_first_ref[:, here], own_second_ref[:, here], projected[mine, :n]
        )
    for copy in send[-2:]:
        copy.wait()


def adam_step(at, inverse, sketched, mixed, grad_turned, gathered, own_first, own_second):
    width, tokens = grad_turned.shape
    features = sketched.shape[1]
    owned = own_first.shape[0]
    inside = pl.BlockSpec(memory_space=pltpu.VMEM)
    outside = pl.BlockSpec(memory_space=pl.ANY)
    return pl.pallas_call(
        step_kernel,
        out_shape=(
            jax.ShapeDtypeStruct((width, features), f32),
            jax.ShapeDtypeStruct((owned, width), f32),
            jax.ShapeDtypeStruct((owned, width), f32),
        ),
        in_specs=[pl.BlockSpec(memory_space=pltpu.SMEM), inside, inside]
        + [outside, outside, outside, inside, inside],
        out_specs=(outside, inside, inside),
        scratch_shapes=[
            pltpu.VMEM((RANK, features), bf16),
            pltpu.VMEM((RANK, tokens), bf16),
            pltpu.VMEM((RANK, TILE), f32),
            pltpu.VMEM((2, TILE, features), f32),
            pltpu.VMEM(mixed.shape, f32),
            pltpu.VMEM(grad_turned.shape, bf16),
            pltpu.VMEM(gathered.shape, bf16),
            pltpu.SemaphoreType.DMA((2 + pl.cdiv(width, TILE),)),
            pltpu.SemaphoreType.DMA((2,)),
        ],
        compiler_params=pltpu.CompilerParams(vmem_limit_bytes=STEP_VMEM),
        cost_estimate=pl.CostEstimate(
            flops=2 * RANK * width * (tokens + features) + 6 * RANK * RANK * tokens,
            bytes_accessed=width * (2 * tokens + 4 * RANK + 4 * features + 16 * owned) + 4 * tokens * RANK,
            transcendentals=RANK * width,
        ),
        name="adam_step",
    )(at, inverse, sketched, mixed, grad_turned, gathered, own_first, own_second)


def local(layer_input, output_grad, sketch, first_moment, second_moment):
    tokens, features = layer_input.shape
    columns = sketch.shape[1]
    own = columns // 8
    share = tokens // 128
    grad_turned = output_grad.T
    gathered = lax.all_gather(pack(first_moment, second_moment), "row", axis=0, tiled=False)

    partial = sketched_term(sketch.T, grad_turned, layer_input)
    half = scatter_sum(partial.reshape(2, columns // 2, features), "core", bf16)
    owned_rows = scatter_sum(half.reshape(4, own, features), "y", bf16).astype(bf16)
    sketched = gather(gather(owned_rows, "y").reshape(columns // 2, features), "core")
    sketched = sketched.reshape(columns, features)

    own_tokens = lax.dynamic_index_in_dim(
        layer_input.reshape(16, 8, share, features), lax.axis_index("col"), 1, keepdims=False
    ).reshape(tokens // 8, features)
    times = lambda a, b: lax.dot_general(a, b, (((1,), (1,)), ((), ())), preferred_element_type=f32)
    mixed = times(own_tokens, sketched[:RANK]).reshape(16, share, RANK)
    mixed = lax.all_to_all(mixed, "row", 0, 0, tiled=False).sum(axis=0)

    gram = times(owned_rows, sketched)
    gram = jnp.stack([gram[k * STEP : k * STEP + PART] for k in range(4)])
    mixed, gram = lax.optimization_barrier((mixed, gram))
    mixed, gram = lax.optimization_barrier((gather(mixed, "core"), scatter_sum(gram, "x")))
    mixed, gram = lax.optimization_barrier((gather(mixed, "y"), full_sum(gram, "z")))
    mixed = mixed.reshape(8 * share, RANK)
    mixed, gathered = lax.optimization_barrier((mixed, gathered))
    mixed = lax.all_gather(mixed, "row", axis=0, tiled=True)
    gram = gather(gram, "x")
    gram = jnp.concatenate([gram[0, :STEP], gram[1, :STEP], gram[2, :STEP], gram[3]], axis=0)
    gram = gather(gather(gram, "y").reshape(columns // 2, columns), "core")

    inverse = inverse_factor(gram.reshape(columns, columns))
    at = lax.axis_index("row").astype(jnp.int32).reshape(1)
    update, new_first, new_second = adam_step(
        at, inverse, sketched, mixed, grad_turned, gathered, first_moment, second_moment
    )
    return update.T, new_first, new_second


def solution(mesh):
    placed = (P(None, "row"), P(None, "col"), P("col", None), P("row", "col"), P("row", "col"))
    return jax.shard_map(
        local,
        mesh=mesh,
        in_specs=placed,
        out_specs=(P("row", "col"), P("row", "col"), P("row", "col")),
        check_vma=False,
    )
```

```python
import jax
import jax.numpy as jnp
from jax import lax
from jax.experimental import pallas as pl
from jax.experimental.pallas import tpu as pltpu
from jax.sharding import PartitionSpec as P

RANK = 512
ADAM_STEP = 10
BLOCK = 128
TILE = 1024
MIX_TILE = 512
STEP_VMEM = 50 << 20
PART, STEP = 24, 16

beta_one = 0.9
beta_two = 0.999
adam_epsilon = 1e-08

f32 = jnp.float32
bf16 = jnp.bfloat16
HIGHEST = lax.Precision.HIGHEST

EXTENT = {"x": 4, "z": 4, "y": 4, "core": 2}
HOME = {"x": ("row", 4), "z": ("row", 1), "y": ("col", 2), "core": ("col", 1)}


def place(sub):
    axis, stride = HOME[sub]
    return lax.axis_index(axis) // stride % EXTENT[sub]


def shift(value, sub, by):
    axis, stride = HOME[sub]
    n = EXTENT[sub]
    pairs = []
    for i in range(16 if axis == "row" else 8):
        at = i // stride % n
        pairs.append((i, i + ((at + by) % n - at) * stride))
    return lax.ppermute(value, axis, pairs)


def scatter_sum(value, sub, wire=f32):
    n, me = EXTENT[sub], place(sub)
    pick = lambda k: lax.dynamic_index_in_dim(value, (me + k) % n, 0, keepdims=False)
    got = [shift(pick(k).astype(wire), sub, k) for k in range(1, n)]
    total = pick(0)
    for term in got:
        total = total + term.astype(value.dtype)
    return total


def gather(value, sub):
    n, me = EXTENT[sub], place(sub)
    got = [value] + [shift(value, sub, k) for k in range(1, n)]
    out = jnp.zeros((n,) + value.shape, value.dtype)
    for k in range(n):
        out = lax.dynamic_update_index_in_dim(out, got[k], (me - k) % n, 0)
    return out


def full_sum(value, sub):
    got = [shift(value, sub, k) for k in range(1, EXTENT[sub])]
    return (value + got[1]) + (got[0] + got[2])


def lane_of(value, k):
    return jnp.take_along_axis(value, jnp.full(value.shape, k, jnp.int32), axis=1)


def row_of(value, k):
    return jnp.broadcast_to(value[k : k + 1], value.shape)


def reciprocal(value):
    guess = pl.reciprocal(value, approx=True)
    return guess * (2.0 - value * guess)


def invert_block(rows, lane, sub):
    rows, scale = list(rows), []
    for g in range(len(rows)):
        group = (lane >= 8 * g) & (lane < 8 * g + 8)
        column = [lane_of(rows[g], 8 * g + m) for m in range(8)]
        now = jnp.where(group, jnp.where(lane == 8 * g + sub, 1.0, 0.0), rows[g])
        units, inverses, tops, diagonal = [], [], {}, None
        for k in range(8):
            pivot = row_of(column[k], k)
            inverses.append(reciprocal(pivot))
            units.append(row_of(now, k))
            factor = jnp.where(sub > k, column[k] * inverses[k], 0.0)
            for m in range(k + 1, 8):
                tops[k, m] = row_of(column[m], k)
                column[m] = column[m] - factor * tops[k, m]
            now = now - factor * units[k]
            diagonal = pivot if k == 0 else jnp.where(sub == k, pivot, diagonal)
        rows[g] = now
        scale.append(lax.rsqrt(diagonal))
        for h in range(g + 1, len(rows)):
            column = [lane_of(rows[h], 8 * g + m) for m in range(8)]
            now = jnp.where(group, 0.0, rows[h])
            for k in range(8):
                factor = column[k] * inverses[k]
                for m in range(k + 1, 8):
                    column[m] = column[m] - factor * tops[k, m]
                now = now - factor * units[k]
            rows[h] = now
    return [a * b for a, b in zip(rows, scale)]


def factor_kernel(gram_ref, out_ref, work):
    size, padded = gram_ref.shape[0], work.shape[0]
    work[...] = jnp.zeros_like(work)
    work[:size, :size] = gram_ref[...]
    lane = lax.broadcasted_iota(jnp.int32, (8, BLOCK), 1)
    sub = lax.broadcasted_iota(jnp.int32, (8, BLOCK), 0)

    def diagonal_inverse(o, n):
        rows = [work[pl.ds(pl.multiple_of(o + 8 * h, 8), 8), pl.ds(o, BLOCK)] for h in range(n // 8)]
        inverse = jnp.concatenate(invert_block(rows, lane, sub), axis=0)
        row_in = lax.broadcasted_iota(jnp.int32, (n, BLOCK), 0)
        lane_in = lax.broadcasted_iota(jnp.int32, (n, BLOCK), 1)
        return jnp.where(row_in >= lane_in, inverse, 0.0)

    def step(b, carry):
        o = pl.multiple_of(b * BLOCK, BLOCK)
        here = pl.ds(o, BLOCK)
        inverse = diagonal_inverse(o, BLOCK)
        panel = work[here, :]
        work[:, here] = jnp.zeros((padded, BLOCK), f32)
        solved = jnp.dot(inverse, panel, precision=HIGHEST, preferred_element_type=f32)
        work[here, :] = solved
        work[here, here] = inverse
        for later in range(1, padded // BLOCK):
            there = pl.ds(later * BLOCK, BLOCK)

            @pl.when(later > b)
            def _():
                work[there, :] -= lax.dot_general(
                    work[here, there], work[here, :], (((0,), (0,)), ((), ())),
                    precision=HIGHEST, preferred_element_type=f32,
                )

        return carry

    lax.fori_loop(0, size // BLOCK, step, 0)
    o, n = size // BLOCK * BLOCK, size % BLOCK
    if n:
        inverse = diagonal_inverse(o, n)
        work[o:size, :] = jnp.dot(
            inverse[:, :n], work[o:size, :], precision=HIGHEST, preferred_element_type=f32
        )
        work[o:size, o:] = inverse
    row_at = lax.broadcasted_iota(jnp.int32, (padded, padded), 0)
    lane_at = lax.broadcasted_iota(jnp.int32, (padded, padded), 1)
    out_ref[...] = jnp.where(row_at >= lane_at, work[...], 0.0)[:size, :size]


def inverse_factor(gram):
    size = gram.shape[0]
    padded = pl.cdiv(size, BLOCK) * BLOCK
    return pl.pallas_call(
        factor_kernel,
        out_shape=jax.ShapeDtypeStruct((size, size), f32),
        in_specs=[pl.BlockSpec(memory_space=pltpu.VMEM)],
        out_specs=pl.BlockSpec(memory_space=pltpu.VMEM),
        scratch_shapes=[pltpu.VMEM((padded, padded), f32)],
        compiler_params=pltpu.CompilerParams(vmem_limit_bytes=16 << 20),
        cost_estimate=pl.CostEstimate(flops=160 * size**3, bytes_accessed=8 * size**2, transcendentals=0),
        name="inverse_factor",
    )(gram)


def two_parts(value):
    high = value.astype(bf16)
    return high, (value - high.astype(f32)).astype(bf16)


def pack_kernel(first_ref, second_ref, out_ref):
    owned = first_ref.shape[0]
    out_ref[:owned, :] = first_ref[...].astype(out_ref.dtype)
    out_ref[owned:, :] = second_ref[...].astype(out_ref.dtype)


def pack(first, second):
    owned, width = first.shape
    return pl.pallas_call(
        pack_kernel,
        out_shape=jax.ShapeDtypeStruct((2 * owned, width), bf16),
        name="pack",
    )(first, second)


def sketched_term(sketch_turned, grad_turned, layer_input):
    token_sketch = jnp.dot(sketch_turned, grad_turned, preferred_element_type=f32)
    rounded = lax.reduce_precision(token_sketch, 8, 7)
    high, low = rounded.astype(bf16), (token_sketch - rounded).astype(bf16)
    times = lambda part: jnp.dot(part, layer_input, preferred_element_type=f32)
    return times(high) + times(low)


def moments(first, second, projected):
    new_first = beta_one * first + (1.0 - beta_one) * projected
    new_second = beta_two * second + (1.0 - beta_two) * projected * projected
    return new_first, new_second


def step_kernel(
    at_ref, inverse_ref, sketched_ref, mixed_ref, grad_ref, gathered_ref, own_first_ref, own_second_ref,
    update_ref, new_first_ref, new_second_ref,
    projector, turned, projected, ready, mixed, grad, gathered, arrived, sent,
):
    width, owned = grad_ref.shape[0], own_first_ref.shape[0]
    tiles = [(o, min(TILE, width - o)) for o in range(0, width, TILE)]
    fetch_mixed = pltpu.make_async_copy(mixed_ref, mixed, arrived.at[0])
    fetch_gathered = pltpu.make_async_copy(gathered_ref, gathered, arrived.at[1])
    fetch_grad = [
        pltpu.make_async_copy(grad_ref.at[pl.ds(o, n)], grad.at[pl.ds(o, n)], arrived.at[2 + i])
        for i, (o, n) in enumerate(tiles)
    ]
    fetch_mixed.start()

    high, low = two_parts(inverse_ref[:RANK, :RANK])
    values = sketched_ref[:RANK, :]
    projector[...] = (
        jnp.dot(low, values, preferred_element_type=f32) + jnp.dot(high, values, preferred_element_type=f32)
    ).astype(bf16)
    times = lambda a, b: lax.dot_general(a, b, (((1,), (1,)), ((), ())), preferred_element_type=f32)
    fetch_mixed.wait()
    fetch_grad[0].start()
    fetch_gathered.start()
    for o in range(0, mixed.shape[0], MIX_TILE):
        here = pl.ds(o, MIX_TILE)
        mixed_high, mixed_low = two_parts(mixed[here, :])
        turned[:, here] = (
            times(high, mixed_low) + times(low, mixed_high) + times(high, mixed_high)
        ).astype(bf16)

    mine = pl.ds(pl.multiple_of(at_ref[0] * owned, owned), owned)
    send = [
        pltpu.make_async_copy(ready.at[i % 2, :n], update_ref.at[pl.ds(o, n)], sent.at[i % 2])
        for i, (o, n) in enumerate(tiles)
    ]
    for i, (o, n) in enumerate(tiles):
        here = pl.ds(o, n)
        fetch_grad[i].wait()
        if i + 1 < len(tiles):
            fetch_grad[i + 1].start()
        projected[:, :n] = times(turned[...], grad[here, :])
        if i == 0:
            fetch_gathered.wait()
        first = gathered[:, :owned, here].reshape(RANK, n).astype(f32)
        second = gathered[:, owned:, here].reshape(RANK, n).astype(f32)
        new_first, new_second = moments(first, second, projected[:, :n])
        root = (1.0 - beta_two**ADAM_STEP) ** 0.5
        below = new_second * lax.rsqrt(new_second) + adam_epsilon * root
        scaled = new_first * (root / (1.0 - beta_one**ADAM_STEP))
        normalized = (scaled * pltpu.reciprocal(below)).astype(bf16)
        if i >= 2:
            send[i - 2].wait()
        ready[i % 2, :n] = lax.dot_general(
            normalized, projector[...], (((0,), (0,)), ((), ())), preferred_element_type=f32
        )
        send[i].start()
        new_first_ref[:, here], new_second_ref[:, here] = moments(
            own_first_ref[:, here], own_second_ref[:, here], projected[mine, :n]
        )
    for copy in send[-2:]:
        copy.wait()


def adam_step(at, inverse, sketched, mixed, grad_turned, gathered, own_first, own_second):
    width, tokens = grad_turned.shape
    features = sketched.shape[1]
    owned = own_first.shape[0]
    inside = pl.BlockSpec(memory_space=pltpu.VMEM)
    outside = pl.BlockSpec(memory_space=pl.ANY)
    return pl.pallas_call(
        step_kernel,
        out_shape=(
            jax.ShapeDtypeStruct((width, features), f32),
            jax.ShapeDtypeStruct((owned, width), f32),
            jax.ShapeDtypeStruct((owned, width), f32),
        ),
        in_specs=[pl.BlockSpec(memory_space=pltpu.SMEM), inside, inside]
        + [outside, outside, outside, inside, inside],
        out_specs=(outside, inside, inside),
        scratch_shapes=[
            pltpu.VMEM((RANK, features), bf16),
            pltpu.VMEM((RANK, tokens), bf16),
            pltpu.VMEM((RANK, TILE), f32),
            pltpu.VMEM((2, TILE, features), f32),
            pltpu.VMEM(mixed.shape, f32),
            pltpu.VMEM(grad_turned.shape, bf16),
            pltpu.VMEM(gathered.shape, bf16),
            pltpu.SemaphoreType.DMA((2 + pl.cdiv(width, TILE),)),
            pltpu.SemaphoreType.DMA((2,)),
        ],
        compiler_params=pltpu.CompilerParams(vmem_limit_bytes=STEP_VMEM),
        cost_estimate=pl.CostEstimate(
            flops=2 * RANK * width * (tokens + features) + 6 * RANK * RANK * tokens,
            bytes_accessed=width * (2 * tokens + 4 * RANK + 4 * features + 16 * owned) + 4 * tokens * RANK,
            transcendentals=RANK * width,
        ),
        name="adam_step",
    )(at, inverse, sketched, mixed, grad_turned, gathered, own_first, own_second)


def local(layer_input, output_grad, sketch, first_moment, second_moment):
    tokens, features = layer_input.shape
    columns = sketch.shape[1]
    own = columns // 8
    share = tokens // 128
    grad_turned = output_grad.T
    gathered = lax.all_gather(pack(first_moment, second_moment), "row", axis=0, tiled=False)

    partial = sketched_term(sketch.T, grad_turned, layer_input)
    half = scatter_sum(partial.reshape(2, columns // 2, features), "core", bf16)
    owned_rows = scatter_sum(half.reshape(4, own, features), "y", bf16).astype(bf16)
    sketched = gather(gather(owned_rows, "y").reshape(columns // 2, features), "core")
    sketched = sketched.reshape(columns, features)

    own_tokens = lax.dynamic_index_in_dim(
        layer_input.reshape(16, 8, share, features), lax.axis_index("col"), 1, keepdims=False
    ).reshape(tokens // 8, features)
    times = lambda a, b: lax.dot_general(a, b, (((1,), (1,)), ((), ())), preferred_element_type=f32)
    mixed = scatter_sum(times(own_tokens, sketched[:RANK]).reshape(4, 4 * share, RANK), "x")
    gram = times(owned_rows, sketched)
    gram = jnp.stack([gram[k * STEP : k * STEP + PART] for k in range(4)])
    mixed, gram = lax.optimization_barrier((mixed, gram))
    mixed, gram = lax.optimization_barrier(
        (scatter_sum(mixed.reshape(4, share, RANK), "z"), scatter_sum(gram, "x"))
    )
    mixed, gram = lax.optimization_barrier((gather(gather(mixed, "core"), "y"), full_sum(gram, "z")))
    mixed, gathered = lax.optimization_barrier((mixed.reshape(8 * share, RANK), gathered))
    mixed = lax.all_gather(mixed, "row", axis=0, tiled=True)
    gram = gather(gram, "x")
    gram = jnp.concatenate([gram[0, :STEP], gram[1, :STEP], gram[2, :STEP], gram[3]], axis=0)
    gram = gather(gather(gram, "y").reshape(columns // 2, columns), "core")

    inverse = inverse_factor(gram.reshape(columns, columns))
    at = lax.axis_index("row").astype(jnp.int32).reshape(1)
    update, new_first, new_second = adam_step(
        at, inverse, sketched, mixed, grad_turned, gathered, first_moment, second_moment
    )
    return update.T, new_first, new_second


def solution(mesh):
    placed = (P(None, "row"), P(None, "col"), P("col", None), P("row", "col"), P("row", "col"))
    return jax.shard_map(
        local,
        mesh=mesh,
        in_specs=placed,
        out_specs=(P("row", "col"), P("row", "col"), P("row", "col")),
        check_vma=False,
    )
```

```python
import jax
import jax.numpy as jnp
from jax import lax
from jax.experimental import pallas as pl
from jax.experimental.pallas import tpu as pltpu
from jax.sharding import PartitionSpec as P

RANK = 512
ADAM_STEP = 10
BLOCK = 128
TILE = 1024
MIX_TILE = 512
STEP_VMEM = 50 << 20
PART, STEP = 24, 16

beta_one = 0.9
beta_two = 0.999
adam_epsilon = 1e-08

f32 = jnp.float32
bf16 = jnp.bfloat16
HIGHEST = lax.Precision.HIGHEST

EXTENT = {"x": 4, "z": 4, "y": 4, "core": 2}
HOME = {"x": ("row", 4), "z": ("row", 1), "y": ("col", 2), "core": ("col", 1)}


def place(sub):
    axis, stride = HOME[sub]
    return lax.axis_index(axis) // stride % EXTENT[sub]


def shift(value, sub, by):
    axis, stride = HOME[sub]
    n = EXTENT[sub]
    pairs = []
    for i in range(16 if axis == "row" else 8):
        at = i // stride % n
        pairs.append((i, i + ((at + by) % n - at) * stride))
    return lax.ppermute(value, axis, pairs)


def scatter_sum(value, sub, wire=f32):
    n, me = EXTENT[sub], place(sub)
    pick = lambda k: lax.dynamic_index_in_dim(value, (me + k) % n, 0, keepdims=False)
    got = [shift(pick(k).astype(wire), sub, k) for k in range(1, n)]
    total = pick(0)
    for term in got:
        total = total + term.astype(value.dtype)
    return total


def gather(value, sub):
    n, me = EXTENT[sub], place(sub)
    got = [value] + [shift(value, sub, k) for k in range(1, n)]
    out = jnp.zeros((n,) + value.shape, value.dtype)
    for k in range(n):
        out = lax.dynamic_update_index_in_dim(out, got[k], (me - k) % n, 0)
    return out


def full_sum(value, sub):
    got = [shift(value, sub, k) for k in range(1, EXTENT[sub])]
    return (value + got[1]) + (got[0] + got[2])


def lane_of(value, k):
    return jnp.take_along_axis(value, jnp.full(value.shape, k, jnp.int32), axis=1)


def row_of(value, k):
    return jnp.broadcast_to(value[k : k + 1], value.shape)


def reciprocal(value):
    guess = pl.reciprocal(value, approx=True)
    return guess * (2.0 - value * guess)


def invert_block(rows, lane, sub):
    rows, scale = list(rows), []
    for g in range(len(rows)):
        group = (lane >= 8 * g) & (lane < 8 * g + 8)
        column = [lane_of(rows[g], 8 * g + m) for m in range(8)]
        now = jnp.where(group, jnp.where(lane == 8 * g + sub, 1.0, 0.0), rows[g])
        units, inverses, tops, diagonal = [], [], {}, None
        for k in range(8):
            pivot = row_of(column[k], k)
            inverses.append(reciprocal(pivot))
            units.append(row_of(now, k))
            factor = jnp.where(sub > k, column[k] * inverses[k], 0.0)
            for m in range(k + 1, 8):
                tops[k, m] = row_of(column[m], k)
                column[m] = column[m] - factor * tops[k, m]
            now = now - factor * units[k]
            diagonal = pivot if k == 0 else jnp.where(sub == k, pivot, diagonal)
        rows[g] = now
        scale.append(lax.rsqrt(diagonal))
        for h in range(g + 1, len(rows)):
            column = [lane_of(rows[h], 8 * g + m) for m in range(8)]
            now = jnp.where(group, 0.0, rows[h])
            for k in range(8):
                factor = column[k] * inverses[k]
                for m in range(k + 1, 8):
                    column[m] = column[m] - factor * tops[k, m]
                now = now - factor * units[k]
            rows[h] = now
    return [a * b for a, b in zip(rows, scale)]


def factor_kernel(gram_ref, out_ref, work):
    size, padded = gram_ref.shape[0], work.shape[0]
    work[...] = jnp.zeros_like(work)
    work[:size, :size] = gram_ref[...]
    lane = lax.broadcasted_iota(jnp.int32, (8, BLOCK), 1)
    sub = lax.broadcasted_iota(jnp.int32, (8, BLOCK), 0)

    def diagonal_inverse(o, n):
        rows = [work[pl.ds(pl.multiple_of(o + 8 * h, 8), 8), pl.ds(o, BLOCK)] for h in range(n // 8)]
        inverse = jnp.concatenate(invert_block(rows, lane, sub), axis=0)
        row_in = lax.broadcasted_iota(jnp.int32, (n, BLOCK), 0)
        lane_in = lax.broadcasted_iota(jnp.int32, (n, BLOCK), 1)
        return jnp.where(row_in >= lane_in, inverse, 0.0)

    def step(b, carry):
        o = pl.multiple_of(b * BLOCK, BLOCK)
        here = pl.ds(o, BLOCK)
        inverse = diagonal_inverse(o, BLOCK)
        panel = work[here, :]
        work[:, here] = jnp.zeros((padded, BLOCK), f32)
        solved = jnp.dot(inverse, panel, precision=HIGHEST, preferred_element_type=f32)
        work[here, :] = solved
        work[here, here] = inverse
        for later in range(1, padded // BLOCK):
            there = pl.ds(later * BLOCK, BLOCK)

            @pl.when(later > b)
            def _():
                work[there, :] -= lax.dot_general(
                    work[here, there], work[here, :], (((0,), (0,)), ((), ())),
                    precision=HIGHEST, preferred_element_type=f32,
                )

        return carry

    lax.fori_loop(0, size // BLOCK, step, 0)
    o, n = size // BLOCK * BLOCK, size % BLOCK
    if n:
        inverse = diagonal_inverse(o, n)
        work[o:size, :] = jnp.dot(
            inverse[:, :n], work[o:size, :], precision=HIGHEST, preferred_element_type=f32
        )
        work[o:size, o:] = inverse
    row_at = lax.broadcasted_iota(jnp.int32, (padded, padded), 0)
    lane_at = lax.broadcasted_iota(jnp.int32, (padded, padded), 1)
    out_ref[...] = jnp.where(row_at >= lane_at, work[...], 0.0)[:size, :size]


def inverse_factor(gram):
    size = gram.shape[0]
    padded = pl.cdiv(size, BLOCK) * BLOCK
    return pl.pallas_call(
        factor_kernel,
        out_shape=jax.ShapeDtypeStruct((size, size), f32),
        in_specs=[pl.BlockSpec(memory_space=pltpu.VMEM)],
        out_specs=pl.BlockSpec(memory_space=pltpu.VMEM),
        scratch_shapes=[pltpu.VMEM((padded, padded), f32)],
        compiler_params=pltpu.CompilerParams(vmem_limit_bytes=16 << 20),
        cost_estimate=pl.CostEstimate(flops=160 * size**3, bytes_accessed=8 * size**2, transcendentals=0),
        name="inverse_factor",
    )(gram)


def two_parts(value):
    high = value.astype(bf16)
    return high, (value - high.astype(f32)).astype(bf16)


def pack_kernel(first_ref, second_ref, out_ref):
    owned = first_ref.shape[0]
    out_ref[:owned, :] = first_ref[...].astype(out_ref.dtype)
    out_ref[owned:, :] = second_ref[...].astype(out_ref.dtype)


def pack(first, second):
    owned, width = first.shape
    return pl.pallas_call(
        pack_kernel,
        out_shape=jax.ShapeDtypeStruct((2 * owned, width), bf16),
        name="pack",
    )(first, second)


def sketched_term(sketch_turned, grad_turned, layer_input):
    token_sketch = jnp.dot(sketch_turned, grad_turned, preferred_element_type=f32)
    rounded = lax.reduce_precision(token_sketch, 8, 7)
    high, low = rounded.astype(bf16), (token_sketch - rounded).astype(bf16)
    times = lambda part: jnp.dot(part, layer_input, preferred_element_type=f32)
    return times(high) + times(low)


def moments(first, second, projected):
    new_first = beta_one * first + (1.0 - beta_one) * projected
    new_second = beta_two * second + (1.0 - beta_two) * projected * projected
    return new_first, new_second


def step_kernel(
    at_ref, inverse_ref, sketched_ref, mixed_ref, grad_ref, gathered_ref, own_first_ref, own_second_ref,
    update_ref, new_first_ref, new_second_ref,
    projector, turned, projected, ready, mixed, grad, gathered, arrived, sent,
):
    width, owned = grad_ref.shape[0], own_first_ref.shape[0]
    tiles = [(o, min(TILE, width - o)) for o in range(0, width, TILE)]
    fetch_mixed = pltpu.make_async_copy(mixed_ref, mixed, arrived.at[0])
    fetch_gathered = pltpu.make_async_copy(gathered_ref, gathered, arrived.at[1])
    fetch_grad = [
        pltpu.make_async_copy(grad_ref.at[pl.ds(o, n)], grad.at[pl.ds(o, n)], arrived.at[2 + i])
        for i, (o, n) in enumerate(tiles)
    ]
    fetch_mixed.start()

    high, low = two_parts(inverse_ref[:RANK, :RANK])
    values = sketched_ref[:RANK, :]
    projector[...] = (
        jnp.dot(low, values, preferred_element_type=f32) + jnp.dot(high, values, preferred_element_type=f32)
    ).astype(bf16)
    times = lambda a, b: lax.dot_general(a, b, (((1,), (1,)), ((), ())), preferred_element_type=f32)
    fetch_mixed.wait()
    fetch_grad[0].start()
    fetch_gathered.start()
    for o in range(0, mixed.shape[0], MIX_TILE):
        here = pl.ds(o, MIX_TILE)
        mixed_high, mixed_low = two_parts(mixed[here, :])
        turned[:, here] = (
            times(high, mixed_low) + times(low, mixed_high) + times(high, mixed_high)
        ).astype(bf16)

    mine = pl.ds(pl.multiple_of(at_ref[0] * owned, owned), owned)
    send = [
        pltpu.make_async_copy(ready.at[i % 2, :n], update_ref.at[pl.ds(o, n)], sent.at[i % 2])
        for i, (o, n) in enumerate(tiles)
    ]
    for i, (o, n) in enumerate(tiles):
        here = pl.ds(o, n)
        fetch_grad[i].wait()
        if i + 1 < len(tiles):
            fetch_grad[i + 1].start()
        projected[:, :n] = times(turned[...], grad[here, :])
        if i == 0:
            fetch_gathered.wait()
        first = gathered[:, :owned, here].reshape(RANK, n).astype(f32)
        second = gathered[:, owned:, here].reshape(RANK, n).astype(f32)
        new_first, new_second = moments(first, second, projected[:, :n])
        root = (1.0 - beta_two**ADAM_STEP) ** 0.5
        below = new_second * lax.rsqrt(new_second) + adam_epsilon * root
        scaled = new_first * (root / (1.0 - beta_one**ADAM_STEP))
        normalized = (scaled * pltpu.reciprocal(below)).astype(bf16)
        if i >= 2:
            send[i - 2].wait()
        ready[i % 2, :n] = lax.dot_general(
            normalized, projector[...], (((0,), (0,)), ((), ())), preferred_element_type=f32
        )
        send[i].start()
        new_first_ref[:, here], new_second_ref[:, here] = moments(
            own_first_ref[:, here], own_second_ref[:, here], projected[mine, :n]
        )
    for copy in send[-2:]:
        copy.wait()


def adam_step(at, inverse, sketched, mixed, grad_turned, gathered, own_first, own_second):
    width, tokens = grad_turned.shape
    features = sketched.shape[1]
    owned = own_first.shape[0]
    inside = pl.BlockSpec(memory_space=pltpu.VMEM)
    outside = pl.BlockSpec(memory_space=pl.ANY)
    return pl.pallas_call(
        step_kernel,
        out_shape=(
            jax.ShapeDtypeStruct((width, features), f32),
            jax.ShapeDtypeStruct((owned, width), f32),
            jax.ShapeDtypeStruct((owned, width), f32),
        ),
        in_specs=[pl.BlockSpec(memory_space=pltpu.SMEM), inside, inside]
        + [outside, outside, outside, inside, inside],
        out_specs=(outside, inside, inside),
        scratch_shapes=[
            pltpu.VMEM((RANK, features), bf16),
            pltpu.VMEM((RANK, tokens), bf16),
            pltpu.VMEM((RANK, TILE), f32),
            pltpu.VMEM((2, TILE, features), f32),
            pltpu.VMEM(mixed.shape, f32),
            pltpu.VMEM(grad_turned.shape, bf16),
            pltpu.VMEM(gathered.shape, bf16),
            pltpu.SemaphoreType.DMA((2 + pl.cdiv(width, TILE),)),
            pltpu.SemaphoreType.DMA((2,)),
        ],
        compiler_params=pltpu.CompilerParams(vmem_limit_bytes=STEP_VMEM),
        cost_estimate=pl.CostEstimate(
            flops=2 * RANK * width * (tokens + features) + 6 * RANK * RANK * tokens,
            bytes_accessed=width * (2 * tokens + 4 * RANK + 4 * features + 16 * owned) + 4 * tokens * RANK,
            transcendentals=RANK * width,
        ),
        name="adam_step",
    )(at, inverse, sketched, mixed, grad_turned, gathered, own_first, own_second)


def local(layer_input, output_grad, sketch, first_moment, second_moment):
    tokens, features = layer_input.shape
    columns = sketch.shape[1]
    own = columns // 8
    share = tokens // 128
    grad_turned = output_grad.T
    gathered = lax.all_gather(pack(first_moment, second_moment), "row", axis=0, tiled=False)

    partial = sketched_term(sketch.T, grad_turned, layer_input)
    own_tokens = lax.dynamic_index_in_dim(
        layer_input.reshape(16, 8, share, features), lax.axis_index("col"), 1, keepdims=False
    ).reshape(tokens // 8, features)
    half = scatter_sum(partial.reshape(2, columns // 2, features), "core", bf16)
    half, own_tokens = lax.optimization_barrier((half, own_tokens))
    owned_rows = scatter_sum(half.reshape(4, own, features), "y", bf16).astype(bf16)
    sketched = gather(gather(owned_rows, "y").reshape(columns // 2, features), "core")
    sketched = sketched.reshape(columns, features)

    times = lambda a, b: lax.dot_general(a, b, (((1,), (1,)), ((), ())), preferred_element_type=f32)
    mixed = scatter_sum(times(own_tokens, sketched[:RANK]).reshape(4, 4 * share, RANK), "x")
    gram = times(owned_rows, sketched)
    gram = jnp.stack([gram[k * STEP : k * STEP + PART] for k in range(4)])
    mixed, gram = lax.optimization_barrier((mixed, gram))
    mixed, gram = lax.optimization_barrier(
        (scatter_sum(mixed.reshape(4, share, RANK), "z"), scatter_sum(gram, "x"))
    )
    mixed, gram = lax.optimization_barrier((gather(mixed, "core"), gram))
    mixed, gram = lax.optimization_barrier((gather(mixed, "y"), full_sum(gram, "z")))
    mixed, gathered = lax.optimization_barrier((mixed.reshape(8 * share, RANK), gathered))
    mixed = lax.all_gather(mixed, "row", axis=0, tiled=True)
    gram = gather(gram, "x")
    gram = jnp.concatenate([gram[0, :STEP], gram[1, :STEP], gram[2, :STEP], gram[3]], axis=0)
    gram = gather(gather(gram, "y").reshape(columns // 2, columns), "core")

    inverse = inverse_factor(gram.reshape(columns, columns))
    at = lax.axis_index("row").astype(jnp.int32).reshape(1)
    update, new_first, new_second = adam_step(
        at, inverse, sketched, mixed, grad_turned, gathered, first_moment, second_moment
    )
    return update.T, new_first, new_second


def solution(mesh):
    placed = (P(None, "row"), P(None, "col"), P("col", None), P("row", "col"), P("row", "col"))
    return jax.shard_map(
        local,
        mesh=mesh,
        in_specs=placed,
        out_specs=(P("row", "col"), P("row", "col"), P("row", "col")),
        check_vma=False,
    )
```

```python
import jax
import jax.numpy as jnp
from jax import lax
from jax.experimental import pallas as pl
from jax.experimental.pallas import tpu as pltpu
from jax.sharding import PartitionSpec as P

RANK = 512
ADAM_STEP = 10
BLOCK = 128
TILE = 1024
MIX_TILE = 512
STEP_VMEM = 50 << 20
PART, STEP = 24, 16

beta_one = 0.9
beta_two = 0.999
adam_epsilon = 1e-08

f32 = jnp.float32
bf16 = jnp.bfloat16
HIGHEST = lax.Precision.HIGHEST

EXTENT = {"x": 4, "z": 4, "y": 4, "core": 2}
HOME = {"x": ("row", 4), "z": ("row", 1), "y": ("col", 2), "core": ("col", 1)}


def place(sub):
    axis, stride = HOME[sub]
    return lax.axis_index(axis) // stride % EXTENT[sub]


def shift(value, sub, by):
    axis, stride = HOME[sub]
    n = EXTENT[sub]
    pairs = []
    for i in range(16 if axis == "row" else 8):
        at = i // stride % n
        pairs.append((i, i + ((at + by) % n - at) * stride))
    return lax.ppermute(value, axis, pairs)


def scatter_sum(value, sub, wire=f32):
    n, me = EXTENT[sub], place(sub)
    pick = lambda k: lax.dynamic_index_in_dim(value, (me + k) % n, 0, keepdims=False)
    got = [shift(pick(k).astype(wire), sub, k) for k in range(1, n)]
    total = pick(0)
    for term in got:
        total = total + term.astype(value.dtype)
    return total


def gather(value, sub):
    n, me = EXTENT[sub], place(sub)
    got = [value] + [shift(value, sub, k) for k in range(1, n)]
    out = jnp.zeros((n,) + value.shape, value.dtype)
    for k in range(n):
        out = lax.dynamic_update_index_in_dim(out, got[k], (me - k) % n, 0)
    return out


def full_sum(value, sub):
    got = [shift(value, sub, k) for k in range(1, EXTENT[sub])]
    return (value + got[1]) + (got[0] + got[2])


def lane_of(value, k):
    return jnp.take_along_axis(value, jnp.full(value.shape, k, jnp.int32), axis=1)


def row_of(value, k):
    return jnp.broadcast_to(value[k : k + 1], value.shape)


def reciprocal(value):
    guess = pl.reciprocal(value, approx=True)
    return guess * (2.0 - value * guess)


def invert_block(rows, lane, sub):
    rows, scale = list(rows), []
    for g in range(len(rows)):
        group = (lane >= 8 * g) & (lane < 8 * g + 8)
        column = [lane_of(rows[g], 8 * g + m) for m in range(8)]
        now = jnp.where(group, jnp.where(lane == 8 * g + sub, 1.0, 0.0), rows[g])
        units, inverses, tops, diagonal = [], [], {}, None
        for k in range(8):
            pivot = row_of(column[k], k)
            inverses.append(reciprocal(pivot))
            units.append(row_of(now, k))
            factor = jnp.where(sub > k, column[k] * inverses[k], 0.0)
            for m in range(k + 1, 8):
                tops[k, m] = row_of(column[m], k)
                column[m] = column[m] - factor * tops[k, m]
            now = now - factor * units[k]
            diagonal = pivot if k == 0 else jnp.where(sub == k, pivot, diagonal)
        rows[g] = now
        scale.append(lax.rsqrt(diagonal))
        for h in range(g + 1, len(rows)):
            column = [lane_of(rows[h], 8 * g + m) for m in range(8)]
            now = jnp.where(group, 0.0, rows[h])
            for k in range(8):
                factor = column[k] * inverses[k]
                for m in range(k + 1, 8):
                    column[m] = column[m] - factor * tops[k, m]
                now = now - factor * units[k]
            rows[h] = now
    return [a * b for a, b in zip(rows, scale)]


def factor_kernel(gram_ref, out_ref, work):
    size, padded = gram_ref.shape[0], work.shape[0]
    work[...] = jnp.zeros_like(work)
    work[:size, :size] = gram_ref[...]
    lane = lax.broadcasted_iota(jnp.int32, (8, BLOCK), 1)
    sub = lax.broadcasted_iota(jnp.int32, (8, BLOCK), 0)

    def diagonal_inverse(o, n):
        rows = [work[pl.ds(pl.multiple_of(o + 8 * h, 8), 8), pl.ds(o, BLOCK)] for h in range(n // 8)]
        inverse = jnp.concatenate(invert_block(rows, lane, sub), axis=0)
        row_in = lax.broadcasted_iota(jnp.int32, (n, BLOCK), 0)
        lane_in = lax.broadcasted_iota(jnp.int32, (n, BLOCK), 1)
        return jnp.where(row_in >= lane_in, inverse, 0.0)

    def step(b, carry):
        o = pl.multiple_of(b * BLOCK, BLOCK)
        here = pl.ds(o, BLOCK)
        inverse = diagonal_inverse(o, BLOCK)
        panel = work[here, :]
        work[:, here] = jnp.zeros((padded, BLOCK), f32)
        solved = jnp.dot(inverse, panel, precision=HIGHEST, preferred_element_type=f32)
        work[here, :] = solved
        work[here, here] = inverse
        for later in range(1, padded // BLOCK):
            there = pl.ds(later * BLOCK, BLOCK)

            @pl.when(later > b)
            def _():
                work[there, :] -= lax.dot_general(
                    work[here, there], work[here, :], (((0,), (0,)), ((), ())),
                    precision=HIGHEST, preferred_element_type=f32,
                )

        return carry

    lax.fori_loop(0, size // BLOCK, step, 0)
    o, n = size // BLOCK * BLOCK, size % BLOCK
    if n:
        inverse = diagonal_inverse(o, n)
        work[o:size, :] = jnp.dot(
            inverse[:, :n], work[o:size, :], precision=HIGHEST, preferred_element_type=f32
        )
        work[o:size, o:] = inverse
    row_at = lax.broadcasted_iota(jnp.int32, (padded, padded), 0)
    lane_at = lax.broadcasted_iota(jnp.int32, (padded, padded), 1)
    out_ref[...] = jnp.where(row_at >= lane_at, work[...], 0.0)[:size, :size]


def inverse_factor(gram):
    size = gram.shape[0]
    padded = pl.cdiv(size, BLOCK) * BLOCK
    return pl.pallas_call(
        factor_kernel,
        out_shape=jax.ShapeDtypeStruct((size, size), f32),
        in_specs=[pl.BlockSpec(memory_space=pltpu.VMEM)],
        out_specs=pl.BlockSpec(memory_space=pltpu.VMEM),
        scratch_shapes=[pltpu.VMEM((padded, padded), f32)],
        compiler_params=pltpu.CompilerParams(vmem_limit_bytes=16 << 20),
        cost_estimate=pl.CostEstimate(flops=160 * size**3, bytes_accessed=8 * size**2, transcendentals=0),
        name="inverse_factor",
    )(gram)


def two_parts(value):
    high = value.astype(bf16)
    return high, (value - high.astype(f32)).astype(bf16)


def pack_kernel(first_ref, second_ref, out_ref):
    owned = first_ref.shape[0]
    out_ref[:owned, :] = first_ref[...].astype(out_ref.dtype)
    out_ref[owned:, :] = second_ref[...].astype(out_ref.dtype)


def pack(first, second):
    owned, width = first.shape
    return pl.pallas_call(
        pack_kernel,
        out_shape=jax.ShapeDtypeStruct((2 * owned, width), bf16),
        name="pack",
    )(first, second)


def sketched_term(sketch_turned, grad_turned, layer_input):
    token_sketch = jnp.dot(sketch_turned, grad_turned, preferred_element_type=f32)
    rounded = lax.reduce_precision(token_sketch, 8, 7)
    high, low = rounded.astype(bf16), (token_sketch - rounded).astype(bf16)
    times = lambda part: jnp.dot(part, layer_input, preferred_element_type=f32)
    return times(high) + times(low)


def moments(first, second, projected):
    new_first = beta_one * first + (1.0 - beta_one) * projected
    new_second = beta_two * second + (1.0 - beta_two) * projected * projected
    return new_first, new_second


def step_kernel(
    at_ref, inverse_ref, sketched_ref, mixed_ref, grad_ref, gathered_ref, own_first_ref, own_second_ref,
    update_ref, new_first_ref, new_second_ref,
    projector, turned, projected, ready, mixed, grad, gathered, arrived, sent,
):
    width, owned = grad_ref.shape[0], own_first_ref.shape[0]
    tiles = [(o, min(TILE, width - o)) for o in range(0, width, TILE)]
    fetch_mixed = pltpu.make_async_copy(mixed_ref, mixed, arrived.at[0])
    fetch_gathered = pltpu.make_async_copy(gathered_ref, gathered, arrived.at[1])
    fetch_grad = [
        pltpu.make_async_copy(grad_ref.at[pl.ds(o, n)], grad.at[pl.ds(o, n)], arrived.at[2 + i])
        for i, (o, n) in enumerate(tiles)
    ]
    fetch_mixed.start()

    high, low = two_parts(inverse_ref[:RANK, :RANK])
    values = sketched_ref[:RANK, :]
    projector[...] = (
        jnp.dot(low, values, preferred_element_type=f32) + jnp.dot(high, values, preferred_element_type=f32)
    ).astype(bf16)
    times = lambda a, b: lax.dot_general(a, b, (((1,), (1,)), ((), ())), preferred_element_type=f32)
    fetch_mixed.wait()
    fetch_grad[0].start()
    fetch_gathered.start()
    for o in range(0, mixed.shape[0], MIX_TILE):
        here = pl.ds(o, MIX_TILE)
        mixed_high, mixed_low = two_parts(mixed[here, :])
        turned[:, here] = (
            times(high, mixed_low) + times(low, mixed_high) + times(high, mixed_high)
        ).astype(bf16)

    mine = pl.ds(pl.multiple_of(at_ref[0] * owned, owned), owned)
    send = [
        pltpu.make_async_copy(ready.at[i % 2, :n], update_ref.at[pl.ds(o, n)], sent.at[i % 2])
        for i, (o, n) in enumerate(tiles)
    ]
    for i, (o, n) in enumerate(tiles):
        here = pl.ds(o, n)
        fetch_grad[i].wait()
        if i + 1 < len(tiles):
            fetch_grad[i + 1].start()
        projected[:, :n] = times(turned[...], grad[here, :])
        if i == 0:
            fetch_gathered.wait()
        first = gathered[:, :owned, here].reshape(RANK, n).astype(f32)
        second = gathered[:, owned:, here].reshape(RANK, n).astype(f32)
        new_first, new_second = moments(first, second, projected[:, :n])
        root = (1.0 - beta_two**ADAM_STEP) ** 0.5
        below = new_second * lax.rsqrt(new_second) + adam_epsilon * root
        scaled = new_first * (root / (1.0 - beta_one**ADAM_STEP))
        normalized = (scaled * pltpu.reciprocal(below)).astype(bf16)
        if i >= 2:
            send[i - 2].wait()
        ready[i % 2, :n] = lax.dot_general(
            normalized, projector[...], (((0,), (0,)), ((), ())), preferred_element_type=f32
        )
        send[i].start()
        new_first_ref[:, here], new_second_ref[:, here] = moments(
            own_first_ref[:, here], own_second_ref[:, here], projected[mine, :n]
        )
    for copy in send[-2:]:
        copy.wait()


def adam_step(at, inverse, sketched, mixed, grad_turned, gathered, own_first, own_second):
    width, tokens = grad_turned.shape
    features = sketched.shape[1]
    owned = own_first.shape[0]
    inside = pl.BlockSpec(memory_space=pltpu.VMEM)
    outside = pl.BlockSpec(memory_space=pl.ANY)
    return pl.pallas_call(
        step_kernel,
        out_shape=(
            jax.ShapeDtypeStruct((width, features), f32),
            jax.ShapeDtypeStruct((owned, width), f32),
            jax.ShapeDtypeStruct((owned, width), f32),
        ),
        in_specs=[pl.BlockSpec(memory_space=pltpu.SMEM), inside, inside]
        + [outside, outside, outside, inside, inside],
        out_specs=(outside, inside, inside),
        scratch_shapes=[
            pltpu.VMEM((RANK, features), bf16),
            pltpu.VMEM((RANK, tokens), bf16),
            pltpu.VMEM((RANK, TILE), f32),
            pltpu.VMEM((2, TILE, features), f32),
            pltpu.VMEM(mixed.shape, f32),
            pltpu.VMEM(grad_turned.shape, bf16),
            pltpu.VMEM(gathered.shape, bf16),
            pltpu.SemaphoreType.DMA((2 + pl.cdiv(width, TILE),)),
            pltpu.SemaphoreType.DMA((2,)),
        ],
        compiler_params=pltpu.CompilerParams(vmem_limit_bytes=STEP_VMEM),
        cost_estimate=pl.CostEstimate(
            flops=2 * RANK * width * (tokens + features) + 6 * RANK * RANK * tokens,
            bytes_accessed=width * (2 * tokens + 4 * RANK + 4 * features + 16 * owned) + 4 * tokens * RANK,
            transcendentals=RANK * width,
        ),
        name="adam_step",
    )(at, inverse, sketched, mixed, grad_turned, gathered, own_first, own_second)


def local(layer_input, output_grad, sketch, first_moment, second_moment):
    tokens, features = layer_input.shape
    columns = sketch.shape[1]
    own = columns // 8
    share = tokens // 128
    grad_turned = output_grad.T
    gathered = lax.all_gather(pack(first_moment, second_moment), "row", axis=0, tiled=False)

    partial = sketched_term(sketch.T, grad_turned, layer_input)
    own_tokens = lax.dynamic_index_in_dim(
        layer_input.reshape(16, 8, share, features), lax.axis_index("col"), 1, keepdims=False
    ).reshape(tokens // 8, features)
    half = scatter_sum(partial.reshape(2, columns // 2, features), "core", bf16)
    half, own_tokens = lax.optimization_barrier((half, own_tokens))
    owned_rows = scatter_sum(half.reshape(4, own, features), "y", bf16).astype(bf16)
    sketched = gather(gather(owned_rows, "y").reshape(columns // 2, features), "core")
    sketched = sketched.reshape(columns, features)

    times = lambda a, b: lax.dot_general(a, b, (((1,), (1,)), ((), ())), preferred_element_type=f32)
    mixed = scatter_sum(times(own_tokens, sketched[:RANK]).reshape(4, 4 * share, RANK), "x")
    gram = times(owned_rows, sketched)
    gram = jnp.stack([gram[k * STEP : k * STEP + PART] for k in range(4)])
    mixed, gram = lax.optimization_barrier((mixed, gram))
    mixed, gram = lax.optimization_barrier(
        (scatter_sum(mixed.reshape(4, share, RANK), "z"), scatter_sum(gram, "x"))
    )
    mixed, gram = lax.optimization_barrier((gather(gather(mixed, "core"), "y"), gram))
    gram = full_sum(gram, "z")
    mixed, gathered = lax.optimization_barrier((mixed.reshape(8 * share, RANK), gathered))
    mixed = lax.all_gather(mixed, "row", axis=0, tiled=True)
    gram = gather(gram, "x")
    gram = jnp.concatenate([gram[0, :STEP], gram[1, :STEP], gram[2, :STEP], gram[3]], axis=0)
    gram = gather(gather(gram, "y").reshape(columns // 2, columns), "core")

    inverse = inverse_factor(gram.reshape(columns, columns))
    at = lax.axis_index("row").astype(jnp.int32).reshape(1)
    update, new_first, new_second = adam_step(
        at, inverse, sketched, mixed, grad_turned, gathered, first_moment, second_moment
    )
    return update.T, new_first, new_second


def solution(mesh):
    placed = (P(None, "row"), P(None, "col"), P("col", None), P("row", "col"), P("row", "col"))
    return jax.shard_map(
        local,
        mesh=mesh,
        in_specs=placed,
        out_specs=(P("row", "col"), P("row", "col"), P("row", "col")),
        check_vma=False,
    )
```

```python
import jax
import jax.numpy as jnp
from jax import lax
from jax.experimental import pallas as pl
from jax.experimental.pallas import tpu as pltpu
from jax.sharding import PartitionSpec as P

RANK = 512
ADAM_STEP = 10
BLOCK = 128
TILE = 1024
MIX_TILE = 512
STEP_VMEM = 50 << 20
PART, STEP = 24, 16

beta_one = 0.9
beta_two = 0.999
adam_epsilon = 1e-08

f32 = jnp.float32
bf16 = jnp.bfloat16
HIGHEST = lax.Precision.HIGHEST

EXTENT = {"x": 4, "z": 4, "y": 4, "core": 2}
HOME = {"x": ("row", 4), "z": ("row", 1), "y": ("col", 2), "core": ("col", 1)}


def place(sub):
    axis, stride = HOME[sub]
    return lax.axis_index(axis) // stride % EXTENT[sub]


def shift(value, sub, by):
    axis, stride = HOME[sub]
    n = EXTENT[sub]
    pairs = []
    for i in range(16 if axis == "row" else 8):
        at = i // stride % n
        pairs.append((i, i + ((at + by) % n - at) * stride))
    return lax.ppermute(value, axis, pairs)


def scatter_sum(value, sub, wire=f32):
    n, me = EXTENT[sub], place(sub)
    pick = lambda k: lax.dynamic_index_in_dim(value, (me + k) % n, 0, keepdims=False)
    got = [shift(pick(k).astype(wire), sub, k) for k in range(1, n)]
    total = pick(0)
    for term in got:
        total = total + term.astype(value.dtype)
    return total


def gather(value, sub):
    n, me = EXTENT[sub], place(sub)
    got = [value] + [shift(value, sub, k) for k in range(1, n)]
    out = jnp.zeros((n,) + value.shape, value.dtype)
    for k in range(n):
        out = lax.dynamic_update_index_in_dim(out, got[k], (me - k) % n, 0)
    return out


def full_sum(value, sub):
    got = [shift(value, sub, k) for k in range(1, EXTENT[sub])]
    return (value + got[1]) + (got[0] + got[2])


def lane_of(value, k):
    return jnp.take_along_axis(value, jnp.full(value.shape, k, jnp.int32), axis=1)


def row_of(value, k):
    return jnp.broadcast_to(value[k : k + 1], value.shape)


def reciprocal(value):
    guess = pl.reciprocal(value, approx=True)
    return guess * (2.0 - value * guess)


def invert_block(rows, lane, sub):
    rows, scale = list(rows), []
    for g in range(len(rows)):
        group = (lane >= 8 * g) & (lane < 8 * g + 8)
        column = [lane_of(rows[g], 8 * g + m) for m in range(8)]
        now = jnp.where(group, jnp.where(lane == 8 * g + sub, 1.0, 0.0), rows[g])
        units, inverses, tops, diagonal = [], [], {}, None
        for k in range(8):
            pivot = row_of(column[k], k)
            inverses.append(reciprocal(pivot))
            units.append(row_of(now, k))
            factor = jnp.where(sub > k, column[k] * inverses[k], 0.0)
            for m in range(k + 1, 8):
                tops[k, m] = row_of(column[m], k)
                column[m] = column[m] - factor * tops[k, m]
            now = now - factor * units[k]
            diagonal = pivot if k == 0 else jnp.where(sub == k, pivot, diagonal)
        rows[g] = now
        scale.append(lax.rsqrt(diagonal))
        for h in range(g + 1, len(rows)):
            column = [lane_of(rows[h], 8 * g + m) for m in range(8)]
            now = jnp.where(group, 0.0, rows[h])
            for k in range(8):
                factor = column[k] * inverses[k]
                for m in range(k + 1, 8):
                    column[m] = column[m] - factor * tops[k, m]
                now = now - factor * units[k]
            rows[h] = now
    return [a * b for a, b in zip(rows, scale)]


def factor_kernel(gram_ref, out_ref, work):
    size, padded = gram_ref.shape[0], work.shape[0]
    work[...] = jnp.zeros_like(work)
    work[:size, :size] = gram_ref[...]
    lane = lax.broadcasted_iota(jnp.int32, (8, BLOCK), 1)
    sub = lax.broadcasted_iota(jnp.int32, (8, BLOCK), 0)

    def diagonal_inverse(o, n):
        rows = [work[pl.ds(pl.multiple_of(o + 8 * h, 8), 8), pl.ds(o, BLOCK)] for h in range(n // 8)]
        inverse = jnp.concatenate(invert_block(rows, lane, sub), axis=0)
        row_in = lax.broadcasted_iota(jnp.int32, (n, BLOCK), 0)
        lane_in = lax.broadcasted_iota(jnp.int32, (n, BLOCK), 1)
        return jnp.where(row_in >= lane_in, inverse, 0.0)

    def step(b, carry):
        o = pl.multiple_of(b * BLOCK, BLOCK)
        here = pl.ds(o, BLOCK)
        inverse = diagonal_inverse(o, BLOCK)
        panel = work[here, :]
        work[:, here] = jnp.zeros((padded, BLOCK), f32)
        solved = jnp.dot(inverse, panel, precision=HIGHEST, preferred_element_type=f32)
        work[here, :] = solved
        work[here, here] = inverse
        for later in range(1, padded // BLOCK):
            there = pl.ds(later * BLOCK, BLOCK)

            @pl.when(later > b)
            def _():
                work[there, :] -= lax.dot_general(
                    work[here, there], work[here, :], (((0,), (0,)), ((), ())),
                    precision=HIGHEST, preferred_element_type=f32,
                )

        return carry

    lax.fori_loop(0, size // BLOCK, step, 0)
    o, n = size // BLOCK * BLOCK, size % BLOCK
    if n:
        inverse = diagonal_inverse(o, n)
        work[o:size, :] = jnp.dot(
            inverse[:, :n], work[o:size, :], precision=HIGHEST, preferred_element_type=f32
        )
        work[o:size, o:] = inverse
    row_at = lax.broadcasted_iota(jnp.int32, (padded, padded), 0)
    lane_at = lax.broadcasted_iota(jnp.int32, (padded, padded), 1)
    out_ref[...] = jnp.where(row_at >= lane_at, work[...], 0.0)[:size, :size]


def inverse_factor(gram):
    size = gram.shape[0]
    padded = pl.cdiv(size, BLOCK) * BLOCK
    return pl.pallas_call(
        factor_kernel,
        out_shape=jax.ShapeDtypeStruct((size, size), f32),
        in_specs=[pl.BlockSpec(memory_space=pltpu.VMEM)],
        out_specs=pl.BlockSpec(memory_space=pltpu.VMEM),
        scratch_shapes=[pltpu.VMEM((padded, padded), f32)],
        compiler_params=pltpu.CompilerParams(vmem_limit_bytes=16 << 20),
        cost_estimate=pl.CostEstimate(flops=12 * size**3, bytes_accessed=8 * size**2, transcendentals=0),
        name="inverse_factor",
    )(gram)


def two_parts(value):
    high = value.astype(bf16)
    return high, (value - high.astype(f32)).astype(bf16)


def pack_kernel(first_ref, second_ref, out_ref):
    owned = first_ref.shape[0]
    out_ref[:owned, :] = first_ref[...].astype(out_ref.dtype)
    out_ref[owned:, :] = second_ref[...].astype(out_ref.dtype)


def pack(first, second):
    owned, width = first.shape
    return pl.pallas_call(
        pack_kernel,
        out_shape=jax.ShapeDtypeStruct((2 * owned, width), bf16),
        name="pack",
    )(first, second)


def sketched_term(sketch_turned, grad_turned, layer_input):
    token_sketch = jnp.dot(sketch_turned, grad_turned, preferred_element_type=f32)
    rounded = lax.reduce_precision(token_sketch, 8, 7)
    high, low = rounded.astype(bf16), (token_sketch - rounded).astype(bf16)
    times = lambda part: jnp.dot(part, layer_input, preferred_element_type=f32)
    return times(high) + times(low)


def moments(first, second, projected):
    new_first = beta_one * first + (1.0 - beta_one) * projected
    new_second = beta_two * second + (1.0 - beta_two) * projected * projected
    return new_first, new_second


def step_kernel(
    at_ref, inverse_ref, sketched_ref, mixed_ref, grad_ref, gathered_ref, own_first_ref, own_second_ref,
    update_ref, new_first_ref, new_second_ref,
    projector, turned, projected, ready, mixed, grad, gathered, arrived, sent,
):
    width, owned = grad_ref.shape[0], own_first_ref.shape[0]
    tiles = [(o, min(TILE, width - o)) for o in range(0, width, TILE)]
    fetch_mixed = pltpu.make_async_copy(mixed_ref, mixed, arrived.at[0])
    fetch_gathered = pltpu.make_async_copy(gathered_ref, gathered, arrived.at[1])
    fetch_grad = [
        pltpu.make_async_copy(grad_ref.at[pl.ds(o, n)], grad.at[pl.ds(o, n)], arrived.at[2 + i])
        for i, (o, n) in enumerate(tiles)
    ]
    fetch_mixed.start()

    high, low = two_parts(inverse_ref[:RANK, :RANK])
    values = sketched_ref[:RANK, :]
    projector[...] = (
        jnp.dot(low, values, preferred_element_type=f32) + jnp.dot(high, values, preferred_element_type=f32)
    ).astype(bf16)
    times = lambda a, b: lax.dot_general(a, b, (((1,), (1,)), ((), ())), preferred_element_type=f32)
    fetch_mixed.wait()
    fetch_grad[0].start()
    fetch_gathered.start()
    for o in range(0, mixed.shape[0], MIX_TILE):
        here = pl.ds(o, MIX_TILE)
        mixed_high, mixed_low = two_parts(mixed[here, :])
        turned[:, here] = (
            times(high, mixed_low) + times(low, mixed_high) + times(high, mixed_high)
        ).astype(bf16)

    mine = pl.ds(pl.multiple_of(at_ref[0] * owned, owned), owned)
    send = [
        pltpu.make_async_copy(ready.at[i % 2, :n], update_ref.at[pl.ds(o, n)], sent.at[i % 2])
        for i, (o, n) in enumerate(tiles)
    ]
    for i, (o, n) in enumerate(tiles):
        here = pl.ds(o, n)
        fetch_grad[i].wait()
        if i + 1 < len(tiles):
            fetch_grad[i + 1].start()
        projected[:, :n] = times(turned[...], grad[here, :])
        if i == 0:
            fetch_gathered.wait()
        first = gathered[:, :owned, here].reshape(RANK, n).astype(f32)
        second = gathered[:, owned:, here].reshape(RANK, n).astype(f32)
        new_first, new_second = moments(first, second, projected[:, :n])
        root = (1.0 - beta_two**ADAM_STEP) ** 0.5
        below = new_second * lax.rsqrt(new_second) + adam_epsilon * root
        scaled = new_first * (root / (1.0 - beta_one**ADAM_STEP))
        normalized = (scaled * pltpu.reciprocal(below)).astype(bf16)
        if i >= 2:
            send[i - 2].wait()
        ready[i % 2, :n] = lax.dot_general(
            normalized, projector[...], (((0,), (0,)), ((), ())), preferred_element_type=f32
        )
        send[i].start()
        new_first_ref[:, here], new_second_ref[:, here] = moments(
            own_first_ref[:, here], own_second_ref[:, here], projected[mine, :n]
        )
    for copy in send[-2:]:
        copy.wait()


def adam_step(at, inverse, sketched, mixed, grad_turned, gathered, own_first, own_second):
    width, tokens = grad_turned.shape
    features = sketched.shape[1]
    owned = own_first.shape[0]
    inside = pl.BlockSpec(memory_space=pltpu.VMEM)
    outside = pl.BlockSpec(memory_space=pl.ANY)
    return pl.pallas_call(
        step_kernel,
        out_shape=(
            jax.ShapeDtypeStruct((width, features), f32),
            jax.ShapeDtypeStruct((owned, width), f32),
            jax.ShapeDtypeStruct((owned, width), f32),
        ),
        in_specs=[pl.BlockSpec(memory_space=pltpu.SMEM), inside, inside]
        + [outside, outside, outside, inside, inside],
        out_specs=(outside, inside, inside),
        scratch_shapes=[
            pltpu.VMEM((RANK, features), bf16),
            pltpu.VMEM((RANK, tokens), bf16),
            pltpu.VMEM((RANK, TILE), f32),
            pltpu.VMEM((2, TILE, features), f32),
            pltpu.VMEM(mixed.shape, f32),
            pltpu.VMEM(grad_turned.shape, bf16),
            pltpu.VMEM(gathered.shape, bf16),
            pltpu.SemaphoreType.DMA((2 + pl.cdiv(width, TILE),)),
            pltpu.SemaphoreType.DMA((2,)),
        ],
        compiler_params=pltpu.CompilerParams(vmem_limit_bytes=STEP_VMEM),
        cost_estimate=pl.CostEstimate(
            flops=2 * RANK * width * (tokens + features) + 6 * RANK * RANK * tokens,
            bytes_accessed=width * (2 * tokens + 4 * RANK + 4 * features + 16 * owned) + 4 * tokens * RANK,
            transcendentals=RANK * width,
        ),
        name="adam_step",
    )(at, inverse, sketched, mixed, grad_turned, gathered, own_first, own_second)


def local(layer_input, output_grad, sketch, first_moment, second_moment):
    tokens, features = layer_input.shape
    columns = sketch.shape[1]
    own = columns // 8
    share = tokens // 128
    grad_turned = output_grad.T
    gathered = lax.all_gather(pack(first_moment, second_moment), "row", axis=0, tiled=False)

    partial = sketched_term(sketch.T, grad_turned, layer_input)
    own_tokens = lax.dynamic_index_in_dim(
        layer_input.reshape(16, 8, share, features), lax.axis_index("col"), 1, keepdims=False
    ).reshape(tokens // 8, features)
    half = scatter_sum(partial.reshape(2, columns // 2, features), "core", bf16)
    half, own_tokens = lax.optimization_barrier((half, own_tokens))
    owned_rows = scatter_sum(half.reshape(4, own, features), "y", bf16).astype(bf16)
    sketched = gather(gather(owned_rows, "y").reshape(columns // 2, features), "core")
    sketched = sketched.reshape(columns, features)

    times = lambda a, b: lax.dot_general(a, b, (((1,), (1,)), ((), ())), preferred_element_type=f32)
    mixed = scatter_sum(times(own_tokens, sketched[:RANK]).reshape(4, 4 * share, RANK), "x")
    gram = times(owned_rows, sketched)
    gram = jnp.stack([gram[k * STEP : k * STEP + PART] for k in range(4)])
    mixed, gram = lax.optimization_barrier((mixed, gram))
    mixed, gram = lax.optimization_barrier(
        (scatter_sum(mixed.reshape(4, share, RANK), "z"), scatter_sum(gram, "x"))
    )
    mixed = gather(gather(mixed, "core"), "y").reshape(8 * share, RANK)
    mixed, gram = lax.optimization_barrier((mixed, gram))
    gram = full_sum(gram, "z")
    mixed, gathered = lax.optimization_barrier((mixed, gathered))
    mixed = lax.all_gather(mixed, "row", axis=0, tiled=True)
    gram = gather(gram, "x")
    gram = jnp.concatenate([gram[0, :STEP], gram[1, :STEP], gram[2, :STEP], gram[3]], axis=0)
    gram = gather(gather(gram, "y").reshape(columns // 2, columns), "core")

    inverse = inverse_factor(gram.reshape(columns, columns))
    at = lax.axis_index("row").astype(jnp.int32).reshape(1)
    update, new_first, new_second = adam_step(
        at, inverse, sketched, mixed, grad_turned, gathered, first_moment, second_moment
    )
    return update.T, new_first, new_second


def solution(mesh):
    placed = (P(None, "row"), P(None, "col"), P("col", None), P("row", "col"), P("row", "col"))
    return jax.shard_map(
        local,
        mesh=mesh,
        in_specs=placed,
        out_specs=(P("row", "col"), P("row", "col"), P("row", "col")),
        check_vma=False,
    )
```

```python
import jax
import jax.numpy as jnp
from jax import lax
from jax.experimental import pallas as pl
from jax.experimental.pallas import tpu as pltpu
from jax.sharding import PartitionSpec as P

RANK = 512
ADAM_STEP = 10
BLOCK = 128
TILE = 1024
MIX_TILE = 512
STEP_VMEM = 50 << 20
PART, STEP = 24, 16

beta_one = 0.9
beta_two = 0.999
adam_epsilon = 1e-08

f32 = jnp.float32
bf16 = jnp.bfloat16
HIGHEST = lax.Precision.HIGHEST

EXTENT = {"x": 4, "z": 4, "y": 4, "core": 2}
HOME = {"x": ("row", 4), "z": ("row", 1), "y": ("col", 2), "core": ("col", 1)}


def place(sub):
    axis, stride = HOME[sub]
    return lax.axis_index(axis) // stride % EXTENT[sub]


def shift(value, sub, by):
    axis, stride = HOME[sub]
    n = EXTENT[sub]
    pairs = []
    for i in range(16 if axis == "row" else 8):
        at = i // stride % n
        pairs.append((i, i + ((at + by) % n - at) * stride))
    return lax.ppermute(value, axis, pairs)


def scatter_sum(value, sub, wire=f32):
    n, me = EXTENT[sub], place(sub)
    pick = lambda k: lax.dynamic_index_in_dim(value, (me + k) % n, 0, keepdims=False)
    got = [shift(pick(k).astype(wire), sub, k) for k in range(1, n)]
    total = pick(0)
    for term in got:
        total = total + term.astype(value.dtype)
    return total


def gather(value, sub):
    n, me = EXTENT[sub], place(sub)
    got = [value] + [shift(value, sub, k) for k in range(1, n)]
    out = jnp.zeros((n,) + value.shape, value.dtype)
    for k in range(n):
        out = lax.dynamic_update_index_in_dim(out, got[k], (me - k) % n, 0)
    return out


def full_sum(value, sub):
    got = [shift(value, sub, k) for k in range(1, EXTENT[sub])]
    return (value + got[1]) + (got[0] + got[2])


def lane_of(value, k):
    return jnp.take_along_axis(value, jnp.full(value.shape, k, jnp.int32), axis=1)


def row_of(value, k):
    return jnp.broadcast_to(value[k : k + 1], value.shape)


def reciprocal(value):
    guess = pl.reciprocal(value, approx=True)
    return guess * (2.0 - value * guess)


def invert_block(rows, lane, sub):
    rows, scale = list(rows), []
    for g in range(len(rows)):
        group = (lane >= 8 * g) & (lane < 8 * g + 8)
        column = [lane_of(rows[g], 8 * g + m) for m in range(8)]
        now = jnp.where(group, jnp.where(lane == 8 * g + sub, 1.0, 0.0), rows[g])
        units, inverses, tops, diagonal = [], [], {}, None
        for k in range(8):
            pivot = row_of(column[k], k)
            inverses.append(reciprocal(pivot))
            units.append(row_of(now, k))
            factor = jnp.where(sub > k, column[k] * inverses[k], 0.0)
            for m in range(k + 1, 8):
                tops[k, m] = row_of(column[m], k)
                column[m] = column[m] - factor * tops[k, m]
            now = now - factor * units[k]
            diagonal = pivot if k == 0 else jnp.where(sub == k, pivot, diagonal)
        rows[g] = now
        scale.append(lax.rsqrt(diagonal))
        for h in range(g + 1, len(rows)):
            column = [lane_of(rows[h], 8 * g + m) for m in range(8)]
            now = jnp.where(group, 0.0, rows[h])
            for k in range(8):
                factor = column[k] * inverses[k]
                for m in range(k + 1, 8):
                    column[m] = column[m] - factor * tops[k, m]
                now = now - factor * units[k]
            rows[h] = now
    return [a * b for a, b in zip(rows, scale)]


def factor_kernel(gram_ref, out_ref, work):
    size, padded = gram_ref.shape[0], work.shape[0]
    work[...] = jnp.zeros_like(work)
    work[:size, :size] = gram_ref[...]
    lane = lax.broadcasted_iota(jnp.int32, (8, BLOCK), 1)
    sub = lax.broadcasted_iota(jnp.int32, (8, BLOCK), 0)

    def diagonal_inverse(o, n):
        rows = [work[pl.ds(pl.multiple_of(o + 8 * h, 8), 8), pl.ds(o, BLOCK)] for h in range(n // 8)]
        inverse = jnp.concatenate(invert_block(rows, lane, sub), axis=0)
        row_in = lax.broadcasted_iota(jnp.int32, (n, BLOCK), 0)
        lane_in = lax.broadcasted_iota(jnp.int32, (n, BLOCK), 1)
        return jnp.where(row_in >= lane_in, inverse, 0.0)

    def step(b, carry):
        o = pl.multiple_of(b * BLOCK, BLOCK)
        here = pl.ds(o, BLOCK)
        inverse = diagonal_inverse(o, BLOCK)
        panel = work[here, :]
        work[:, here] = jnp.zeros((padded, BLOCK), f32)
        solved = jnp.dot(inverse, panel, precision=HIGHEST, preferred_element_type=f32)
        work[here, :] = solved
        work[here, here] = inverse
        for later in range(1, padded // BLOCK):
            there = pl.ds(later * BLOCK, BLOCK)

            @pl.when(later > b)
            def _():
                work[there, :] -= lax.dot_general(
                    work[here, there], work[here, :], (((0,), (0,)), ((), ())),
                    precision=HIGHEST, preferred_element_type=f32,
                )

        return carry

    lax.fori_loop(0, size // BLOCK, step, 0)
    o, n = size // BLOCK * BLOCK, size % BLOCK
    if n:
        inverse = diagonal_inverse(o, n)
        work[o:size, :] = jnp.dot(
            inverse[:, :n], work[o:size, :], precision=HIGHEST, preferred_element_type=f32
        )
        work[o:size, o:] = inverse
    row_at = lax.broadcasted_iota(jnp.int32, (padded, padded), 0)
    lane_at = lax.broadcasted_iota(jnp.int32, (padded, padded), 1)
    out_ref[...] = jnp.where(row_at >= lane_at, work[...], 0.0)[:size, :size]


def inverse_factor(gram):
    size = gram.shape[0]
    padded = pl.cdiv(size, BLOCK) * BLOCK
    return pl.pallas_call(
        factor_kernel,
        out_shape=jax.ShapeDtypeStruct((size, size), f32),
        in_specs=[pl.BlockSpec(memory_space=pltpu.VMEM)],
        out_specs=pl.BlockSpec(memory_space=pltpu.VMEM),
        scratch_shapes=[pltpu.VMEM((padded, padded), f32)],
        compiler_params=pltpu.CompilerParams(vmem_limit_bytes=16 << 20),
        cost_estimate=pl.CostEstimate(flops=12 * size**3, bytes_accessed=8 * size**2, transcendentals=0),
        name="inverse_factor",
    )(gram)


def two_parts(value):
    high = value.astype(bf16)
    return high, (value - high.astype(f32)).astype(bf16)


def pack_kernel(first_ref, second_ref, out_ref):
    owned = first_ref.shape[0]
    out_ref[:owned, :] = first_ref[...].astype(out_ref.dtype)
    out_ref[owned:, :] = second_ref[...].astype(out_ref.dtype)


def pack(first, second):
    owned, width = first.shape
    return pl.pallas_call(
        pack_kernel,
        out_shape=jax.ShapeDtypeStruct((2 * owned, width), bf16),
        name="pack",
    )(first, second)


def sketched_term(sketch_turned, grad_turned, layer_input):
    token_sketch = jnp.dot(sketch_turned, grad_turned, preferred_element_type=f32)
    rounded = lax.reduce_precision(token_sketch, 8, 7)
    high, low = rounded.astype(bf16), (token_sketch - rounded).astype(bf16)
    times = lambda part: jnp.dot(part, layer_input, preferred_element_type=f32)
    return times(high) + times(low)


def moments(first, second, projected):
    new_first = beta_one * first + (1.0 - beta_one) * projected
    new_second = beta_two * second + (1.0 - beta_two) * projected * projected
    return new_first, new_second


def step_kernel(
    at_ref, inverse_ref, sketched_ref, mixed_ref, grad_ref, gathered_ref, own_first_ref, own_second_ref,
    update_ref, new_first_ref, new_second_ref,
    projector, turned, projected, ready, mixed, grad, gathered, arrived, sent,
):
    width, owned = grad_ref.shape[0], own_first_ref.shape[0]
    tiles = [(o, min(TILE, width - o)) for o in range(0, width, TILE)]
    fetch_mixed = pltpu.make_async_copy(mixed_ref, mixed, arrived.at[0])
    fetch_gathered = pltpu.make_async_copy(gathered_ref, gathered, arrived.at[1])
    fetch_grad = [
        pltpu.make_async_copy(grad_ref.at[pl.ds(o, n)], grad.at[pl.ds(o, n)], arrived.at[2 + i])
        for i, (o, n) in enumerate(tiles)
    ]
    fetch_mixed.start()

    high, low = two_parts(inverse_ref[:RANK, :RANK])
    values = sketched_ref[:RANK, :]
    projector[...] = (
        jnp.dot(low, values, preferred_element_type=f32) + jnp.dot(high, values, preferred_element_type=f32)
    ).astype(bf16)
    times = lambda a, b: lax.dot_general(a, b, (((1,), (1,)), ((), ())), preferred_element_type=f32)
    fetch_mixed.wait()
    fetch_grad[0].start()
    fetch_gathered.start()
    for o in range(0, mixed.shape[0], MIX_TILE):
        here = pl.ds(o, MIX_TILE)
        mixed_high, mixed_low = two_parts(mixed[here, :])
        turned[:, here] = (
            times(high, mixed_low) + times(low, mixed_high) + times(high, mixed_high)
        ).astype(bf16)

    mine = pl.ds(pl.multiple_of(at_ref[0] * owned, owned), owned)
    send = [
        pltpu.make_async_copy(ready.at[i % 2, :n], update_ref.at[pl.ds(o, n)], sent.at[i % 2])
        for i, (o, n) in enumerate(tiles)
    ]
    for i, (o, n) in enumerate(tiles):
        here = pl.ds(o, n)
        fetch_grad[i].wait()
        if i + 1 < len(tiles):
            fetch_grad[i + 1].start()
        projected[:, :n] = times(turned[...], grad[here, :])
        if i == 0:
            fetch_gathered.wait()
        first = gathered[:, :owned, here].reshape(RANK, n).astype(f32)
        second = gathered[:, owned:, here].reshape(RANK, n).astype(f32)
        new_first, new_second = moments(first, second, projected[:, :n])
        root = (1.0 - beta_two**ADAM_STEP) ** 0.5
        below = new_second * lax.rsqrt(new_second) + adam_epsilon * root
        scaled = new_first * (root / (1.0 - beta_one**ADAM_STEP))
        normalized = (scaled * pltpu.reciprocal(below)).astype(bf16)
        if i >= 2:
            send[i - 2].wait()
        ready[i % 2, :n] = lax.dot_general(
            normalized, projector[...], (((0,), (0,)), ((), ())), preferred_element_type=f32
        )
        send[i].start()
        new_first_ref[:, here], new_second_ref[:, here] = moments(
            own_first_ref[:, here], own_second_ref[:, here], projected[mine, :n]
        )
    for copy in send[-2:]:
        copy.wait()


def adam_step(at, inverse, sketched, mixed, grad_turned, gathered, own_first, own_second):
    width, tokens = grad_turned.shape
    features = sketched.shape[1]
    owned = own_first.shape[0]
    inside = pl.BlockSpec(memory_space=pltpu.VMEM)
    outside = pl.BlockSpec(memory_space=pl.ANY)
    return pl.pallas_call(
        step_kernel,
        out_shape=(
            jax.ShapeDtypeStruct((width, features), f32),
            jax.ShapeDtypeStruct((owned, width), f32),
            jax.ShapeDtypeStruct((owned, width), f32),
        ),
        in_specs=[pl.BlockSpec(memory_space=pltpu.SMEM), inside, inside]
        + [outside, outside, outside, inside, inside],
        out_specs=(outside, inside, inside),
        scratch_shapes=[
            pltpu.VMEM((RANK, features), bf16),
            pltpu.VMEM((RANK, tokens), bf16),
            pltpu.VMEM((RANK, TILE), f32),
            pltpu.VMEM((2, TILE, features), f32),
            pltpu.VMEM(mixed.shape, f32),
            pltpu.VMEM(grad_turned.shape, bf16),
            pltpu.VMEM(gathered.shape, bf16),
            pltpu.SemaphoreType.DMA((2 + pl.cdiv(width, TILE),)),
            pltpu.SemaphoreType.DMA((2,)),
        ],
        compiler_params=pltpu.CompilerParams(vmem_limit_bytes=STEP_VMEM),
        cost_estimate=pl.CostEstimate(
            flops=2 * RANK * width * (tokens + features) + 6 * RANK * RANK * tokens,
            bytes_accessed=width * (2 * tokens + 4 * RANK + 4 * features + 16 * owned) + 4 * tokens * RANK,
            transcendentals=RANK * width,
        ),
        name="adam_step",
    )(at, inverse, sketched, mixed, grad_turned, gathered, own_first, own_second)


def local(layer_input, output_grad, sketch, first_moment, second_moment):
    tokens, features = layer_input.shape
    columns = sketch.shape[1]
    own = columns // 8
    share = tokens // 128
    grad_turned = output_grad.T
    gathered = lax.all_gather(pack(first_moment, second_moment), "row", axis=0, tiled=False)

    partial = sketched_term(sketch.T, grad_turned, layer_input)
    own_tokens = lax.dynamic_index_in_dim(
        layer_input.reshape(16, 8, share, features), lax.axis_index("col"), 1, keepdims=False
    ).reshape(tokens // 8, features)
    half = scatter_sum(partial.reshape(2, columns // 2, features), "core", bf16)
    half, own_tokens = lax.optimization_barrier((half, own_tokens))
    owned_rows = scatter_sum(half.reshape(4, own, features), "y", bf16).astype(bf16)
    sketched = gather(gather(owned_rows, "y").reshape(columns // 2, features), "core")
    sketched = sketched.reshape(columns, features)

    times = lambda a, b: lax.dot_general(a, b, (((1,), (1,)), ((), ())), preferred_element_type=f32)
    mixed = scatter_sum(times(own_tokens, sketched[:RANK]).reshape(4, 4 * share, RANK), "x")
    gram = times(owned_rows, sketched)
    gram = jnp.stack([gram[k * STEP : k * STEP + PART] for k in range(4)])
    mixed = gather(scatter_sum(mixed.reshape(4, share, RANK), "z"), "core")
    mixed, gram = lax.optimization_barrier((mixed, gram))
    mixed, gram = gather(mixed, "y").reshape(8 * share, RANK), scatter_sum(gram, "x")
    mixed, gram = lax.optimization_barrier((mixed, gram))
    gram = full_sum(gram, "z")
    mixed, gathered = lax.optimization_barrier((mixed, gathered))
    mixed = lax.all_gather(mixed, "row", axis=0, tiled=True)
    gram = gather(gram, "x")
    gram = jnp.concatenate([gram[0, :STEP], gram[1, :STEP], gram[2, :STEP], gram[3]], axis=0)
    gram = gather(gather(gram, "y").reshape(columns // 2, columns), "core")

    inverse = inverse_factor(gram.reshape(columns, columns))
    at = lax.axis_index("row").astype(jnp.int32).reshape(1)
    update, new_first, new_second = adam_step(
        at, inverse, sketched, mixed, grad_turned, gathered, first_moment, second_moment
    )
    return update.T, new_first, new_second


def solution(mesh):
    placed = (P(None, "row"), P(None, "col"), P("col", None), P("row", "col"), P("row", "col"))
    return jax.shard_map(
        local,
        mesh=mesh,
        in_specs=placed,
        out_specs=(P("row", "col"), P("row", "col"), P("row", "col")),
        check_vma=False,
    )
```

```python
import jax
import jax.numpy as jnp
from jax import lax
from jax.experimental import pallas as pl
from jax.experimental.pallas import tpu as pltpu
from jax.sharding import PartitionSpec as P

RANK = 512
ADAM_STEP = 10
BLOCK = 128
TILE = 1024
MIX_TILE = 512
STEP_VMEM = 50 << 20
PART, STEP = 24, 16

beta_one = 0.9
beta_two = 0.999
adam_epsilon = 1e-08

f32 = jnp.float32
bf16 = jnp.bfloat16
HIGHEST = lax.Precision.HIGHEST

EXTENT = {"x": 4, "z": 4, "y": 4, "core": 2}
HOME = {"x": ("row", 4), "z": ("row", 1), "y": ("col", 2), "core": ("col", 1)}


def place(sub):
    axis, stride = HOME[sub]
    return lax.axis_index(axis) // stride % EXTENT[sub]


def shift(value, sub, by):
    axis, stride = HOME[sub]
    n = EXTENT[sub]
    pairs = []
    for i in range(16 if axis == "row" else 8):
        at = i // stride % n
        pairs.append((i, i + ((at + by) % n - at) * stride))
    return lax.ppermute(value, axis, pairs)


def scatter_sum(value, sub, wire=f32):
    n, me = EXTENT[sub], place(sub)
    pick = lambda k: lax.dynamic_index_in_dim(value, (me + k) % n, 0, keepdims=False)
    got = [shift(pick(k).astype(wire), sub, k) for k in range(1, n)]
    total = pick(0)
    for term in got:
        total = total + term.astype(value.dtype)
    return total


def gather(value, sub):
    n, me = EXTENT[sub], place(sub)
    got = [value] + [shift(value, sub, k) for k in range(1, n)]
    out = jnp.zeros((n,) + value.shape, value.dtype)
    for k in range(n):
        out = lax.dynamic_update_index_in_dim(out, got[k], (me - k) % n, 0)
    return out


def full_sum(value, sub):
    got = [shift(value, sub, k) for k in range(1, EXTENT[sub])]
    return (value + got[1]) + (got[0] + got[2])


def lane_of(value, k):
    return jnp.take_along_axis(value, jnp.full(value.shape, k, jnp.int32), axis=1)


def row_of(value, k):
    return jnp.broadcast_to(value[k : k + 1], value.shape)


def reciprocal(value):
    guess = pl.reciprocal(value, approx=True)
    return guess * (2.0 - value * guess)


def invert_block(rows, lane, sub):
    rows, scale = list(rows), []
    for g in range(len(rows)):
        group = (lane >= 8 * g) & (lane < 8 * g + 8)
        column = [lane_of(rows[g], 8 * g + m) for m in range(8)]
        now = jnp.where(group, jnp.where(lane == 8 * g + sub, 1.0, 0.0), rows[g])
        units, inverses, tops, diagonal = [], [], {}, None
        for k in range(8):
            pivot = row_of(column[k], k)
            inverses.append(reciprocal(pivot))
            units.append(row_of(now, k))
            factor = jnp.where(sub > k, column[k] * inverses[k], 0.0)
            for m in range(k + 1, 8):
                tops[k, m] = row_of(column[m], k)
                column[m] = column[m] - factor * tops[k, m]
            now = now - factor * units[k]
            diagonal = pivot if k == 0 else jnp.where(sub == k, pivot, diagonal)
        rows[g] = now
        scale.append(lax.rsqrt(diagonal))
        for h in range(g + 1, len(rows)):
            column = [lane_of(rows[h], 8 * g + m) for m in range(8)]
            now = jnp.where(group, 0.0, rows[h])
            for k in range(8):
                factor = column[k] * inverses[k]
                for m in range(k + 1, 8):
                    column[m] = column[m] - factor * tops[k, m]
                now = now - factor * units[k]
            rows[h] = now
    return [a * b for a, b in zip(rows, scale)]


def factor_kernel(gram_ref, out_ref, work):
    size, padded = gram_ref.shape[0], work.shape[0]
    work[...] = jnp.zeros_like(work)
    work[:size, :size] = gram_ref[...]
    lane = lax.broadcasted_iota(jnp.int32, (8, BLOCK), 1)
    sub = lax.broadcasted_iota(jnp.int32, (8, BLOCK), 0)

    def diagonal_inverse(o, n):
        rows = [work[pl.ds(pl.multiple_of(o + 8 * h, 8), 8), pl.ds(o, BLOCK)] for h in range(n // 8)]
        inverse = jnp.concatenate(invert_block(rows, lane, sub), axis=0)
        row_in = lax.broadcasted_iota(jnp.int32, (n, BLOCK), 0)
        lane_in = lax.broadcasted_iota(jnp.int32, (n, BLOCK), 1)
        return jnp.where(row_in >= lane_in, inverse, 0.0)

    def step(b, carry):
        o = pl.multiple_of(b * BLOCK, BLOCK)
        here = pl.ds(o, BLOCK)
        inverse = diagonal_inverse(o, BLOCK)
        panel = work[here, :]
        work[:, here] = jnp.zeros((padded, BLOCK), f32)
        solved = jnp.dot(inverse, panel, precision=HIGHEST, preferred_element_type=f32)
        work[here, :] = solved
        work[here, here] = inverse
        for later in range(1, padded // BLOCK):
            there = pl.ds(later * BLOCK, BLOCK)

            @pl.when(later > b)
            def _():
                work[there, :] -= lax.dot_general(
                    work[here, there], work[here, :], (((0,), (0,)), ((), ())),
                    precision=HIGHEST, preferred_element_type=f32,
                )

        return carry

    lax.fori_loop(0, size // BLOCK, step, 0)
    o, n = size // BLOCK * BLOCK, size % BLOCK
    if n:
        inverse = diagonal_inverse(o, n)
        work[o:size, :] = jnp.dot(
            inverse[:, :n], work[o:size, :], precision=HIGHEST, preferred_element_type=f32
        )
        work[o:size, o:] = inverse
    row_at = lax.broadcasted_iota(jnp.int32, (padded, padded), 0)
    lane_at = lax.broadcasted_iota(jnp.int32, (padded, padded), 1)
    out_ref[...] = jnp.where(row_at >= lane_at, work[...], 0.0)[:size, :size]


def inverse_factor(gram):
    size = gram.shape[0]
    padded = pl.cdiv(size, BLOCK) * BLOCK
    return pl.pallas_call(
        factor_kernel,
        out_shape=jax.ShapeDtypeStruct((size, size), f32),
        in_specs=[pl.BlockSpec(memory_space=pltpu.VMEM)],
        out_specs=pl.BlockSpec(memory_space=pltpu.VMEM),
        scratch_shapes=[pltpu.VMEM((padded, padded), f32)],
        compiler_params=pltpu.CompilerParams(vmem_limit_bytes=16 << 20),
        cost_estimate=pl.CostEstimate(flops=12 * size**3, bytes_accessed=8 * size**2, transcendentals=0),
        name="inverse_factor",
    )(gram)


def two_parts(value):
    high = value.astype(bf16)
    return high, (value - high.astype(f32)).astype(bf16)


def pack_kernel(first_ref, second_ref, out_ref):
    owned = first_ref.shape[0]
    out_ref[:owned, :] = first_ref[...].astype(out_ref.dtype)
    out_ref[owned:, :] = second_ref[...].astype(out_ref.dtype)


def pack(first, second):
    owned, width = first.shape
    return pl.pallas_call(
        pack_kernel,
        out_shape=jax.ShapeDtypeStruct((2 * owned, width), bf16),
        name="pack",
    )(first, second)


def sketched_term(sketch_turned, grad_turned, layer_input):
    token_sketch = jnp.dot(sketch_turned, grad_turned, preferred_element_type=f32)
    rounded = lax.reduce_precision(token_sketch, 8, 7)
    high, low = rounded.astype(bf16), (token_sketch - rounded).astype(bf16)
    times = lambda part: jnp.dot(part, layer_input, preferred_element_type=f32)
    return times(high) + times(low)


def moments(first, second, projected):
    new_first = beta_one * first + (1.0 - beta_one) * projected
    new_second = beta_two * second + (1.0 - beta_two) * projected * projected
    return new_first, new_second


def step_kernel(
    at_ref, inverse_ref, sketched_ref, mixed_ref, grad_ref, gathered_ref, own_first_ref, own_second_ref,
    update_ref, new_first_ref, new_second_ref,
    projector, turned, projected, ready, mixed, grad, gathered, arrived, sent,
):
    width, owned = grad_ref.shape[0], own_first_ref.shape[0]
    tiles = [(o, min(TILE, width - o)) for o in range(0, width, TILE)]
    parts = [pl.ds(o, MIX_TILE) for o in range(0, mixed.shape[0], MIX_TILE)]
    fetch_mixed = [
        pltpu.make_async_copy(mixed_ref.at[here], mixed.at[here], arrived.at[1 + len(tiles) + i])
        for i, here in enumerate(parts)
    ]
    fetch_gathered = pltpu.make_async_copy(gathered_ref, gathered, arrived.at[0])
    fetch_grad = [
        pltpu.make_async_copy(grad_ref.at[pl.ds(o, n)], grad.at[pl.ds(o, n)], arrived.at[1 + i])
        for i, (o, n) in enumerate(tiles)
    ]
    fetch_mixed[0].start()
    fetch_mixed[1].start()

    high, low = two_parts(inverse_ref[:RANK, :RANK])
    times = lambda a, b: lax.dot_general(a, b, (((1,), (1,)), ((), ())), preferred_element_type=f32)
    halves = [(pl.ds(o, RANK // 2), o, o + RANK // 2) for o in (0, RANK // 2)]
    for rows, o, end in halves:
        values = sketched_ref[:end, :]
        projector[rows, :] = (
            jnp.dot(low[o:end, :end], values, preferred_element_type=f32)
            + jnp.dot(high[o:end, :end], values, preferred_element_type=f32)
        ).astype(bf16)
    after = fetch_mixed[2:] + [fetch_grad[0], fetch_gathered]
    for i, here in enumerate(parts):
        fetch_mixed[i].wait()
        if i + 1 < len(parts):
            after.pop(0).start()
        else:
            for copy in after:
                copy.start()
        mixed_high, mixed_low = two_parts(mixed[here, :])
        for rows, o, end in halves:
            turned[rows, here] = (
                times(high[o:end, :end], mixed_low[:, :end])
                + times(low[o:end, :end], mixed_high[:, :end])
                + times(high[o:end, :end], mixed_high[:, :end])
            ).astype(bf16)

    mine = pl.ds(pl.multiple_of(at_ref[0] * owned, owned), owned)
    send = [
        pltpu.make_async_copy(ready.at[i % 2, :n], update_ref.at[pl.ds(o, n)], sent.at[i % 2])
        for i, (o, n) in enumerate(tiles)
    ]
    for i, (o, n) in enumerate(tiles):
        here = pl.ds(o, n)
        fetch_grad[i].wait()
        if i + 1 < len(tiles):
            fetch_grad[i + 1].start()
        projected[:, :n] = times(turned[...], grad[here, :])
        if i == 0:
            fetch_gathered.wait()
        first = gathered[:, :owned, here].reshape(RANK, n).astype(f32)
        second = gathered[:, owned:, here].reshape(RANK, n).astype(f32)
        new_first, new_second = moments(first, second, projected[:, :n])
        root = (1.0 - beta_two**ADAM_STEP) ** 0.5
        below = new_second * lax.rsqrt(new_second) + adam_epsilon * root
        scaled = new_first * (root / (1.0 - beta_one**ADAM_STEP))
        normalized = (scaled * pltpu.reciprocal(below)).astype(bf16)
        if i >= 2:
            send[i - 2].wait()
        ready[i % 2, :n] = lax.dot_general(
            normalized, projector[...], (((0,), (0,)), ((), ())), preferred_element_type=f32
        )
        send[i].start()
        new_first_ref[:, here], new_second_ref[:, here] = moments(
            own_first_ref[:, here], own_second_ref[:, here], projected[mine, :n]
        )
    for copy in send[-2:]:
        copy.wait()


def adam_step(at, inverse, sketched, mixed, grad_turned, gathered, own_first, own_second):
    width, tokens = grad_turned.shape
    features = sketched.shape[1]
    owned = own_first.shape[0]
    inside = pl.BlockSpec(memory_space=pltpu.VMEM)
    outside = pl.BlockSpec(memory_space=pl.ANY)
    return pl.pallas_call(
        step_kernel,
        out_shape=(
            jax.ShapeDtypeStruct((width, features), f32),
            jax.ShapeDtypeStruct((owned, width), f32),
            jax.ShapeDtypeStruct((owned, width), f32),
        ),
        in_specs=[pl.BlockSpec(memory_space=pltpu.SMEM), inside, inside]
        + [outside, outside, outside, inside, inside],
        out_specs=(outside, inside, inside),
        scratch_shapes=[
            pltpu.VMEM((RANK, features), bf16),
            pltpu.VMEM((RANK, tokens), bf16),
            pltpu.VMEM((RANK, TILE), f32),
            pltpu.VMEM((2, TILE, features), f32),
            pltpu.VMEM(mixed.shape, f32),
            pltpu.VMEM(grad_turned.shape, bf16),
            pltpu.VMEM(gathered.shape, bf16),
            pltpu.SemaphoreType.DMA((1 + pl.cdiv(width, TILE) + tokens // MIX_TILE,)),
            pltpu.SemaphoreType.DMA((2,)),
        ],
        compiler_params=pltpu.CompilerParams(vmem_limit_bytes=STEP_VMEM),
        cost_estimate=pl.CostEstimate(
            flops=2 * RANK * width * (tokens + features) + 6 * RANK * RANK * tokens,
            bytes_accessed=width * (2 * tokens + 4 * RANK + 4 * features + 16 * owned) + 4 * tokens * RANK,
            transcendentals=RANK * width,
        ),
        name="adam_step",
    )(at, inverse, sketched, mixed, grad_turned, gathered, own_first, own_second)


def local(layer_input, output_grad, sketch, first_moment, second_moment):
    tokens, features = layer_input.shape
    columns = sketch.shape[1]
    own = columns // 8
    share = tokens // 128
    grad_turned = output_grad.T
    gathered = lax.all_gather(pack(first_moment, second_moment), "row", axis=0, tiled=False)

    partial = sketched_term(sketch.T, grad_turned, layer_input)
    own_tokens = lax.dynamic_index_in_dim(
        layer_input.reshape(16, 8, share, features), lax.axis_index("col"), 1, keepdims=False
    ).reshape(tokens // 8, features)
    half = scatter_sum(partial.reshape(2, columns // 2, features), "core", bf16)
    half, own_tokens = lax.optimization_barrier((half, own_tokens))
    owned_rows = scatter_sum(half.reshape(4, own, features), "y", bf16).astype(bf16)
    sketched = gather(gather(owned_rows, "y").reshape(columns // 2, features), "core")
    sketched = sketched.reshape(columns, features)

    times = lambda a, b: lax.dot_general(a, b, (((1,), (1,)), ((), ())), preferred_element_type=f32)
    mixed = scatter_sum(times(own_tokens, sketched[:RANK]).reshape(4, 4 * share, RANK), "x")
    gram = times(owned_rows, sketched)
    gram = jnp.stack([gram[k * STEP : k * STEP + PART] for k in range(4)])
    mixed = gather(scatter_sum(mixed.reshape(4, share, RANK), "z"), "core")
    mixed, gram = lax.optimization_barrier((mixed, gram))
    mixed, gram = gather(mixed, "y").reshape(8 * share, RANK), scatter_sum(gram, "x")
    mixed, gram = lax.optimization_barrier((mixed, gram))
    gram = full_sum(gram, "z")
    mixed, gathered = lax.optimization_barrier((mixed, gathered))
    mixed = lax.all_gather(mixed, "row", axis=0, tiled=True)
    gram = gather(gram, "x")
    gram = jnp.concatenate([gram[0, :STEP], gram[1, :STEP], gram[2, :STEP], gram[3]], axis=0)
    gram = gather(gather(gram, "y").reshape(columns // 2, columns), "core")

    inverse = inverse_factor(gram.reshape(columns, columns))
    at = lax.axis_index("row").astype(jnp.int32).reshape(1)
    update, new_first, new_second = adam_step(
        at, inverse, sketched, mixed, grad_turned, gathered, first_moment, second_moment
    )
    return update.T, new_first, new_second


def solution(mesh):
    placed = (P(None, "row"), P(None, "col"), P("col", None), P("row", "col"), P("row", "col"))
    return jax.shard_map(
        local,
        mesh=mesh,
        in_specs=placed,
        out_specs=(P("row", "col"), P("row", "col"), P("row", "col")),
        check_vma=False,
    )
```
